256 devices in a mesh: grp: 4 (over x), tile: 64 (over z, y, core).
Axes of the slice: x: 4, y: 4, z: 8, core: 2. Of those that a mesh axis runs over, the one named last changes fastest.
Arguments:
- obs_anom: bfloat16 [8192, 64, 256], P(('grp', 'tile')), may hold values from -6 to 6
- innov: bfloat16 [8192, 64, 256], P(('grp', 'tile')), may hold values from -6 to 6
- obs_rinv: float32 [8192, 64], P(('grp', 'tile')), may hold values from 0.5 to 5
- obs_pos: int32 [8192, 64], P(('grp', 'tile')), may hold values from 0 to 32767
- obs_count: int32 [8192], P(('grp', 'tile')), may hold values from 1 to 64
- obs_region: int32 [8192, 1], P(('grp', 'tile')), may hold values from 0 to 63; in each aligned block of 32 rows (0 to 31, 32 to 63, ...) at most 2 rows name the same one
- obs_partner: int32 [8192, 6], P(('grp', 'tile')), may hold values from 0 to 7, all different within a row
- state_anom: bfloat16 [4, 128, 4096, 256], P('grp', 'tile'), may hold values from -6 to 6
- coeff: float32 [4, 128, 256, 256], P('grp', 'tile'), may hold values from -0.375 to 0.375
Outputs:
- updated: bfloat16 [4, 128, 4096, 256], P('grp', 'tile')
- new_coeff: float32 [4, 128, 256, 256], P('grp', 'tile')
The draws below stay inside these ranges and needn't reach their ends.
Inputs may be any that keep to these rules, and one draw needn't show every extreme that they name: `obs_region`: among the 32 observation blocks of one device (aligned blocks of rows), no region is named more than 2 times; some region is named exactly 2 times. `obs_partner`: the 6 partners of one observation block are different.
All inputs are finite; a program needn't handle non-finite values.
Results may differ from the reference program's by a relative error of at most 0.02.
Values may be sent and summed in bfloat16 or wider, within the bound.
A program may use at most 192 MiB of HBM per device.

```python
import math
import jax
import jax.numpy as jnp
import numpy as np
from jax import lax

M = 256
BS = 4096
OBS = 64
K = 6
SB_DEV = 2
OB_DEV = 32
CAP = 2
GROUPS = 4
REGIONS = 64
NOB = 8192
REGION_CELLS = 32768
N_GRP = 4
N_TILE = 64


def plant(values, key, low, largest):
    dims = values.shape
    index_at = [jax.random.randint(jax.random.fold_in(key, axis), (), 0, dims[axis]) for axis in range(len(dims))]
    values = values.at[tuple(index_at)].set(low)
    longest = dims.index(max(dims))
    index_at[longest] = (index_at[longest] + 1) % dims[longest]
    return values.at[tuple(index_at)].set(largest)


def level_of(stream_key, shape, cuts, least, largest):
    factor_of, own = 1.0, jax.random.fold_in(stream_key, 6)
    for position, shards_of in cuts:
        draws = jnp.exp(jax.random.uniform(jax.random.fold_in(own, position), (shards_of,), jnp.float32, least / len(cuts), largest / len(cuts)))
        factor_of = factor_of * jnp.repeat(draws, shape[position] // shards_of).reshape([-1 if axis == position else 1 for axis in range(len(shape))])
    return factor_of


def picks_of(rng, rows, count, top, lift):
    sequence = jax.random.permutation(jax.random.fold_in(rng, 1), count)
    pull = sequence
    for power in range(3):
        pull = pull * pull // count
    pull = pull * lift // count
    lots = jax.random.randint(jax.random.fold_in(rng, 2), (rows, count), 0, 4096) + pull
    fixed_rows = jax.random.permutation(jax.random.fold_in(rng, 3), rows)[jnp.arange(count) % rows]
    lots = jnp.where(jnp.arange(rows)[:, None] == fixed_rows[None, :], 1 << 14, lots)
    merit = lots * count + jnp.arange(count)
    return lax.top_k(merit.astype(jnp.int32), top)[1].astype(jnp.int32)


def routed_block(own_key, own, number, rows, number_of, top, bound, slope):
    sequence = jax.random.permutation(own_key, number_of)
    packed, usual = load_shares(number_of, rows * top, bound, slope, True), load_shares(number_of, rows * top, bound, slope, False)
    places = jnp.arange(number_of)

    def named(lengths, offset_by):
        used = int((lengths > 0).sum())
        fixed = max(1, used // 4)
        shifted = fixed + (places - fixed + offset_by * (used - fixed)) % max(1, number_of - fixed)
        return jnp.zeros((number_of,), jnp.int32).at[sequence[jnp.where(places < fixed, places, shifted)]].set(jnp.asarray(lengths, jnp.int32))

    lengths = jnp.where(number % 4 == 0, named(packed, number // 4), named(usual, number - number // 4 - 1))
    mixed = jax.random.permutation(jax.random.fold_in(own, 3), number_of)
    donor, receiver = mixed[0:number_of // 2 * 2:2], mixed[1:number_of // 2 * 2:2]
    margin = jnp.minimum(lengths[donor] - 1, bound - lengths[receiver]) // 2
    margin = jnp.where((donor == sequence[0]) | (receiver == sequence[0]) | (lengths[receiver] == 0), 0, jnp.maximum(margin, 0))
    shifted = jax.random.randint(jax.random.fold_in(own, 4), (number_of // 2,), 0, 1 << 20) % (margin + 1)
    lengths = lengths.at[donor].add(-shifted).at[receiver].add(shifted)
    labels = jnp.searchsorted(jnp.cumsum(lengths), jnp.arange(rows * top), side="right").astype(jnp.int32)
    grid = labels.reshape(top, rows).T
    grid = grid[jax.random.permutation(jax.random.fold_in(own, 1), rows)]
    offset_by = jax.random.randint(jax.random.fold_in(own, 2), (rows, 1), 0, top)
    return jnp.take_along_axis(grid, (jnp.arange(top)[None, :] + offset_by) % top, axis=1)


def load_shares(number_of, total, bound, slope, full):
    weights = [(1 << 20) // math.isqrt(rank ** slope) + 1 for rank in range(1, number_of + 1)]
    largest = bound if full else min(bound, max(-(-total // number_of), total * weights[0] // sum(weights)))
    least = 1 if total - largest >= number_of - 1 else 0
    given, spare = [largest] + [least] * (number_of - 1), total - largest - least * (number_of - 1)
    while spare > 0:
        movable = [i for i in range(1, number_of) if given[i] < largest] or [i for i in range(1, number_of) if given[i] < bound]
        mass, budget = sum([weights[i] for i in movable]), spare
        for i in movable:
            addition = min(bound - given[i], max(1, budget * weights[i] // mass), spare)
            given[i] = given[i] + addition
            spare = spare - addition
    return np.array(given)


def scatter_about(stream_key, shape, deviation, most, pieces=(), kind=jnp.bfloat16):
    array = deviation * jax.random.normal(stream_key, shape, jnp.float32)
    if pieces:
        array = array * level_of(stream_key, shape, pieces, -0.22, 0.18)
    return jnp.clip(array, -most, most).astype(kind)


def setup_inputs(seed: int = 0) -> dict:
    arg_keys = jax.random.split(jax.random.key(seed), 10)
    obs_anom = scatter_about(arg_keys[0], (NOB, OBS, M), 1.0, 6.0, ((0, 256),))
    innov = scatter_about(arg_keys[1], (NOB, OBS, M), 1.0, 6.0, ((0, 256),))
    obs_rinv = jnp.clip(jnp.exp(math.log(5.0) - 2.3025851 * jax.random.uniform(arg_keys[2], (NOB, OBS), jnp.float32) ** level_of(arg_keys[2], (NOB, OBS), ((0, 256),), -0.2, 0.2)), 0.5, 5.0)
    obs_pos = plant(jax.random.randint(arg_keys[3], (NOB, OBS), 0, REGION_CELLS), jax.random.fold_in(arg_keys[3], 1), 0, REGION_CELLS - 1).astype(jnp.int32)
    obs_count = plant(jax.random.randint(arg_keys[4], (NOB,), 1, OBS + 1), jax.random.fold_in(arg_keys[4], 1), 1, OBS).astype(jnp.int32)
    obs_region_keys = jax.random.split(jax.random.fold_in(arg_keys[5], 1), NOB // OB_DEV)
    obs_region_turns = jax.random.permutation(jax.random.fold_in(arg_keys[5], 3), NOB // OB_DEV)
    obs_region = jax.vmap(lambda own, number: routed_block(jax.random.fold_in(arg_keys[5], 2), own, number, OB_DEV, N_TILE, 1, CAP, 2))(obs_region_keys, obs_region_turns).reshape((NOB, 1))
    obs_partner = picks_of(arg_keys[6], NOB, N_GRP * SB_DEV, K, 0)
    state_anom = scatter_about(arg_keys[7], (GROUPS, REGIONS * SB_DEV, BS, M), 1.0, 6.0, ((0, 4), (1, 64)))
    coeff = scatter_about(arg_keys[8], (GROUPS, REGIONS * SB_DEV, M, M), M ** -0.5, 0.375, ((0, 4), (1, 64)), jnp.float32)
    return {"obs_anom": obs_anom, "innov": innov, "obs_rinv": obs_rinv, "obs_pos": obs_pos, "obs_count": obs_count, "obs_region": obs_region, "obs_partner": obs_partner, "state_anom": state_anom, "coeff": coeff}


relaxation = 0.5


def taper_weights(positions, partners, counts, inverse_var, width, ensemble_members):
    center = (partners.astype(jnp.float32) + 0.5) * width
    offset = (positions.astype(jnp.float32)[..., None, :] - center[..., :, None]) / (2.0 * width)
    index = jnp.arange(positions.shape[-1], dtype=jnp.int32)
    live = index < counts[..., None]
    weight = jnp.exp(-offset * offset) * inverse_var[..., None, :] / (ensemble_members - 1.0)
    return jnp.where(live[..., None, :], weight, 0.0)


def reference(obs_anom, innov, obs_rinv, obs_pos, obs_count, obs_region, obs_partner, state_anom, coeff):
    nob, observation_count, ensemble_members = obs_anom.shape
    groups, columns, width, _ = state_anom.shape
    nlocal = N_GRP * SB_DEV
    weights = taper_weights(obs_pos, obs_partner, obs_count, obs_rinv, width, ensemble_members)

    def step(total, idx):
        start = (idx * OB_DEV).astype(jnp.int32)
        anom_part = lax.dynamic_slice_in_dim(obs_anom, start, OB_DEV, 0)
        innov_part = lax.dynamic_slice_in_dim(innov, start, OB_DEV, 0)
        weight_part = lax.dynamic_slice_in_dim(weights, start, OB_DEV, 0)
        region_part = lax.dynamic_slice_in_dim(obs_region[:, 0], start, OB_DEV, 0)
        partner_part = lax.dynamic_slice_in_dim(obs_partner, start, OB_DEV, 0)
        scaled = (weight_part[..., None] * innov_part[:, None].astype(jnp.float32)).astype(jnp.bfloat16)
        product = jnp.einsum("qim,qkin->qkmn", anom_part.astype(jnp.float32), scaled.astype(jnp.float32), precision=lax.Precision.HIGHEST)
        flat = (region_part[:, None] * nlocal + partner_part).reshape(-1).astype(jnp.int32)
        total = total.at[flat].add(product.reshape(-1, ensemble_members, ensemble_members))
        return total, None

    initial_total = jnp.zeros((N_TILE * nlocal, ensemble_members, ensemble_members), jnp.float32)
    total, _ = lax.scan(step, initial_total, jnp.arange(nob // OB_DEV, dtype=jnp.int32))
    total = total.reshape(N_TILE, N_GRP, SB_DEV, ensemble_members, ensemble_members).transpose(1, 0, 2, 3, 4)
    total = total.reshape(groups, columns, ensemble_members, ensemble_members)
    new_coeff = (1.0 - relaxation) * coeff + relaxation * total
    base_coef = ((1.0 - relaxation) * coeff).astype(jnp.bfloat16).reshape(-1, ensemble_members, ensemble_members)
    gain_coef = (relaxation * total).astype(jnp.bfloat16).reshape(-1, ensemble_members, ensemble_members)

    def one_block(items):
        anomalies, base, gain = items
        first = jnp.dot(anomalies, base, preferred_element_type=jnp.float32)
        second = jnp.dot(anomalies, gain, preferred_element_type=jnp.float32)
        return (anomalies.astype(jnp.float32) + first + second).astype(jnp.bfloat16)

    updated = lax.map(one_block, (state_anom.reshape(-1, width, ensemble_members), base_coef, gain_coef))
    return updated.reshape(state_anom.shape), new_coeff
```

```python
import jax
import jax.numpy as jnp
from jax import lax
from jax.experimental import pallas as pl
from jax.experimental.pallas import tpu as pltpu
from jax.sharding import PartitionSpec as P

relaxation = 0.5
bf16, f32, i32 = jnp.bfloat16, jnp.float32, jnp.int32
MESH = pl.DeviceIdType.MESH
MIB = 1024 * 1024

ROWS = 16
CAPS = (64, 54, 42, 30)
STAY = 40
RING = sum(CAPS)
SEND = 2 * CAPS[0] + STAY
HOPS = len(CAPS)
NZ, NY, NX, NR = 8, 4, 4, 64
LISTS = 2 * HOPS


def hop_base(way, hop):
    return way * RING + sum(CAPS[:hop])


def taper_weights(positions, partners, counts, inverse_var, width, ensemble_members):
    center = (partners.astype(jnp.float32) + 0.5) * width
    offset = (positions.astype(jnp.float32)[..., None, :] - center[..., :, None]) / (2.0 * width)
    index = jnp.arange(positions.shape[-1], dtype=jnp.int32)
    live = index < counts[..., None]
    weight = jnp.exp(-offset * offset) * inverse_var[..., None, :] / (ensemble_members - 1.0)
    return jnp.where(live[..., None, :], weight, 0.0)


def pack_kernel(region, count, partner, pos, rinv, anom, innov, send, send_w, head, wall, size, fill, first, seat_a, seat_b):
    nblock, members = anom.shape[0], anom.shape[2]
    width = 4096.0
    z = lax.axis_index("tile") // 8

    grain = lax.broadcasted_iota(i32, (128, 128), 0)
    lane = lax.broadcasted_iota(i32, (128, 128), 1)
    repeat = (lax.broadcasted_iota(i32, (128, nblock), 0) // 4 == lax.broadcasted_iota(i32, (128, nblock), 1)).astype(f32)
    column = lax.broadcasted_iota(i32, (128, 64), 1)
    quarter = (column // 16 == lax.broadcasted_iota(i32, (128, 64), 0) % 4).astype(f32)
    fold = (lax.broadcasted_iota(i32, (64, 128), 0) % 16 == lax.broadcasted_iota(i32, (64, 128), 1) % 16).astype(f32)

    def exact(a, b):
        return jnp.dot(a, b, precision=lax.Precision.HIGHEST, preferred_element_type=f32)

    def spread(values):
        return exact(exact(repeat, values) * quarter, fold)

    paired = jnp.zeros((nblock, 128), f32)
    block_of_lane = lax.broadcasted_iota(i32, (nblock, 128), 1) // 16
    for k in range(partner.shape[1]):
        paired = jnp.where(partner[:, k : k + 1] == block_of_lane, 1.0, paired)
    center = ((lane // 16).astype(f32) + 0.5) * width
    offset = (spread(pos[...].astype(f32)) - center) / (2.0 * width)
    wall[...] = jnp.exp(-offset * offset) * spread(rinv[...]) / (members - 1.0) * exact(repeat, paired)

    def clear(i, c):
        size[i] = 0
        fill[i] = 0
        for row in range(2):
            head[row, i] = 0
            head[row, i + NR] = 0
        return c

    lax.fori_loop(0, NR, clear, 0)

    def measure(o, c):
        r = region[o, 0]
        size[r] = size[r] + (count[o] + 15) // 16
        return c

    lax.fori_loop(0, nblock, measure, 0)

    def plane(distance):
        return lax.rem(z + distance, NZ) * 8

    def total(distance):
        base = plane(distance)
        return sum(size[base + i] for i in range(8))

    d = [total(distance) for distance in range(NZ)]
    right, left = d[1] + d[2] + d[3], d[5] + d[6] + d[7]
    far_right = jnp.clip((d[4] + left - right + 1) // 2, 0, d[4])
    far_left = d[4] - far_right
    loads = (
        (right + far_right, d[2] + d[3] + far_right, d[3] + far_right, far_right),
        (left + far_left, d[6] + d[5] + far_left, d[5] + far_left, far_left),
    )
    over = (d[0] > STAY).astype(i32)
    for way in range(2):
        for hop in range(HOPS):
            over = over | (loads[way][hop] > CAPS[hop]).astype(i32)
    head[1, NR] = over

    def seat_far(i, used):
        used_right, used_left = used
        r = plane(4) + i
        n = size[r]
        a = jnp.minimum(n, far_right - used_right)
        b = n - a
        head[0, r] = used_right * 256 + a
        head[0, NR + r] = used_left * 256 + b
        first[r] = a
        seat_a[r] = used_right
        seat_b[r] = CAPS[0] + used_left
        return used_right + a, used_left + b

    used_right, used_left = lax.fori_loop(0, 8, seat_far, (jnp.int32(0), jnp.int32(0)))

    def seat_near(distance, base, row, shift, used):
        def seat(i, used):
            r = plane(distance) + i
            n = size[r]
            head[row, shift + r] = used * 256 + n
            first[r] = n
            seat_a[r] = base + used
            seat_b[r] = base + used
            return used + n

        return lax.fori_loop(0, 8, seat, used)

    for distance in (3, 2, 1):
        used_right = seat_near(distance, 0, 0, 0, used_right)
    for distance in (5, 6, 7):
        used_left = seat_near(distance, CAPS[0], 0, NR, used_left)
    seat_near(0, 2 * CAPS[0], 1, 0, jnp.int32(0))

    row_of_lane = lax.broadcasted_iota(i32, (1, 128), 1) % 16

    def place(o, c):
        r, live = region[o, 0], count[o]
        grains = (live + 15) // 16
        start = fill[r]
        fill[r] = start + grains
        a, b, most = seat_a[r], seat_b[r], first[r]

        def one(q, c):
            f = start + q
            slot = jnp.minimum(jnp.where(f < most, a + f, b + f - most), SEND - 1)
            rows = pl.ds(pl.multiple_of(q * ROWS, ROWS), ROWS)
            send[slot, :, 0:members] = anom[o, rows, :]
            send[slot, :, members : 2 * members] = innov[o, rows, :]
            weight = wall[pl.ds(o * 4 + q, 1), :]
            send_w[pl.ds(slot, 1), :] = jnp.where(row_of_lane < live - q * ROWS, weight, 0.0)
            return c

        return lax.fori_loop(0, grains, one, c)

    lax.fori_loop(0, nblock, place, 0)


def pack(region, count, partner, pos, rinv, anom, innov):
    members = anom.shape[2]
    vmem, smem = pl.BlockSpec(memory_space=pltpu.VMEM), pl.BlockSpec(memory_space=pltpu.SMEM)
    return pl.pallas_call(
        pack_kernel,
        out_shape=(
            jax.ShapeDtypeStruct((SEND, ROWS, 2 * members), bf16),
            jax.ShapeDtypeStruct((SEND, 128), f32),
            jax.ShapeDtypeStruct((8, 128), i32),
        ),
        in_specs=[smem, smem, vmem, vmem, vmem, vmem, vmem],
        out_specs=(vmem, vmem, smem),
        scratch_shapes=[pltpu.VMEM((128, 128), f32)] + [pltpu.SMEM((NR,), i32)] * 5,
        compiler_params=pltpu.CompilerParams(vmem_limit_bytes=32 * MIB),
    )(region, count, partner, pos, rinv, anom, innov)


def ring_kernel(send, send_w, head, zm, zs, wm, ws, hm, hs, zsend, zrecv, ssend, srecv, osend, orecv):
    tile = lax.axis_index("tile")
    z, inner = tile // 8, tile % 8
    ways = (lax.rem(z + 1, NZ) * 8 + inner, lax.rem(z + NZ - 1, NZ) * 8 + inner)
    sibling = tile + 1 - 2 * (tile % 2)

    barrier = pltpu.get_barrier_semaphore()
    for other in (*ways, sibling):
        pl.semaphore_signal(barrier, inc=1, device_id={"tile": other}, device_id_type=MESH)
    pl.semaphore_wait(barrier, 3)

    def copy(src, dst, send_sem, recv_sem, other):
        return pltpu.make_async_remote_copy(
            src_ref=src, dst_ref=dst, send_sem=send_sem, recv_sem=recv_sem, device_id={"tile": other}, device_id_type=MESH
        )

    edges = (0, *CAPS[::-1])

    def hop_copies(way, hop):
        out = []
        for k in range(HOPS - hop):
            lo, n = edges[k], edges[k + 1] - edges[k]
            if hop == 0:
                src = send.at[pl.ds(way * CAPS[0] + lo, n)]
            else:
                src = zm.at[pl.ds(hop_base(way, hop - 1) + lo, n)]
            out.append((k, src, zm.at[pl.ds(hop_base(way, hop) + lo, n)]))
        entry = way * HOPS + hop
        src_w = send_w.at[pl.ds(way * CAPS[0], CAPS[0])] if hop == 0 else wm.at[entry - 1]
        src_h = head if hop == 0 else hm.at[entry - 1]
        out.append((4, src_w, wm.at[entry]))
        out.append((5, src_h, hm.at[entry]))
        return {
            k: copy(src, dst, zsend.at[way, hop, k], zrecv.at[way, hop, k], ways[way]) for k, src, dst in out
        }

    def sibling_copies(way, hop):
        entry = way * HOPS + hop
        span = pl.ds(hop_base(way, hop), CAPS[hop])
        pairs = ((zm.at[span], zs.at[span]), (wm.at[entry], ws.at[entry]), (hm.at[entry], hs.at[entry]))
        return [copy(s, t, ssend.at[entry, i], srecv.at[entry, i], sibling) for i, (s, t) in enumerate(pairs)]

    z_copies = [[hop_copies(way, hop) for hop in range(HOPS)] for way in range(2)]
    order = [[5, 4, *range(HOPS - hop)] for hop in range(HOPS)]
    for k in order[0]:
        for way in range(2):
            z_copies[way][0][k].start()
    side = [
        copy(send.at[pl.ds(2 * CAPS[0], STAY)], zs.at[pl.ds(2 * RING, STAY)], osend.at[0], orecv.at[0], sibling),
        copy(send_w.at[pl.ds(2 * CAPS[0], STAY)], ws.at[LISTS, pl.ds(0, STAY)], osend.at[1], orecv.at[1], sibling),
        copy(head, hs.at[LISTS], osend.at[2], orecv.at[2], sibling),
    ]
    for c in side:
        c.start()
    for hop in range(HOPS):
        for k in order[hop]:
            for way in range(2):
                z_copies[way][hop][k].wait_recv()
                if hop + 1 < HOPS and k in z_copies[way][hop + 1]:
                    z_copies[way][hop + 1][k].start()
        for way in range(2):
            more = sibling_copies(way, hop)
            for c in more:
                c.start()
            side += more
    for way in range(2):
        for hop in range(HOPS):
            for k in order[hop]:
                z_copies[way][hop][k].wait_send()
    for c in side:
        c.wait()


def ring(send, send_w, head):
    hbm = pl.BlockSpec(memory_space=pl.ANY)
    members2 = send.shape[2]
    dma = pltpu.SemaphoreType.DMA
    return pl.pallas_call(
        ring_kernel,
        out_shape=(
            jax.ShapeDtypeStruct((2 * RING, ROWS, members2), bf16),
            jax.ShapeDtypeStruct((2 * RING + STAY, ROWS, members2), bf16),
            jax.ShapeDtypeStruct((LISTS, CAPS[0], 128), f32),
            jax.ShapeDtypeStruct((LISTS + 1, CAPS[0], 128), f32),
            jax.ShapeDtypeStruct((LISTS, 8, 128), i32),
            jax.ShapeDtypeStruct((LISTS + 1, 8, 128), i32),
        ),
        in_specs=[hbm] * 3,
        out_specs=(hbm,) * 6,
        scratch_shapes=[
            dma((2, HOPS, 6)),
            dma((2, HOPS, 6)),
            dma((LISTS, 3)),
            dma((LISTS, 3)),
            dma((3,)),
            dma((3,)),
        ],
        compiler_params=pltpu.CompilerParams(collective_id=0, has_side_effects=True),
    )(send, send_w, head)


def partial_kernel(head, hm, hs, send, send_w, zm, zs, wm, ws, p, flag, v, wv, pa, pn, pw, acc, sem):
    members = pa.shape[1]
    tile = lax.axis_index("tile")
    z, core = tile // 8, tile % 2
    mine = 2 * RING + STAY
    loads = (
        (zm, v.at[pl.ds(0, 2 * RING)]),
        (send.at[pl.ds(2 * CAPS[0], STAY)], v.at[pl.ds(2 * RING, STAY)]),
        (zs, v.at[pl.ds(mine, mine)]),
        (wm, wv.at[pl.ds(0, LISTS)]),
        (send_w.at[pl.ds(2 * CAPS[0], STAY)], wv.at[LISTS, pl.ds(0, STAY)]),
        (ws, wv.at[pl.ds(LISTS + 1, LISTS + 1)]),
    )
    copies = [pltpu.make_async_copy(s, t, sem.at[i]) for i, (s, t) in enumerate(loads)]
    for c in copies:
        c.start()

    over = head[1, NR]
    for i in range(LISTS):
        over = over | hm[i, 1, NR] | hs[i, 1, NR]
    over = over | hs[LISTS, 1, NR]
    flag[...] = jnp.full(flag.shape, over, i32).astype(f32)

    expand = (lax.broadcasted_iota(i32, (256, 16), 0) // 16 == lax.broadcasted_iota(i32, (256, 16), 1)).astype(bf16)
    keep = (lax.broadcasted_iota(i32, (256, 128), 0) % 16 == lax.broadcasted_iota(i32, (256, 128), 1) % 16).astype(f32)
    pick = (lax.broadcasted_iota(i32, (8, 128), 1) // 16 == lax.broadcasted_iota(i32, (8, 128), 0)).astype(bf16)

    lists = []
    for who in range(2):
        for way in range(2):
            for hop in range(HOPS):
                entry = way * HOPS + hop
                source = hs if who else hm
                lists.append((source, entry, 0, way * NR, who * mine + hop_base(way, hop), CAPS[hop], who * (LISTS + 1) + entry))
        lists.append((hs if who else head, LISTS if who else None, 1, 0, who * mine + 2 * RING, STAY, who * (LISTS + 1) + LISTS))

    for c in copies:
        c.wait()

    def one_region(yp, carry):
        r = z * 8 + yp * 2 + core
        n = jnp.int32(0)
        for source, entry, row, shift, base, cap, wlist in lists:
            value = source[row, shift + r] if entry is None else source[entry, row, shift + r]
            start, grains = value // 256, value % 256
            grains = jnp.clip(cap - start, 0, grains)

            def gather(i, n, base=base, start=start, wlist=wlist):
                slot = start + i
                rows = pl.ds(pl.multiple_of(n * ROWS, ROWS), ROWS)
                pa[rows, :] = v[base + slot, :, 0:members]
                pn[rows, :] = v[base + slot, :, members : 2 * members]
                pw[pl.ds(n, 1), :] = wv[wlist, pl.ds(slot, 1), :]
                return n + 1

            n = lax.fori_loop(0, grains, gather, n)
        chunks = (n + 15) // 16

        def blank(i, c):
            rows = pl.ds(pl.multiple_of(i * ROWS, ROWS), ROWS)
            pa[rows, :] = jnp.zeros((ROWS, members), bf16)
            pn[rows, :] = jnp.zeros((ROWS, members), bf16)
            pw[pl.ds(i, 1), :] = jnp.zeros((1, 128), f32)
            return c

        lax.fori_loop(n, chunks * 16, blank, 0)
        acc[...] = jnp.zeros_like(acc)

        def chunk(k, c):
            rows = pl.ds(pl.multiple_of(k * 256, 256), 256)
            grains = pw[pl.ds(pl.multiple_of(k * 16, 16), 16), :].astype(bf16)
            wide = jnp.dot(expand, grains, preferred_element_type=f32) * keep
            weight = lax.dot_general(pick, wide.astype(bf16), (((1,), (1,)), ((), ())), preferred_element_type=f32)
            turned = pa[rows, :].astype(f32).T
            innovation = pn[rows, :]
            for b in range(8):
                scaled = (turned * weight[b : b + 1, :]).astype(bf16)
                acc[b] += jnp.dot(scaled, innovation, preferred_element_type=f32)
            return c

        lax.fori_loop(0, chunks, chunk, 0)
        for xp in range(NX):
            p[0, yp, xp] = acc[2 * xp].astype(bf16)
            p[1, xp, yp] = acc[2 * xp + 1].astype(bf16)
        return carry

    lax.fori_loop(0, NY, one_region, 0)


def partials(head, hm, hs, send, send_w, zm, zs, wm, ws):
    members = send.shape[2] // 2
    hbm, smem = pl.BlockSpec(memory_space=pl.ANY), pl.BlockSpec(memory_space=pltpu.SMEM)
    vmem = pl.BlockSpec(memory_space=pltpu.VMEM)
    most = 16 * 8
    return pl.pallas_call(
        partial_kernel,
        out_shape=(
            jax.ShapeDtypeStruct((2, 4, 4, members, members), bf16),
            jax.ShapeDtypeStruct((8, 128), f32),
        ),
        in_specs=[smem] * 3 + [hbm] * 6,
        out_specs=(vmem, vmem),
        scratch_shapes=[
            pltpu.VMEM((2 * (2 * RING + STAY), ROWS, 2 * members), bf16),
            pltpu.VMEM((2 * (LISTS + 1), CAPS[0], 128), f32),
            pltpu.VMEM((most * ROWS, members), bf16),
            pltpu.VMEM((most * ROWS, members), bf16),
            pltpu.VMEM((most, 128), f32),
            pltpu.VMEM((8, members, members), f32),
            pltpu.SemaphoreType.DMA((6,)),
        ],
        compiler_params=pltpu.CompilerParams(vmem_limit_bytes=48 * MIB),
    )(head, hm, hs, send, send_w, zm, zs, wm, ws)


def reduce_kernel(p, flag, total, flag_out, ro, rd, sb, u, ro2, rd2, sb2, ff, sems, recvs, fsend, frecv):
    x, tile = lax.axis_index("grp"), lax.axis_index("tile")
    z, y, core = tile // 8, (tile % 8) // 2, tile % 2

    def along(axis, step):
        if axis == 0:
            return x, z * 8 + lax.rem(y + step, NY) * 2 + core
        return lax.rem(x + step, NX), tile

    barrier = pltpu.get_barrier_semaphore()
    for axis in range(2):
        for step in (1, 3):
            pl.semaphore_signal(barrier, inc=1, device_id=along(axis, step), device_id_type=MESH)
    pl.semaphore_wait(barrier, 4)

    def copy(src, dst, half, phase, k, axis, step):
        return pltpu.make_async_remote_copy(
            src_ref=src, dst_ref=dst, send_sem=sems.at[half, phase, k], recv_sem=recvs.at[half, phase, k],
            device_id=along(axis, step), device_id_type=MESH,
        )

    def flag_copy(src, dst, k, axis, step):
        return pltpu.make_async_remote_copy(
            src_ref=ff.at[src], dst_ref=ff.at[dst], send_sem=fsend.at[k], recv_sem=frecv.at[k],
            device_id=along(axis, step), device_id_type=MESH,
        )

    ff[0] = flag[...]
    flags = [flag_copy(0, 1, 0, 0, 1), flag_copy(0, 2, 1, 0, 3)]
    for c in flags:
        c.start()

    first = []
    for half in range(2):
        me = y if half == 0 else x
        right, left, far = lax.rem(me + 1, 4), lax.rem(me + 3, 4), lax.rem(me + 2, 4)
        lo, hi = pl.ds(0, 2), pl.ds(2, 2)
        first.append([
            copy(p.at[half, far, lo], ro.at[half, 0], half, 0, 0, half, 1),
            copy(p.at[half, far, hi], ro.at[half, 1], half, 0, 1, half, 3),
            copy(p.at[half, right, hi], rd.at[half, 0, hi], half, 0, 2, half, 1),
            copy(p.at[half, left, lo], rd.at[half, 1, lo], half, 0, 3, half, 3),
            copy(sb.at[half, 0], rd.at[half, 0, lo], half, 0, 4, half, 1),
            copy(sb.at[half, 1], rd.at[half, 1, hi], half, 0, 5, half, 3),
        ])
    for k in range(4):
        for half in range(2):
            first[half][k].start()

    flags[0].wait_recv()
    ff[3] = ff[0] + ff[1]
    flags.append(flag_copy(3, 4, 2, 0, 1))
    flags[2].start()

    def wide(ref):
        return ref[...].astype(f32)

    for k in range(2):
        for half in range(2):
            me = y if half == 0 else x
            to = lax.rem(me + (1 if k == 0 else 3), 4)
            first[half][k].wait_recv()
            for i in range(2):
                sb[half, k, i] = (wide(p.at[half, to, 2 * k + i]) + wide(ro.at[half, k, i])).astype(bf16)
            first[half][4 + k].start()

    flags[1].wait_recv()
    flags[2].wait_recv()
    ff[5] = ff[0] + ff[2] + ff[4]
    flags += [flag_copy(5, 6, 3, 1, 1), flag_copy(5, 7, 4, 1, 3)]
    flags[3].start()
    flags[4].start()

    second = []
    for half in range(2):
        me, other = (y, x) if half == 0 else (x, y)
        for k in (2, 3, 4, 5):
            first[half][k].wait_recv()
        for i in range(4):
            u[half, i] = (wide(p.at[half, me, i]) + wide(rd.at[half, 0, i]) + wide(rd.at[half, 1, i])).astype(bf16)
        axis = 1 - half
        right, left, far = lax.rem(other + 1, 4), lax.rem(other + 3, 4), lax.rem(other + 2, 4)
        rows = u.shape[2] // 2
        lo, hi = pl.ds(0, rows), pl.ds(rows, rows)
        second.append([
            copy(u.at[half, far, lo], ro2.at[half, 0], half, 1, 0, axis, 1),
            copy(u.at[half, far, hi], ro2.at[half, 1], half, 1, 1, axis, 3),
            copy(u.at[half, right, hi], rd2.at[half, 0, hi], half, 1, 2, axis, 1),
            copy(u.at[half, left, lo], rd2.at[half, 1, lo], half, 1, 3, axis, 3),
            copy(sb2.at[half, 0], rd2.at[half, 0, lo], half, 1, 4, axis, 1),
            copy(sb2.at[half, 1], rd2.at[half, 1, hi], half, 1, 5, axis, 3),
        ])
        for k in range(4):
            second[half][k].start()

    flags[3].wait_recv()
    ff[8] = ff[5] + ff[6]
    flags.append(flag_copy(8, 9, 5, 1, 1))
    flags[5].start()

    for half in range(2):
        other = x if half == 0 else y
        rows = u.shape[2] // 2
        for k in range(2):
            to = lax.rem(other + (1 if k == 0 else 3), 4)
            second[half][k].wait_recv()
            sb2[half, k] = (wide(u.at[half, to, pl.ds(k * rows, rows)]) + wide(ro2.at[half, k])).astype(bf16)
            second[half][4 + k].start()

    flags[4].wait_recv()
    flags[5].wait_recv()
    flag_out[...] = ff[5] + ff[7] + ff[9]

    for half in range(2):
        other = x if half == 0 else y
        for k in (2, 3, 4, 5):
            second[half][k].wait_recv()
        total[half] = wide(u.at[half, other]) + wide(rd2.at[half, 0]) + wide(rd2.at[half, 1])

    for c in (*first[0], *first[1], *second[0], *second[1], *flags):
        c.wait_send()


def reduce_plane(p, flag):
    members = p.shape[-1]
    vmem = pl.BlockSpec(memory_space=pltpu.VMEM)
    square = (members, members)
    dma = pltpu.SemaphoreType.DMA
    return pl.pallas_call(
        reduce_kernel,
        out_shape=(jax.ShapeDtypeStruct((2, *square), f32), jax.ShapeDtypeStruct((8, 128), f32)),
        in_specs=[vmem] * 2,
        out_specs=(vmem, vmem),
        scratch_shapes=[
            pltpu.VMEM((2, 2, 2, *square), bf16),
            pltpu.VMEM((2, 2, 4, *square), bf16),
            pltpu.VMEM((2, 2, 2, *square), bf16),
            pltpu.VMEM((2, 4, *square), bf16),
            pltpu.VMEM((2, 2, members // 2, members), bf16),
            pltpu.VMEM((2, 2, *square), bf16),
            pltpu.VMEM((2, 2, members // 2, members), bf16),
            pltpu.VMEM((10, 8, 128), f32),
            dma((2, 2, 6)),
            dma((2, 2, 6)),
            dma((6,)),
            dma((6,)),
        ],
        compiler_params=pltpu.CompilerParams(collective_id=1, has_side_effects=True, vmem_limit_bytes=32 * MIB),
    )(p, flag)


def update_kernel(state, coeff, total, updated, new_coeff, coef):
    @pl.when(pl.program_id(1) == 0)
    def _():
        base = (1.0 - relaxation) * coeff[...]
        gain = relaxation * total[...]
        new_coeff[...] = base + gain
        coef[0] = base.astype(bf16)
        coef[1] = gain.astype(bf16)

    s = state[...]
    moved = jnp.dot(s, coef[0], preferred_element_type=f32) + jnp.dot(s, coef[1], preferred_element_type=f32)
    updated[...] = (s.astype(f32) + moved).astype(bf16)


def update(state, coeff, total):
    _, blocks, width, members = state.shape
    step = 1024
    square = (members, members)
    rows = pl.BlockSpec((None, None, step, members), lambda j, i: (0, j, i, 0))
    one = pl.BlockSpec((None, None, *square), lambda j, i: (0, j, 0, 0))
    return pl.pallas_call(
        update_kernel,
        grid=(blocks, width // step),
        out_shape=(jax.ShapeDtypeStruct(state.shape, bf16), jax.ShapeDtypeStruct(coeff.shape, f32)),
        in_specs=[rows, one, pl.BlockSpec((None, *square), lambda j, i: (j, 0, 0))],
        out_specs=(rows, one),
        scratch_shapes=[pltpu.VMEM((2, *square), bf16)],
        compiler_params=pltpu.CompilerParams(vmem_limit_bytes=32 * MIB),
    )(state, coeff, total)


def padded_total(obs_anom, innov, obs_rinv, obs_pos, obs_count, obs_region, obs_partner, blocks, width):
    tile_count = lax.axis_size("tile")
    nblock, observation_count, ensemble_members = obs_anom.shape
    partition_count = obs_partner.shape[1]
    nlocal = lax.axis_size("grp") * blocks
    per_neighbour = max(2, (2 * nblock + tile_count - 1) // tile_count)
    slot_count = tile_count * per_neighbour
    slot_grouping = 8
    region = obs_region[:, 0]
    order = jnp.arange(nblock, dtype=jnp.int32)
    before = (region[None, :] == region[:, None]) & (order[None, :] < order[:, None])
    destination = region * per_neighbour + jnp.sum(before.astype(jnp.int32), axis=1)
    assignment_rule = destination[None, :] == jnp.arange(slot_count, dtype=jnp.int32)[:, None]
    place_half = assignment_rule.astype(jnp.bfloat16)
    place_int = assignment_rule.astype(jnp.int32)
    labels = jnp.concatenate([obs_count[:, None], obs_partner], axis=1)
    sent_labels = jnp.dot(place_int, labels).reshape(tile_count, per_neighbour, partition_count + 1)
    stacked = jnp.concatenate([obs_anom, innov], axis=2).reshape(nblock, -1)
    packed = jnp.dot(place_half, stacked, preferred_element_type=jnp.bfloat16)
    packed = packed.reshape(tile_count, per_neighbour, observation_count, 2 * ensemble_members)
    sent_pos = jnp.dot(place_int, obs_pos).reshape(tile_count, per_neighbour, observation_count)
    sent_var = jnp.dot(assignment_rule.astype(jnp.float32), obs_rinv, precision=lax.Precision.HIGHEST)
    sent_var = sent_var.reshape(tile_count, per_neighbour, observation_count)

    def exchange(array):
        return lax.all_to_all(array, "tile", split_axis=0, concat_axis=0, tiled=True)

    received_panels = exchange(packed).reshape(slot_count, observation_count, 2 * ensemble_members)
    flattened_labels = exchange(sent_labels).reshape(slot_count, partition_count + 1)
    recv_anom = received_panels[:, :, :ensemble_members]
    recv_innov = received_panels[:, :, ensemble_members:]
    flattened_positions = exchange(sent_pos).reshape(slot_count, observation_count)
    flattened_variances = exchange(sent_var).reshape(slot_count, observation_count)
    partners = flattened_labels[:, 1:]
    block_index = jnp.arange(nlocal, dtype=jnp.int32)

    def accumulate_group(step, total):
        start = step * slot_grouping

        def part(array):
            return lax.dynamic_slice_in_dim(array, start, slot_grouping, 0)

        weights = taper_weights(
            part(flattened_positions), part(partners), part(flattened_labels)[:, 0], part(flattened_variances), width,
            ensemble_members,
        )
        scaled_part = (weights[..., None] * part(recv_innov)[:, None].astype(jnp.float32)).astype(jnp.bfloat16)
        picked = (part(partners)[..., None] == block_index).astype(jnp.bfloat16)
        by_block = jnp.einsum("qkb,qkin->qbin", picked, scaled_part, preferred_element_type=jnp.float32).astype(jnp.bfloat16)
        return total + jnp.einsum("qim,qbin->bmn", part(recv_anom), by_block, preferred_element_type=jnp.float32)

    initial_total = jnp.zeros((nlocal, ensemble_members, ensemble_members), jnp.float32)
    running_totals = lax.fori_loop(0, slot_count // slot_grouping, accumulate_group, initial_total)
    return lax.psum_scatter(running_totals.astype(jnp.bfloat16), "grp", scatter_dimension=0, tiled=True).astype(jnp.float32)


def on_device(obs_anom, innov, obs_rinv, obs_pos, obs_count, obs_region, obs_partner, state_anom, coeff):
    send, send_w, head = pack(obs_region, obs_count, obs_partner, obs_pos, obs_rinv, obs_anom, innov)
    zm, zs, wm, ws, hm, hs = ring(send, send_w, head)
    p, flag = partials(head, hm, hs, send, send_w, zm, zs, wm, ws)
    fast, flags = reduce_plane(p, flag)
    blocks, width = state_anom.shape[1:3]
    total = lax.cond(
        flags[0, 0] > 0,
        lambda *obs: padded_total(*obs[:-1], blocks, width),
        lambda *obs: obs[-1],
        obs_anom, innov, obs_rinv, obs_pos, obs_count, obs_region, obs_partner, fast,
    )
    return update(state_anom, coeff, total)


def solution(mesh):
    return jax.shard_map(
        on_device,
        mesh=mesh,
        in_specs=(
            P(("grp", "tile"), None, None),
            P(("grp", "tile"), None, None),
            P(("grp", "tile"), None),
            P(("grp", "tile"), None),
            P(("grp", "tile")),
            P(("grp", "tile"), None),
            P(("grp", "tile"), None),
            P("grp", "tile", None, None),
            P("grp", "tile", None, None),
        ),
        out_specs=(P("grp", "tile", None, None), P("grp", "tile", None, None)),
        check_vma=False,
    )
```

```python
import jax
import jax.numpy as jnp
from jax import lax
from jax.experimental import pallas as pl
from jax.experimental.pallas import tpu as pltpu
from jax.sharding import PartitionSpec as P

relaxation = 0.5
bf16, f32, i32 = jnp.bfloat16, jnp.float32, jnp.int32
MESH = pl.DeviceIdType.MESH
MIB = 1024 * 1024

ROWS = 16
CAPS = (64, 50, 40, 28)
STAY = 40
SEND = 2 * CAPS[0] + STAY
HOPS = len(CAPS)
NZ, NY, NX, NR = 8, 4, 4, 64
LISTS = 2 * HOPS


def taper_weights(positions, partners, counts, inverse_var, width, ensemble_members):
    center = (partners.astype(jnp.float32) + 0.5) * width
    offset = (positions.astype(jnp.float32)[..., None, :] - center[..., :, None]) / (2.0 * width)
    index = jnp.arange(positions.shape[-1], dtype=jnp.int32)
    live = index < counts[..., None]
    weight = jnp.exp(-offset * offset) * inverse_var[..., None, :] / (ensemble_members - 1.0)
    return jnp.where(live[..., None, :], weight, 0.0)


def pack_kernel(region, count, partner, pos, rinv, anom, innov, send, send_w, head, wall, size, fill, first, seat_a, seat_b):
    nblock, members = anom.shape[0], anom.shape[2]
    width = 4096.0
    z = lax.axis_index("tile") // 8

    lane = lax.broadcasted_iota(i32, (128, 128), 1)
    repeat = (lax.broadcasted_iota(i32, (128, nblock), 0) // 4 == lax.broadcasted_iota(i32, (128, nblock), 1)).astype(f32)
    column = lax.broadcasted_iota(i32, (128, 64), 1)
    quarter = (column // 16 == lax.broadcasted_iota(i32, (128, 64), 0) % 4).astype(f32)
    fold = (lax.broadcasted_iota(i32, (64, 128), 0) % 16 == lax.broadcasted_iota(i32, (64, 128), 1) % 16).astype(f32)

    def exact(a, b):
        return jnp.dot(a, b, precision=lax.Precision.HIGHEST, preferred_element_type=f32)

    def spread(values):
        return exact(exact(repeat, values) * quarter, fold)

    partners = lax.dot_general(
        repeat, partner[...].astype(f32), (((1,), (1,)), ((), ())), precision=lax.Precision.HIGHEST, preferred_element_type=f32
    )
    block_of_lane = (lane // 16).astype(f32)
    paired = jnp.zeros((128, 128), f32)
    for k in range(partner.shape[0]):
        paired = jnp.where(partners[:, k : k + 1] == block_of_lane, 1.0, paired)
    center = (block_of_lane + 0.5) * width
    offset = (spread(pos[...].astype(f32)) - center) / (2.0 * width)
    wall[...] = jnp.exp(-offset * offset) * spread(rinv[...]) / (members - 1.0) * paired

    def clear(i, c):
        size[i] = 0
        fill[i] = 0
        return c

    lax.fori_loop(0, NR, clear, 0)

    def blank(i, c):
        send[i] = jnp.zeros(send.shape[1:], bf16)
        return c

    lax.fori_loop(0, SEND, blank, 0)
    send_w[...] = jnp.zeros_like(send_w)

    def measure(o, c):
        r = region[o]
        size[r] = size[r] + (count[o] + 15) // 16
        return c

    lax.fori_loop(0, nblock, measure, 0)

    def plane(distance):
        return lax.rem(z + distance, NZ) * 8

    def total(distance):
        base = plane(distance)
        return sum(size[base + i] for i in range(8))

    d = [total(distance) for distance in range(NZ)]
    right, left = d[1] + d[2] + d[3], d[5] + d[6] + d[7]
    far_right = jnp.clip((d[4] + left - right + 1) // 2, 0, d[4])
    far_left = d[4] - far_right
    loads = (
        (right + far_right, d[2] + d[3] + far_right, d[3] + far_right, far_right),
        (left + far_left, d[6] + d[5] + far_left, d[5] + far_left, far_left),
    )
    over = (d[0] > STAY).astype(i32)
    for way in range(2):
        for hop in range(HOPS):
            over = over | (loads[way][hop] > CAPS[hop]).astype(i32)

    head_row = lax.broadcasted_iota(i32, (8, 128), 0)
    head_lane = lax.broadcasted_iota(i32, (8, 128), 1)

    def noted(header, row, at, value):
        return jnp.where((head_row == row) & (head_lane == at), value, header)

    header = noted(jnp.zeros((8, 128), i32), 1, NR, over)

    def seat_far(i, carry):
        used_right, used_left, header = carry
        r = plane(4) + i
        n = size[r]
        a = jnp.minimum(n, far_right - used_right)
        b = n - a
        header = noted(noted(header, 0, r, used_right * 256 + a), 0, NR + r, used_left * 256 + b)
        first[r] = a
        seat_a[r] = used_right
        seat_b[r] = CAPS[0] + used_left
        return used_right + a, used_left + b, header

    used_right, used_left, header = lax.fori_loop(0, 8, seat_far, (jnp.int32(0), jnp.int32(0), header))

    def seat_near(distance, base, row, shift, carry):
        def seat(i, carry):
            used, header = carry
            r = plane(distance) + i
            n = size[r]
            first[r] = n
            seat_a[r] = base + used
            seat_b[r] = base + used
            return used + n, noted(header, row, shift + r, used * 256 + n)

        return lax.fori_loop(0, 8, seat, carry)

    for distance in (3, 2, 1):
        used_right, header = seat_near(distance, 0, 0, 0, (used_right, header))
    for distance in (5, 6, 7):
        used_left, header = seat_near(distance, CAPS[0], 0, NR, (used_left, header))
    _, header = seat_near(0, 2 * CAPS[0], 1, 0, (jnp.int32(0), header))
    head[...] = header

    row_of_lane = lax.broadcasted_iota(i32, (1, 128), 1) % 16

    def place(o, c):
        r, live = region[o], count[o]
        grains = (live + 15) // 16
        start = fill[r]
        fill[r] = start + grains
        a, b, most = seat_a[r], seat_b[r], first[r]

        def one(q, c):
            f = start + q
            slot = jnp.minimum(jnp.where(f < most, a + f, b + f - most), SEND - 1)
            rows = pl.ds(pl.multiple_of(q * ROWS, ROWS), ROWS)
            send[slot, :, 0:members] = anom[o, rows, :]
            send[slot, :, members : 2 * members] = innov[o, rows, :]
            weight = wall[pl.ds(o * 4 + q, 1), :]
            send_w[pl.ds(slot, 1), :] = jnp.where(row_of_lane < live - q * ROWS, weight, 0.0)
            return c

        return lax.fori_loop(0, grains, one, c)

    lax.fori_loop(0, nblock, place, 0)


def pack(region, count, partner, pos, rinv, anom, innov):
    members = anom.shape[2]
    vmem, smem = pl.BlockSpec(memory_space=pltpu.VMEM), pl.BlockSpec(memory_space=pltpu.SMEM)
    return pl.pallas_call(
        pack_kernel,
        out_shape=(
            jax.ShapeDtypeStruct((SEND, ROWS, 2 * members), bf16),
            jax.ShapeDtypeStruct((SEND, 128), f32),
            jax.ShapeDtypeStruct((8, 128), i32),
        ),
        in_specs=[smem, smem, vmem, vmem, vmem, vmem, vmem],
        out_specs=(vmem, vmem, vmem),
        scratch_shapes=[pltpu.VMEM((128, 128), f32)] + [pltpu.SMEM((NR,), i32)] * 5,
        compiler_params=pltpu.CompilerParams(vmem_limit_bytes=16 * MIB),
    )(region, count, partner, pos, rinv, anom, innov)


def exchange_kernel(send, send_w, head, total, flag_out, *scratch):
    scratch = list(scratch)

    def take(n):
        out = scratch[:n]
        del scratch[:n]
        return out

    zm, zs, wm, ws = take(LISTS), take(LISTS + 1), take(LISTS), take(LISTS + 1)
    hm, hs, hsm, pa, pn, pw, acc, p, ro, rd, sb, u, ro2, rd2, sb2, ff = take(16)
    zsend, zrecv, ssend, srecv, osend, orecv, hsem, sems, recvs, fsend, frecv = take(11)

    members = pa.shape[1]
    x, tile = lax.axis_index("grp"), lax.axis_index("tile")
    z, inner = tile // 8, tile % 8
    y, core = inner // 2, inner % 2
    sibling = tile + 1 - 2 * core

    def around(step):
        return x, lax.rem(z + step, NZ) * 8 + inner

    def along(axis, step):
        if axis == 0:
            return x, z * 8 + lax.rem(y + step, NY) * 2 + core
        return lax.rem(x + step, NX), tile

    ways = (around(1), around(NZ - 1))
    barrier = pltpu.get_barrier_semaphore()
    for other in (*ways, (x, sibling), along(0, 1), along(0, 3), along(1, 1), along(1, 3)):
        pl.semaphore_signal(barrier, inc=1, device_id=other, device_id_type=MESH)
    pl.semaphore_wait(barrier, 7)

    def copy(src, dst, send_sem, recv_sem, other):
        return pltpu.make_async_remote_copy(
            src_ref=src, dst_ref=dst, send_sem=send_sem, recv_sem=recv_sem, device_id=other, device_id_type=MESH
        )

    edges = (0, *CAPS[::-1])

    def hop_copies(way, hop):
        entry = way * HOPS + hop
        out = []
        for k in range(HOPS - hop):
            lo, n = edges[k], edges[k + 1] - edges[k]
            src = send.at[pl.ds(way * CAPS[0] + lo, n)] if hop == 0 else zm[entry - 1].at[pl.ds(lo, n)]
            out.append((k, src, zm[entry].at[pl.ds(lo, n)]))
        out.append((4, send_w.at[pl.ds(way * CAPS[0], CAPS[0])] if hop == 0 else wm[entry - 1], wm[entry]))
        out.append((5, head if hop == 0 else hm.at[entry - 1], hm.at[entry]))
        return {k: copy(src, dst, zsend.at[way, hop, k], zrecv.at[way, hop, k], ways[way]) for k, src, dst in out}

    z_copies = [[hop_copies(way, hop) for hop in range(HOPS)] for way in range(2)]
    order = [[5, 4, *range(HOPS - hop)] for hop in range(HOPS)]
    side = [
        [copy(s, t, ssend.at[e, i], srecv.at[e, i], (x, sibling)) for i, (s, t) in enumerate(
            ((hm.at[e], hs.at[e]), (zm[e], zs[e]), (wm[e], ws[e])))]
        for e in range(LISTS)
    ]
    stay = pl.ds(2 * CAPS[0], STAY)
    side.append([
        copy(head, hs.at[LISTS], osend.at[0], orecv.at[0], (x, sibling)),
        copy(send.at[stay], zs[LISTS], osend.at[1], orecv.at[1], (x, sibling)),
        copy(send_w.at[stay], ws[LISTS], osend.at[2], orecv.at[2], (x, sibling)),
    ])
    to_scalar = [pltpu.make_async_copy(hm.at[e], hsm.at[e], hsem.at[e]) for e in range(LISTS)]
    to_scalar.append(pltpu.make_async_copy(head, hsm.at[LISTS], hsem.at[LISTS]))
    to_scalar += [pltpu.make_async_copy(hs.at[e], hsm.at[LISTS + 1 + e], hsem.at[LISTS + 1 + e]) for e in range(LISTS + 1)]

    for k in order[0]:
        for way in range(2):
            z_copies[way][0][k].start()
    for c in side[LISTS]:
        c.start()
    to_scalar[LISTS].start()

    expand = (lax.broadcasted_iota(i32, (256, 16), 0) // 16 == lax.broadcasted_iota(i32, (256, 16), 1)).astype(bf16)
    keep = (lax.broadcasted_iota(i32, (256, 128), 0) % 16 == lax.broadcasted_iota(i32, (256, 128), 1) % 16).astype(f32)
    pick = (lax.broadcasted_iota(i32, (8, 128), 1) // 16 == lax.broadcasted_iota(i32, (8, 128), 0)).astype(bf16)

    def accumulate(entry, row, shift, cap, mode):
        own = entry == LISTS
        halves = (
            (send if own else zm[entry], send_w if own else wm[entry], entry, 2 * CAPS[0] if own else 0),
            (zs[entry], ws[entry], LISTS + 1 + entry, 0),
        )

        def one_region(yp, carry):
            r = z * 8 + yp * 2 + core
            for half, (panels, weights, at, base) in enumerate(halves):
                value = hsm[at, row, shift + r]
                start, grains = value // 256, value % 256
                for i in range(8):
                    slot = base + jnp.minimum(start + i, cap - 1)
                    rows = pl.ds(half * 128 + i * ROWS, ROWS)
                    pa[rows, :] = panels[slot, :, 0:members]
                    pn[rows, :] = panels[slot, :, members : 2 * members]
                    pw[pl.ds(half * 8 + i, 1), :] = jnp.where(i < grains, weights[pl.ds(slot, 1), :], 0.0)
            wide = jnp.dot(expand, pw[...].astype(bf16), preferred_element_type=f32) * keep
            weight = lax.dot_general(pick, wide.astype(bf16), (((1,), (1,)), ((), ())), preferred_element_type=f32)
            turned = pa[...].astype(f32).T
            innovation = pn[...]
            for b in range(8):
                scaled = (turned * weight[b : b + 1, :]).astype(bf16)
                product = jnp.dot(scaled, innovation, preferred_element_type=f32)
                if mode == 0:
                    acc[yp, b] = product
                elif mode == 1:
                    acc[yp, b] += product
                elif b % 2 == 0:
                    p[0, yp, b // 2] = (acc[yp, b] + product).astype(bf16)
                else:
                    p[1, b // 2, yp] = (acc[yp, b] + product).astype(bf16)
            return carry

        lax.fori_loop(0, NY, one_region, 0)

    def ready(entry):
        for c in side[entry]:
            c.wait_recv()
        for at in (entry, LISTS + 1 + entry):
            if at > LISTS:
                to_scalar[at].start()
            to_scalar[at].wait()

    for hop in range(HOPS):
        for k in order[hop]:
            for way in range(2):
                entry = way * HOPS + hop
                z_copies[way][hop][k].wait_recv()
                if k in z_copies[way][min(hop + 1, HOPS - 1)] and hop + 1 < HOPS:
                    z_copies[way][hop + 1][k].start()
                if k == 5:
                    side[entry][0].start()
                    to_scalar[entry].start()
        for way in range(2):
            entry = way * HOPS + hop
            side[entry][1].start()
            side[entry][2].start()
        if hop == 0:
            ready(LISTS)
            accumulate(LISTS, 1, 0, STAY, 0)
        else:
            for way in range(2):
                ready(way * HOPS + hop - 1)
                accumulate(way * HOPS + hop - 1, 0, way * NR, CAPS[hop - 1], 1)
    for way in range(2):
        ready(way * HOPS + HOPS - 1)
        accumulate(way * HOPS + HOPS - 1, 0, way * NR, CAPS[HOPS - 1], 1 + way)

    def half_copy(src, dst, half, phase, k, axis, step):
        return copy(src, dst, sems.at[half, phase, k], recvs.at[half, phase, k], along(axis, step))

    first = []
    for half in range(2):
        me = y if half == 0 else x
        right, left, far = lax.rem(me + 1, 4), lax.rem(me + 3, 4), lax.rem(me + 2, 4)
        lo, hi = pl.ds(0, 2), pl.ds(2, 2)
        first.append([
            half_copy(p.at[half, far, lo], ro.at[half, 0], half, 0, 0, half, 1),
            half_copy(p.at[half, far, hi], ro.at[half, 1], half, 0, 1, half, 3),
            half_copy(p.at[half, right, hi], rd.at[half, 0, hi], half, 0, 2, half, 1),
            half_copy(p.at[half, left, lo], rd.at[half, 1, lo], half, 0, 3, half, 3),
            half_copy(sb.at[half, 0], rd.at[half, 0, lo], half, 0, 4, half, 1),
            half_copy(sb.at[half, 1], rd.at[half, 1, hi], half, 0, 5, half, 3),
        ])
    for k in range(4):
        for half in range(2):
            first[half][k].start()

    def flag_copy(src, dst, k, axis, step):
        return copy(ff.at[src], ff.at[dst], fsend.at[k], frecv.at[k], along(axis, step))

    flag = head[...] + hs[LISTS]
    for e in range(LISTS):
        flag = flag + hm[e] + hs[e]
    ff[0] = flag.astype(f32)
    flags = [flag_copy(0, 1, 0, 0, 1), flag_copy(0, 2, 1, 0, 3)]
    for c in flags:
        c.start()
    flags[0].wait_recv()
    ff[3] = ff[0] + ff[1]
    flags.append(flag_copy(3, 4, 2, 0, 1))
    flags[2].start()

    def wide_of(ref):
        return ref[...].astype(f32)

    for k in range(2):
        for half in range(2):
            me = y if half == 0 else x
            to = lax.rem(me + (1 if k == 0 else 3), 4)
            first[half][k].wait_recv()
            for i in range(2):
                sb[half, k, i] = (wide_of(p.at[half, to, 2 * k + i]) + wide_of(ro.at[half, k, i])).astype(bf16)
            first[half][4 + k].start()

    flags[1].wait_recv()
    flags[2].wait_recv()
    ff[5] = ff[0] + ff[2] + ff[4]
    flags += [flag_copy(5, 6, 3, 1, 1), flag_copy(5, 7, 4, 1, 3)]
    flags[3].start()
    flags[4].start()

    second = []
    for half in range(2):
        me, other = (y, x) if half == 0 else (x, y)
        for k in (2, 3, 4, 5):
            first[half][k].wait_recv()
        for i in range(4):
            u[half, i] = (wide_of(p.at[half, me, i]) + wide_of(rd.at[half, 0, i]) + wide_of(rd.at[half, 1, i])).astype(bf16)
        axis = 1 - half
        right, left, far = lax.rem(other + 1, 4), lax.rem(other + 3, 4), lax.rem(other + 2, 4)
        rows = u.shape[2] // 2
        lo, hi = pl.ds(0, rows), pl.ds(rows, rows)
        second.append([
            half_copy(u.at[half, far, lo], ro2.at[half, 0], half, 1, 0, axis, 1),
            half_copy(u.at[half, far, hi], ro2.at[half, 1], half, 1, 1, axis, 3),
            half_copy(u.at[half, right, hi], rd2.at[half, 0, hi], half, 1, 2, axis, 1),
            half_copy(u.at[half, left, lo], rd2.at[half, 1, lo], half, 1, 3, axis, 3),
            half_copy(sb2.at[half, 0], rd2.at[half, 0, lo], half, 1, 4, axis, 1),
            half_copy(sb2.at[half, 1], rd2.at[half, 1, hi], half, 1, 5, axis, 3),
        ])
        for k in range(4):
            second[half][k].start()

    flags[3].wait_recv()
    ff[8] = ff[5] + ff[6]
    flags.append(flag_copy(8, 9, 5, 1, 1))
    flags[5].start()

    for half in range(2):
        other = x if half == 0 else y
        rows = u.shape[2] // 2
        for k in range(2):
            to = lax.rem(other + (1 if k == 0 else 3), 4)
            second[half][k].wait_recv()
            sb2[half, k] = (wide_of(u.at[half, to, pl.ds(k * rows, rows)]) + wide_of(ro2.at[half, k])).astype(bf16)
            second[half][4 + k].start()

    flags[4].wait_recv()
    flags[5].wait_recv()
    flag_out[...] = ff[5] + ff[7] + ff[9]

    for half in range(2):
        other = x if half == 0 else y
        for k in (2, 3, 4, 5):
            second[half][k].wait_recv()
        total[half] = wide_of(u.at[half, other]) + wide_of(rd2.at[half, 0]) + wide_of(rd2.at[half, 1])

    for way in range(2):
        for hop in range(HOPS):
            for k in order[hop]:
                z_copies[way][hop][k].wait_send()
    for group in side:
        for c in group:
            c.wait_send()
    for c in (*first[0], *first[1], *second[0], *second[1], *flags):
        c.wait_send()


def exchange(send, send_w, head):
    vmem = pl.BlockSpec(memory_space=pltpu.VMEM)
    members = send.shape[2] // 2
    square = (members, members)
    dma = pltpu.SemaphoreType.DMA
    panels = [pltpu.VMEM((cap, ROWS, 2 * members), bf16) for cap in CAPS] * 2
    weights = [pltpu.VMEM((CAPS[0], 128), f32)] * LISTS
    return pl.pallas_call(
        exchange_kernel,
        out_shape=(jax.ShapeDtypeStruct((2, *square), f32), jax.ShapeDtypeStruct((8, 128), f32)),
        in_specs=[vmem] * 3,
        out_specs=(vmem, vmem),
        scratch_shapes=[
            *panels,
            *panels,
            pltpu.VMEM((STAY, ROWS, 2 * members), bf16),
            *weights,
            *weights,
            pltpu.VMEM((STAY, 128), f32),
            pltpu.VMEM((LISTS, 8, 128), i32),
            pltpu.VMEM((LISTS + 1, 8, 128), i32),
            pltpu.SMEM((2 * LISTS + 2, 8, 128), i32),
            pltpu.VMEM(square, bf16),
            pltpu.VMEM(square, bf16),
            pltpu.VMEM((16, 128), f32),
            pltpu.VMEM((4, 8, *square), f32),
            pltpu.VMEM((2, 4, 4, *square), bf16),
            pltpu.VMEM((2, 2, 2, *square), bf16),
            pltpu.VMEM((2, 2, 4, *square), bf16),
            pltpu.VMEM((2, 2, 2, *square), bf16),
            pltpu.VMEM((2, 4, *square), bf16),
            pltpu.VMEM((2, 2, members // 2, members), bf16),
            pltpu.VMEM((2, 2, *square), bf16),
            pltpu.VMEM((2, 2, members // 2, members), bf16),
            pltpu.VMEM((10, 8, 128), f32),
            dma((2, HOPS, 6)),
            dma((2, HOPS, 6)),
            dma((LISTS, 3)),
            dma((LISTS, 3)),
            dma((3,)),
            dma((3,)),
            dma((2 * LISTS + 2,)),
            dma((2, 2, 6)),
            dma((2, 2, 6)),
            dma((6,)),
            dma((6,)),
        ],
        compiler_params=pltpu.CompilerParams(collective_id=0, has_side_effects=True, vmem_limit_bytes=46 * MIB),
    )(send, send_w, head)


def update_kernel(state, coeff, total, updated, new_coeff, coef):
    @pl.when(pl.program_id(1) == 0)
    def _():
        base = (1.0 - relaxation) * coeff[...]
        gain = relaxation * total[...]
        new_coeff[...] = base + gain
        coef[0] = base.astype(bf16)
        coef[1] = gain.astype(bf16)

    s = state[...]
    moved = jnp.dot(s, coef[0], preferred_element_type=f32) + jnp.dot(s, coef[1], preferred_element_type=f32)
    updated[...] = (s.astype(f32) + moved).astype(bf16)


def update(state, coeff, total):
    _, blocks, width, members = state.shape
    step = 2048
    square = (members, members)
    rows = pl.BlockSpec((None, None, step, members), lambda j, i: (0, j, i, 0))
    one = pl.BlockSpec((None, None, *square), lambda j, i: (0, j, 0, 0))
    return pl.pallas_call(
        update_kernel,
        grid=(blocks, width // step),
        out_shape=(jax.ShapeDtypeStruct(state.shape, bf16), jax.ShapeDtypeStruct(coeff.shape, f32)),
        in_specs=[rows, one, pl.BlockSpec((None, *square), lambda j, i: (j, 0, 0))],
        out_specs=(rows, one),
        scratch_shapes=[pltpu.VMEM((2, *square), bf16)],
        compiler_params=pltpu.CompilerParams(vmem_limit_bytes=16 * MIB),
    )(state, coeff, total)


def padded_total(obs_anom, innov, obs_rinv, obs_pos, obs_count, obs_region, obs_partner, blocks, width):
    tile_count = lax.axis_size("tile")
    nblock, observation_count, ensemble_members = obs_anom.shape
    partition_count = obs_partner.shape[1]
    nlocal = lax.axis_size("grp") * blocks
    per_neighbour = max(2, (2 * nblock + tile_count - 1) // tile_count)
    slot_count = tile_count * per_neighbour
    slot_grouping = 8
    region = obs_region[:, 0]
    order = jnp.arange(nblock, dtype=jnp.int32)
    before = (region[None, :] == region[:, None]) & (order[None, :] < order[:, None])
    destination = region * per_neighbour + jnp.sum(before.astype(jnp.int32), axis=1)
    assignment_rule = destination[None, :] == jnp.arange(slot_count, dtype=jnp.int32)[:, None]
    place_half = assignment_rule.astype(jnp.bfloat16)
    place_int = assignment_rule.astype(jnp.int32)
    labels = jnp.concatenate([obs_count[:, None], obs_partner], axis=1)
    sent_labels = jnp.dot(place_int, labels).reshape(tile_count, per_neighbour, partition_count + 1)
    stacked = jnp.concatenate([obs_anom, innov], axis=2).reshape(nblock, -1)
    packed = jnp.dot(place_half, stacked, preferred_element_type=jnp.bfloat16)
    packed = packed.reshape(tile_count, per_neighbour, observation_count, 2 * ensemble_members)
    sent_pos = jnp.dot(place_int, obs_pos).reshape(tile_count, per_neighbour, observation_count)
    sent_var = jnp.dot(assignment_rule.astype(jnp.float32), obs_rinv, precision=lax.Precision.HIGHEST)
    sent_var = sent_var.reshape(tile_count, per_neighbour, observation_count)

    def exchange(array):
        return lax.all_to_all(array, "tile", split_axis=0, concat_axis=0, tiled=True)

    received_panels = exchange(packed).reshape(slot_count, observation_count, 2 * ensemble_members)
    flattened_labels = exchange(sent_labels).reshape(slot_count, partition_count + 1)
    recv_anom = received_panels[:, :, :ensemble_members]
    recv_innov = received_panels[:, :, ensemble_members:]
    flattened_positions = exchange(sent_pos).reshape(slot_count, observation_count)
    flattened_variances = exchange(sent_var).reshape(slot_count, observation_count)
    partners = flattened_labels[:, 1:]
    block_index = jnp.arange(nlocal, dtype=jnp.int32)

    def accumulate_group(step, total):
        start = step * slot_grouping

        def part(array):
            return lax.dynamic_slice_in_dim(array, start, slot_grouping, 0)

        weights = taper_weights(
            part(flattened_positions), part(partners), part(flattened_labels)[:, 0], part(flattened_variances), width,
            ensemble_members,
        )
        scaled_part = (weights[..., None] * part(recv_innov)[:, None].astype(jnp.float32)).astype(jnp.bfloat16)
        picked = (part(partners)[..., None] == block_index).astype(jnp.bfloat16)
        by_block = jnp.einsum("qkb,qkin->qbin", picked, scaled_part, preferred_element_type=jnp.float32).astype(jnp.bfloat16)
        return total + jnp.einsum("qim,qbin->bmn", part(recv_anom), by_block, preferred_element_type=jnp.float32)

    initial_total = jnp.zeros((nlocal, ensemble_members, ensemble_members), jnp.float32)
    running_totals = lax.fori_loop(0, slot_count // slot_grouping, accumulate_group, initial_total)
    return lax.psum_scatter(running_totals.astype(jnp.bfloat16), "grp", scatter_dimension=0, tiled=True).astype(jnp.float32)


def on_device(obs_anom, innov, obs_rinv, obs_pos, obs_count, obs_region, obs_partner, state_anom, coeff):
    send, send_w, head = pack(obs_region[:, 0], obs_count, obs_partner.T, obs_pos, obs_rinv, obs_anom, innov)
    fast, flags = exchange(send, send_w, head)
    blocks, width = state_anom.shape[1:3]
    total = lax.cond(
        flags[1, NR] > 0,
        lambda *obs: padded_total(*obs[:-1], blocks, width),
        lambda *obs: obs[-1],
        obs_anom, innov, obs_rinv, obs_pos, obs_count, obs_region, obs_partner, fast,
    )
    return update(state_anom, coeff, total)


def solution(mesh):
    return jax.shard_map(
        on_device,
        mesh=mesh,
        in_specs=(
            P(("grp", "tile"), None, None),
            P(("grp", "tile"), None, None),
            P(("grp", "tile"), None),
            P(("grp", "tile"), None),
            P(("grp", "tile")),
            P(("grp", "tile"), None),
            P(("grp", "tile"), None),
            P("grp", "tile", None, None),
            P("grp", "tile", None, None),
        ),
        out_specs=(P("grp", "tile", None, None), P("grp", "tile", None, None)),
        check_vma=False,
    )
```

```python
import jax
import jax.numpy as jnp
from jax import lax
from jax.experimental import pallas as pl
from jax.experimental.pallas import tpu as pltpu
from jax.sharding import PartitionSpec as P

relaxation = 0.5
bf16, f32, i32 = jnp.bfloat16, jnp.float32, jnp.int32
MESH = pl.DeviceIdType.MESH
MIB = 1024 * 1024

ROWS = 16
CAPS = (64, 50, 40, 28)
STAY = 40
SEND = 2 * CAPS[0] + STAY
HOPS = len(CAPS)
NZ, NY, NX, NR = 8, 4, 4, 64
LISTS = 2 * HOPS
HALF = 128
WCAPS = tuple((cap + 7) // 8 * 8 for cap in CAPS)
STAGES = 2 * HOPS


def taper_weights(positions, partners, counts, inverse_var, width, ensemble_members):
    center = (partners.astype(jnp.float32) + 0.5) * width
    offset = (positions.astype(jnp.float32)[..., None, :] - center[..., :, None]) / (2.0 * width)
    index = jnp.arange(positions.shape[-1], dtype=jnp.int32)
    live = index < counts[..., None]
    weight = jnp.exp(-offset * offset) * inverse_var[..., None, :] / (ensemble_members - 1.0)
    return jnp.where(live[..., None, :], weight, 0.0)


def pack_kernel(region, count, partner, pos, rinv, anom, innov, send, send_b, send_w, head, wall, held, size, fill, first, seat_a, seat_b, sem):
    nblock, members = anom.shape[0], anom.shape[2]
    width = 4096.0
    z = lax.axis_index("tile") // 8
    loads = [pltpu.make_async_copy(source, held.at[i], sem.at[i]) for i, source in enumerate((anom, innov))]
    for c in loads:
        c.start()

    lane = lax.broadcasted_iota(i32, (128, 128), 1)
    repeat = (lax.broadcasted_iota(i32, (128, nblock), 0) // 4 == lax.broadcasted_iota(i32, (128, nblock), 1)).astype(f32)
    column = lax.broadcasted_iota(i32, (128, 64), 1)
    quarter = (column // 16 == lax.broadcasted_iota(i32, (128, 64), 0) % 4).astype(f32)
    fold = (lax.broadcasted_iota(i32, (64, 128), 0) % 16 == lax.broadcasted_iota(i32, (64, 128), 1) % 16).astype(f32)

    def exact(a, b):
        return jnp.dot(a, b, precision=lax.Precision.HIGHEST, preferred_element_type=f32)

    def spread(values):
        return exact(exact(repeat, values) * quarter, fold)

    partners = lax.dot_general(
        repeat, partner[...].astype(f32), (((1,), (1,)), ((), ())), precision=lax.Precision.HIGHEST, preferred_element_type=f32
    )
    block_of_lane = (lane // 16).astype(f32)
    paired = jnp.zeros((128, 128), f32)
    for k in range(partner.shape[0]):
        paired = jnp.where(partners[:, k : k + 1] == block_of_lane, 1.0, paired)
    center = (block_of_lane + 0.5) * width
    offset = (spread(pos[...].astype(f32)) - center) / (2.0 * width)
    wall[...] = jnp.exp(-offset * offset) * spread(rinv[...]) / (members - 1.0) * paired

    def clear(i, c):
        size[i] = 0
        fill[i] = 0
        return c

    lax.fori_loop(0, NR, clear, 0)

    def blank(i, c):
        send[i] = jnp.zeros(send.shape[1:], bf16)
        send_b[i] = jnp.zeros(send_b.shape[1:], bf16)
        return c

    lax.fori_loop(0, SEND, blank, 0)
    send_w[...] = jnp.zeros_like(send_w)

    def measure(o, c):
        r = region[o]
        size[r] = size[r] + (count[o] + 15) // 16
        return c

    lax.fori_loop(0, nblock, measure, 0)

    def plane(distance):
        return lax.rem(z + distance, NZ) * 8

    def total(distance):
        base = plane(distance)
        return sum(size[base + i] for i in range(8))

    d = [total(distance) for distance in range(NZ)]
    right, left = d[1] + d[2] + d[3], d[5] + d[6] + d[7]
    far_right = jnp.clip((d[4] + left - right + 1) // 2, 0, d[4])
    far_left = d[4] - far_right
    counts = (
        (right + far_right, d[2] + d[3] + far_right, d[3] + far_right, far_right),
        (left + far_left, d[6] + d[5] + far_left, d[5] + far_left, far_left),
    )
    over = (d[0] > STAY).astype(i32)
    for way in range(2):
        for hop in range(HOPS):
            over = over | (counts[way][hop] > CAPS[hop]).astype(i32)

    head_row = lax.broadcasted_iota(i32, (8, 128), 0)
    head_lane = lax.broadcasted_iota(i32, (8, 128), 1)

    def noted(header, row, at, value):
        return jnp.where((head_row == row) & (head_lane == at), value, header)

    header = noted(jnp.zeros((8, 128), i32), 1, NR, over)

    def seat_far(i, carry):
        used_right, used_left, header = carry
        r = plane(4) + i
        n = size[r]
        a = jnp.minimum(n, far_right - used_right)
        b = n - a
        header = noted(noted(header, 0, r, used_right * 256 + a), 0, NR + r, used_left * 256 + b)
        first[r] = a
        seat_a[r] = used_right
        seat_b[r] = CAPS[0] + used_left
        return used_right + a, used_left + b, header

    used_right, used_left, header = lax.fori_loop(0, 8, seat_far, (jnp.int32(0), jnp.int32(0), header))

    def seat_near(distance, base, row, shift, carry):
        def seat(i, carry):
            used, header = carry
            r = plane(distance) + i
            n = size[r]
            first[r] = n
            seat_a[r] = base + used
            seat_b[r] = base + used
            return used + n, noted(header, row, shift + r, used * 256 + n)

        return lax.fori_loop(0, 8, seat, carry)

    for distance in (3, 2, 1):
        used_right, header = seat_near(distance, 0, 0, 0, (used_right, header))
    for distance in (5, 6, 7):
        used_left, header = seat_near(distance, CAPS[0], 0, NR, (used_left, header))
    _, header = seat_near(0, 2 * CAPS[0], 1, 0, (jnp.int32(0), header))
    head[...] = header
    for c in loads:
        c.wait()

    row_of_lane = lax.broadcasted_iota(i32, (1, 128), 1) % 16

    def place(o, c):
        r, live = region[o], count[o]
        grains = (live + 15) // 16
        start = fill[r]
        fill[r] = start + grains
        a, b, most = seat_a[r], seat_b[r], first[r]

        def one(q, c):
            f = start + q
            slot = jnp.minimum(jnp.where(f < most, a + f, b + f - most), SEND - 1)
            rows = pl.ds(pl.multiple_of(q * ROWS, ROWS), ROWS)
            send[slot, :, 0:members] = held[0, o, rows, :]
            send[slot, :, members : members + HALF] = held[1, o, rows, 0:HALF]
            send_b[slot] = held[1, o, rows, HALF:members]
            weight = wall[pl.ds(o * 4 + q, 1), :]
            send_w[pl.ds(slot, 1), :] = jnp.where(row_of_lane < live - q * ROWS, weight, 0.0)
            return c

        return lax.fori_loop(0, grains, one, c)

    lax.fori_loop(0, nblock, place, 0)


def pack(region, count, partner, pos, rinv, anom, innov):
    members = anom.shape[2]
    vmem, smem = pl.BlockSpec(memory_space=pltpu.VMEM), pl.BlockSpec(memory_space=pltpu.SMEM)
    hbm = pl.BlockSpec(memory_space=pl.ANY)
    return pl.pallas_call(
        pack_kernel,
        out_shape=(
            jax.ShapeDtypeStruct((SEND, ROWS, members + HALF), bf16),
            jax.ShapeDtypeStruct((SEND, ROWS, HALF), bf16),
            jax.ShapeDtypeStruct((SEND, 128), f32),
            jax.ShapeDtypeStruct((8, 128), i32),
        ),
        in_specs=[smem, smem, vmem, vmem, vmem, hbm, hbm],
        out_specs=(vmem, vmem, vmem, vmem),
        scratch_shapes=[
            pltpu.VMEM((128, 128), f32),
            pltpu.VMEM((2, *anom.shape), bf16),
            *[pltpu.SMEM((NR,), i32)] * 5,
            pltpu.SemaphoreType.DMA((2,)),
        ],
        compiler_params=pltpu.CompilerParams(vmem_limit_bytes=16 * MIB),
    )(region, count, partner, pos, rinv, anom, innov)


def exchange_kernel(send, send_b, send_w, head, total, flag_out, *scratch):
    scratch = list(scratch)

    def take(n):
        out = scratch[:n]
        del scratch[:n]
        return out

    zm, zs, bm, bs = take(LISTS), take(LISTS + 1), take(LISTS), take(LISTS + 1)
    wm, ws = take(LISTS), take(LISTS + 1)
    hm, hs, hsm, pn, pw, kept_a, kept_w, acc, ff = take(9)
    p, ro, rd, sb, u, ro2, rd2, sb2 = (take(2) for _ in range(8))
    zsend, zrecv, ssend, srecv, hsem, sems, recvs, fsend, frecv = take(9)

    members = acc.shape[3]
    x, tile = lax.axis_index("grp"), lax.axis_index("tile")
    z, inner = tile // 8, tile % 8
    y, core = inner // 2, inner % 2
    sibling = tile + 1 - 2 * core

    def around(step):
        return x, lax.rem(z + step, NZ) * 8 + inner

    def along(axis, step):
        if axis == 0:
            return x, z * 8 + lax.rem(y + step, NY) * 2 + core
        return lax.rem(x + step, NX), tile

    ways = (around(1), around(NZ - 1))
    barrier = pltpu.get_barrier_semaphore()
    for other in (*ways, (x, sibling), along(0, 1), along(0, 3), along(1, 1), along(1, 3)):
        pl.semaphore_signal(barrier, inc=1, device_id=other, device_id_type=MESH)
    pl.semaphore_wait(barrier, 7)

    def copy(src, dst, send_sem, recv_sem, other):
        return pltpu.make_async_remote_copy(
            src_ref=src, dst_ref=dst, send_sem=send_sem, recv_sem=recv_sem, device_id=other, device_id_type=MESH
        )

    edges = (0, *CAPS[::-1])

    def hop_copies(way, hop):
        entry = way * HOPS + hop
        base = way * CAPS[0]
        out = []
        for k in range(HOPS - hop):
            lo, n = edges[k], edges[k + 1] - edges[k]
            src = send.at[pl.ds(base + lo, n)] if hop == 0 else zm[entry - 1].at[pl.ds(lo, n)]
            out.append((k, src, zm[entry].at[pl.ds(lo, n)]))
        rows = WCAPS[hop]
        out.append((4, send_w.at[pl.ds(base, rows)] if hop == 0 else wm[entry - 1].at[pl.ds(0, rows)], wm[entry]))
        out.append((5, head if hop == 0 else hm.at[entry - 1], hm.at[entry]))
        for k in range(HOPS - hop):
            lo, n = edges[k], edges[k + 1] - edges[k]
            src = send_b.at[pl.ds(base + lo, n)] if hop == 0 else bm[entry - 1].at[pl.ds(lo, n)]
            out.append((6 + k, src, bm[entry].at[pl.ds(lo, n)]))
        return {k: copy(src, dst, zsend.at[way, hop, k], zrecv.at[way, hop, k], ways[way]) for k, src, dst in out}

    z_copies = [[hop_copies(way, hop) for hop in range(HOPS)] for way in range(2)]
    order = [[5, 4, *range(HOPS - hop)] for hop in range(HOPS)]
    stay = pl.ds(2 * CAPS[0], STAY)
    pairs = [((hm.at[e], hs.at[e]), (zm[e], zs[e]), (wm[e], ws[e]), (bm[e], bs[e])) for e in range(LISTS)]
    pairs.append((
        (head, hs.at[LISTS]), (send.at[stay], zs[LISTS]), (send_w.at[stay], ws[LISTS]), (send_b.at[stay], bs[LISTS])
    ))
    side = [
        [copy(s, t, ssend.at[e, i], srecv.at[e, i], (x, sibling)) for i, (s, t) in enumerate(pairs[e])] for e in range(LISTS + 1)
    ]
    to_scalar = [pltpu.make_async_copy(hm.at[e], hsm.at[e], hsem.at[e]) for e in range(LISTS)]
    to_scalar.append(pltpu.make_async_copy(head, hsm.at[LISTS], hsem.at[LISTS]))
    to_scalar += [pltpu.make_async_copy(hs.at[e], hsm.at[LISTS + 1 + e], hsem.at[LISTS + 1 + e]) for e in range(LISTS + 1)]

    for k in order[0]:
        for way in range(2):
            z_copies[way][0][k].start()
    for c in side[LISTS]:
        c.start()
    to_scalar[LISTS].start()

    expand = (lax.broadcasted_iota(i32, (1024, 64), 0) // 16 == lax.broadcasted_iota(i32, (1024, 64), 1)).astype(bf16)
    keep = (lax.broadcasted_iota(i32, (1024, 128), 0) % 16 == lax.broadcasted_iota(i32, (1024, 128), 1) % 16).astype(f32)
    pick = (lax.broadcasted_iota(i32, (8, 128), 1) // 16 == lax.broadcasted_iota(i32, (8, 128), 0)).astype(bf16)

    own_stage, far_stage = (LISTS,), (HOPS - 1, LISTS - 1)
    stages = [own_stage, *((way * HOPS + hop,) for hop in range(HOPS - 1) for way in range(2)), far_stage]

    def place_of(at, entry, r):
        row, shift = (1, 0) if entry == LISTS else (0, entry // HOPS * NR)
        value = hsm[at, row, shift + r]
        return value // 256, value % 256

    def slots(entries, who, r):
        found = []
        for entry in entries:
            start, grains = place_of(entry + who * (LISTS + 1), entry, r)
            own = entry == LISTS
            base = 2 * CAPS[0] if own and not who else 0
            cap = STAY if own else CAPS[entry % HOPS]
            found.append((start, grains, base, cap))
        out = []
        for i in range(8):
            start, grains, base, cap = found[0]
            slot = base + jnp.minimum(start + i, cap - 1)
            if len(found) == 1:
                out.append((None, slot, None, i < grains))
            else:
                start_2, grains_2, _, cap_2 = found[1]
                slot_2 = jnp.clip(start_2 + i - grains, 0, cap_2 - 1)
                out.append((i < grains, slot, slot_2, i < grains + grains_2))
        return out

    def sources(entries, who, mine, theirs, own):
        return [theirs[e] if who else (own if e == LISTS else mine[e]) for e in entries]

    def multiply(stage, target):
        for yp in range(NY):
            turned = pn[yp].astype(f32).T
            anomalies = kept_a[stage, yp]
            for b in range(8):
                weight = kept_w[stage, b : b + 1, yp * 256 : (yp + 1) * 256]
                product = jnp.dot((turned * weight).astype(bf16), anomalies, preferred_element_type=f32)
                if stage == 0:
                    acc[yp, b] = product
                elif stage < STAGES - 1:
                    acc[yp, b] += product
                elif b % 2 == 0:
                    target[0, yp, b // 2] = (acc[yp, b] + product).astype(bf16)
                else:
                    target[1, b // 2, yp] = (acc[yp, b] + product).astype(bf16)

    def first_columns(stage):
        entries = stages[stage]

        def gather(yp, carry):
            r = z * 8 + yp * 2 + core
            for who in range(2):
                panels = sources(entries, who, zm, zs, send)
                weights = sources(entries, who, wm, ws, send_w)
                for i, (first_list, slot, slot_2, live) in enumerate(slots(entries, who, r)):
                    panel, weight = panels[0][slot], weights[0][pl.ds(slot, 1), :]
                    if first_list is not None:
                        panel = jnp.where(first_list, panel, panels[1][slot_2])
                        weight = jnp.where(first_list, weight, weights[1][pl.ds(slot_2, 1), :])
                    rows = pl.ds(who * 128 + i * ROWS, ROWS)
                    kept_a[stage, yp, rows, :] = panel[:, 0:members]
                    pn[yp, rows, :] = panel[:, members : members + HALF]
                    pw[pl.ds(yp * 16 + who * 8 + i, 1), :] = jnp.where(live, weight, 0.0)
            return carry

        lax.fori_loop(0, NY, gather, 0)
        wide = jnp.dot(expand, pw[...].astype(bf16), preferred_element_type=f32) * keep
        kept_w[stage] = lax.dot_general(pick, wide.astype(bf16), (((1,), (1,)), ((), ())), preferred_element_type=f32)
        multiply(stage, p[0])

    def other_columns(stage):
        entries = stages[stage]

        def gather(yp, carry):
            r = z * 8 + yp * 2 + core
            for who in range(2):
                panels = sources(entries, who, bm, bs, send_b)
                for i, (first_list, slot, slot_2, live) in enumerate(slots(entries, who, r)):
                    panel = panels[0][slot]
                    if first_list is not None:
                        panel = jnp.where(first_list, panel, panels[1][slot_2])
                    pn[yp, pl.ds(who * 128 + i * ROWS, ROWS), :] = panel
            return carry

        lax.fori_loop(0, NY, gather, 0)
        multiply(stage, p[1])

    def ready(entry):
        for c in side[entry][0:3]:
            c.wait_recv()
        for at in (entry, LISTS + 1 + entry):
            if at > LISTS:
                to_scalar[at].start()
            to_scalar[at].wait()

    def wide_of(ref):
        return ref[...].astype(f32)

    def flag_copy(src, dst, k, axis, step):
        return copy(ff.at[src], ff.at[dst], fsend.at[k], frecv.at[k], along(axis, step))

    flags = [
        flag_copy(0, 1, 0, 0, 1), flag_copy(0, 2, 1, 0, 3), flag_copy(3, 4, 2, 0, 1),
        flag_copy(5, 6, 3, 1, 1), flag_copy(5, 7, 4, 1, 3), flag_copy(8, 9, 5, 1, 1),
    ]

    def reducer(part):
        p_, ro_, rd_, sb_, u_, ro2_, rd2_, sb2_ = (buffers[part] for buffers in (p, ro, rd, sb, u, ro2, rd2, sb2))
        rows = HALF // 2

        def half_copy(src, dst, half, phase, k, axis, step):
            return copy(src, dst, sems.at[part, half, phase, k], recvs.at[part, half, phase, k], along(axis, step))

        def triple(me):
            return lax.rem(me + 1, 4), lax.rem(me + 3, 4), lax.rem(me + 2, 4)

        first, second = [], []
        for half in range(2):
            me, other = (y, x) if half == 0 else (x, y)
            right, left, far = triple(me)
            lo, hi = pl.ds(0, 2), pl.ds(2, 2)
            first.append([
                half_copy(p_.at[half, far, lo], ro_.at[half, 0], half, 0, 0, half, 1),
                half_copy(p_.at[half, far, hi], ro_.at[half, 1], half, 0, 1, half, 3),
                half_copy(p_.at[half, right, hi], rd_.at[half, 0, hi], half, 0, 2, half, 1),
                half_copy(p_.at[half, left, lo], rd_.at[half, 1, lo], half, 0, 3, half, 3),
                half_copy(sb_.at[half, 0], rd_.at[half, 0, lo], half, 0, 4, half, 1),
                half_copy(sb_.at[half, 1], rd_.at[half, 1, hi], half, 0, 5, half, 3),
            ])
            axis = 1 - half
            right, left, far = triple(other)
            lo, hi = pl.ds(0, rows), pl.ds(rows, rows)
            second.append([
                half_copy(u_.at[half, far, lo], ro2_.at[half, 0], half, 1, 0, axis, 1),
                half_copy(u_.at[half, far, hi], ro2_.at[half, 1], half, 1, 1, axis, 3),
                half_copy(u_.at[half, right, hi], rd2_.at[half, 0, hi], half, 1, 2, axis, 1),
                half_copy(u_.at[half, left, lo], rd2_.at[half, 1, lo], half, 1, 3, axis, 3),
                half_copy(sb2_.at[half, 0], rd2_.at[half, 0, lo], half, 1, 4, axis, 1),
                half_copy(sb2_.at[half, 1], rd2_.at[half, 1, hi], half, 1, 5, axis, 3),
            ])

        def begin():
            for k in range(4):
                for half in range(2):
                    first[half][k].start()
            if part == 0:
                flag = head[...] + hs[LISTS]
                for e in range(LISTS):
                    flag = flag + hm[e] + hs[e]
                ff[0] = flag.astype(f32)
                flags[0].start()
                flags[1].start()

        def pass_on():
            for k in range(2):
                for half in range(2):
                    me = y if half == 0 else x
                    to = lax.rem(me + (1 if k == 0 else 3), 4)
                    first[half][k].wait_recv()
                    for i in range(2):
                        sb_[half, k, i] = (wide_of(p_.at[half, to, 2 * k + i]) + wide_of(ro_.at[half, k, i])).astype(bf16)
                    first[half][4 + k].start()
            if part == 0:
                flags[0].wait_recv()
                ff[3] = ff[0] + ff[1]
                flags[2].start()

        def turn():
            for half in range(2):
                me = y if half == 0 else x
                for k in (2, 3, 4, 5):
                    first[half][k].wait_recv()
                for i in range(4):
                    u_[half, i] = (
                        wide_of(p_.at[half, me, i]) + wide_of(rd_.at[half, 0, i]) + wide_of(rd_.at[half, 1, i])
                    ).astype(bf16)
                for k in range(4):
                    second[half][k].start()
            if part == 0:
                flags[1].wait_recv()
                flags[2].wait_recv()
                ff[5] = ff[0] + ff[2] + ff[4]
                flags[3].start()
                flags[4].start()

        def pass_on_again():
            for half in range(2):
                other = x if half == 0 else y
                for k in range(2):
                    to = lax.rem(other + (1 if k == 0 else 3), 4)
                    second[half][k].wait_recv()
                    sb2_[half, k] = (wide_of(u_.at[half, to, pl.ds(k * rows, rows)]) + wide_of(ro2_.at[half, k])).astype(bf16)
                    second[half][4 + k].start()
            if part == 0:
                flags[3].wait_recv()
                ff[8] = ff[5] + ff[6]
                flags[5].start()

        def finish():
            for half in range(2):
                other = x if half == 0 else y
                for k in (2, 3, 4, 5):
                    second[half][k].wait_recv()
                turned = wide_of(u_.at[half, other]) + wide_of(rd2_.at[half, 0]) + wide_of(rd2_.at[half, 1])
                total[half, :, part * HALF : (part + 1) * HALF] = turned.T
            if part == 0:
                flags[4].wait_recv()
                flags[5].wait_recv()
                flag_out[...] = ff[5] + ff[7] + ff[9]

        def drain():
            for c in (*first[0], *first[1], *second[0], *second[1]):
                c.wait_send()

        return begin, (pass_on, turn, pass_on_again, finish), drain

    begin_a, steps_a, drain_a = reducer(0)
    begin_b, steps_b, drain_b = reducer(1)

    for hop in range(HOPS):
        for k in order[hop]:
            for way in range(2):
                entry = way * HOPS + hop
                z_copies[way][hop][k].wait_recv()
                if hop + 1 < HOPS and k in z_copies[way][hop + 1]:
                    z_copies[way][hop + 1][k].start()
                if k == 5:
                    side[entry][0].start()
                    to_scalar[entry].start()
        for way in range(2):
            entry = way * HOPS + hop
            side[entry][1].start()
            side[entry][2].start()
        if hop == HOPS - 2:
            for k in range(HOPS):
                for way in range(2):
                    z_copies[way][0][6 + k].start()
        if hop == 0:
            ready(LISTS)
            first_columns(0)
        else:
            for way in range(2):
                ready(way * HOPS + hop - 1)
                first_columns(1 + 2 * (hop - 1) + way)
    for entry in far_stage:
        ready(entry)
    first_columns(STAGES - 1)
    begin_a()

    for hop in range(HOPS):
        for k in range(HOPS - hop):
            for way in range(2):
                z_copies[way][hop][6 + k].wait_recv()
                if hop + 1 < HOPS and 6 + k in z_copies[way][hop + 1]:
                    z_copies[way][hop + 1][6 + k].start()
        for way in range(2):
            side[way * HOPS + hop][3].start()
        if hop == 0:
            side[LISTS][3].wait_recv()
            other_columns(0)
            steps_a[0]()
        else:
            for way in range(2):
                side[way * HOPS + hop - 1][3].wait_recv()
                other_columns(1 + 2 * (hop - 1) + way)
                if way == 0:
                    steps_a[hop]()
    for entry in far_stage:
        side[entry][3].wait_recv()
    other_columns(STAGES - 1)
    begin_b()
    for step in steps_b:
        step()

    drain_a()
    drain_b()
    for way in range(2):
        for hop in range(HOPS):
            for k in z_copies[way][hop]:
                z_copies[way][hop][k].wait_send()
    for group in side:
        for c in group:
            c.wait_send()
    for c in flags:
        c.wait_send()


def exchange(send, send_b, send_w, head):
    vmem = pl.BlockSpec(memory_space=pltpu.VMEM)
    members = send.shape[2] - HALF
    square, slab, thin = (members, members), (HALF, members), (HALF // 2, members)
    dma = pltpu.SemaphoreType.DMA
    panels = [pltpu.VMEM((cap, ROWS, members + HALF), bf16) for cap in CAPS] * 2
    others = [pltpu.VMEM((cap, ROWS, HALF), bf16) for cap in CAPS] * 2
    weights = [pltpu.VMEM((cap, 128), f32) for cap in WCAPS] * 2
    return pl.pallas_call(
        exchange_kernel,
        out_shape=(
            jax.ShapeDtypeStruct((2, *square), f32),
            jax.ShapeDtypeStruct((8, 128), f32),
        ),
        in_specs=[vmem] * 4,
        out_specs=(vmem, vmem),
        scratch_shapes=[
            *panels,
            *panels,
            pltpu.VMEM((STAY, ROWS, members + HALF), bf16),
            *others,
            *others,
            pltpu.VMEM((STAY, ROWS, HALF), bf16),
            *weights,
            *weights,
            pltpu.VMEM((STAY, 128), f32),
            pltpu.VMEM((LISTS, 8, 128), i32),
            pltpu.VMEM((LISTS + 1, 8, 128), i32),
            pltpu.SMEM((2 * LISTS + 2, 8, 128), i32),
            pltpu.VMEM((NY, 256, HALF), bf16),
            pltpu.VMEM((NY * 16, 128), f32),
            pltpu.VMEM((STAGES, NY, 256, members), bf16),
            pltpu.VMEM((STAGES, 8, NY * 256), f32),
            pltpu.VMEM((NY, 8, *slab), f32),
            pltpu.VMEM((10, 8, 128), f32),
            *[pltpu.VMEM((2, 4, 4, *slab), bf16)] * 2,
            *[pltpu.VMEM((2, 2, 2, *slab), bf16)] * 2,
            *[pltpu.VMEM((2, 2, 4, *slab), bf16)] * 2,
            *[pltpu.VMEM((2, 2, 2, *slab), bf16)] * 2,
            *[pltpu.VMEM((2, 4, *slab), bf16)] * 2,
            *[pltpu.VMEM((2, 2, *thin), bf16)] * 2,
            *[pltpu.VMEM((2, 2, *slab), bf16)] * 2,
            *[pltpu.VMEM((2, 2, *thin), bf16)] * 2,
            dma((2, HOPS, 6 + HOPS)),
            dma((2, HOPS, 6 + HOPS)),
            dma((LISTS + 1, 4)),
            dma((LISTS + 1, 4)),
            dma((2 * LISTS + 2,)),
            dma((2, 2, 2, 6)),
            dma((2, 2, 2, 6)),
            dma((6,)),
            dma((6,)),
        ],
        compiler_params=pltpu.CompilerParams(collective_id=0, has_side_effects=True, vmem_limit_bytes=46 * MIB),
    )(send, send_b, send_w, head)


def update_kernel(state, coeff, total, updated, new_coeff, coef):
    @pl.when(pl.program_id(1) == 0)
    def _():
        new = (1.0 - relaxation) * coeff[...] + relaxation * total[...]
        new_coeff[...] = new
        coef[...] = new.astype(bf16)

    s = state[...]
    updated[...] = (s.astype(f32) + jnp.dot(s, coef[...], preferred_element_type=f32)).astype(bf16)


def update(state, coeff, total):
    _, blocks, width, members = state.shape
    step = 2048
    square = (members, members)
    rows = pl.BlockSpec((None, None, step, members), lambda j, i: (0, j, i, 0))
    one = pl.BlockSpec((None, None, *square), lambda j, i: (0, j, 0, 0))
    return pl.pallas_call(
        update_kernel,
        grid=(blocks, width // step),
        out_shape=(jax.ShapeDtypeStruct(state.shape, bf16), jax.ShapeDtypeStruct(coeff.shape, f32)),
        in_specs=[rows, one, pl.BlockSpec((None, *square), lambda j, i: (j, 0, 0))],
        out_specs=(rows, one),
        scratch_shapes=[pltpu.VMEM(square, bf16)],
        compiler_params=pltpu.CompilerParams(vmem_limit_bytes=16 * MIB),
    )(state, coeff, total)


def padded_total(obs_anom, innov, obs_rinv, obs_pos, obs_count, obs_region, obs_partner, blocks, width):
    tile_count = lax.axis_size("tile")
    nblock, observation_count, ensemble_members = obs_anom.shape
    partition_count = obs_partner.shape[1]
    nlocal = lax.axis_size("grp") * blocks
    per_neighbour = max(2, (2 * nblock + tile_count - 1) // tile_count)
    slot_count = tile_count * per_neighbour
    slot_grouping = 8
    region = obs_region[:, 0]
    order = jnp.arange(nblock, dtype=jnp.int32)
    before = (region[None, :] == region[:, None]) & (order[None, :] < order[:, None])
    destination = region * per_neighbour + jnp.sum(before.astype(jnp.int32), axis=1)
    assignment_rule = destination[None, :] == jnp.arange(slot_count, dtype=jnp.int32)[:, None]
    place_half = assignment_rule.astype(jnp.bfloat16)
    place_int = assignment_rule.astype(jnp.int32)
    labels = jnp.concatenate([obs_count[:, None], obs_partner], axis=1)
    sent_labels = jnp.dot(place_int, labels).reshape(tile_count, per_neighbour, partition_count + 1)
    stacked = jnp.concatenate([obs_anom, innov], axis=2).reshape(nblock, -1)
    packed = jnp.dot(place_half, stacked, preferred_element_type=jnp.bfloat16)
    packed = packed.reshape(tile_count, per_neighbour, observation_count, 2 * ensemble_members)
    sent_pos = jnp.dot(place_int, obs_pos).reshape(tile_count, per_neighbour, observation_count)
    sent_var = jnp.dot(assignment_rule.astype(jnp.float32), obs_rinv, precision=lax.Precision.HIGHEST)
    sent_var = sent_var.reshape(tile_count, per_neighbour, observation_count)

    def exchange(array):
        return lax.all_to_all(array, "tile", split_axis=0, concat_axis=0, tiled=True)

    received_panels = exchange(packed).reshape(slot_count, observation_count, 2 * ensemble_members)
    flattened_labels = exchange(sent_labels).reshape(slot_count, partition_count + 1)
    recv_anom = received_panels[:, :, :ensemble_members]
    recv_innov = received_panels[:, :, ensemble_members:]
    flattened_positions = exchange(sent_pos).reshape(slot_count, observation_count)
    flattened_variances = exchange(sent_var).reshape(slot_count, observation_count)
    partners = flattened_labels[:, 1:]
    block_index = jnp.arange(nlocal, dtype=jnp.int32)

    def accumulate_group(step, total):
        start = step * slot_grouping

        def part(array):
            return lax.dynamic_slice_in_dim(array, start, slot_grouping, 0)

        weights = taper_weights(
            part(flattened_positions), part(partners), part(flattened_labels)[:, 0], part(flattened_variances), width,
            ensemble_members,
        )
        scaled_part = (weights[..., None] * part(recv_innov)[:, None].astype(jnp.float32)).astype(jnp.bfloat16)
        picked = (part(partners)[..., None] == block_index).astype(jnp.bfloat16)
        by_block = jnp.einsum("qkb,qkin->qbin", picked, scaled_part, preferred_element_type=jnp.float32).astype(jnp.bfloat16)
        return total + jnp.einsum("qim,qbin->bmn", part(recv_anom), by_block, preferred_element_type=jnp.float32)

    initial_total = jnp.zeros((nlocal, ensemble_members, ensemble_members), jnp.float32)
    running_totals = lax.fori_loop(0, slot_count // slot_grouping, accumulate_group, initial_total)
    return lax.psum_scatter(running_totals.astype(jnp.bfloat16), "grp", scatter_dimension=0, tiled=True).astype(jnp.float32)


def on_device(obs_anom, innov, obs_rinv, obs_pos, obs_count, obs_region, obs_partner, state_anom, coeff):
    send, send_b, send_w, head = pack(obs_region[:, 0], obs_count, obs_partner.T, obs_pos, obs_rinv, obs_anom, innov)
    fast, flags = exchange(send, send_b, send_w, head)
    blocks, width = state_anom.shape[1:3]
    total = lax.cond(
        flags[1, NR] > 0,
        lambda *obs: padded_total(*obs[:-1], blocks, width),
        lambda *obs: obs[-1],
        obs_anom, innov, obs_rinv, obs_pos, obs_count, obs_region, obs_partner, fast,
    )
    return update(state_anom, coeff, total)


def solution(mesh):
    return jax.shard_map(
        on_device,
        mesh=mesh,
        in_specs=(
            P(("grp", "tile"), None, None),
            P(("grp", "tile"), None, None),
            P(("grp", "tile"), None),
            P(("grp", "tile"), None),
            P(("grp", "tile")),
            P(("grp", "tile"), None),
            P(("grp", "tile"), None),
            P("grp", "tile", None, None),
            P("grp", "tile", None, None),
        ),
        out_specs=(P("grp", "tile", None, None), P("grp", "tile", None, None)),
        check_vma=False,
    )
```

```python
import jax
import jax.numpy as jnp
from jax import lax
from jax.experimental import pallas as pl
from jax.experimental.pallas import tpu as pltpu
from jax.sharding import PartitionSpec as P

relaxation = 0.5
bf16, f32, i32 = jnp.bfloat16, jnp.float32, jnp.int32
MESH = pl.DeviceIdType.MESH
MIB = 1024 * 1024

ROWS = 16
CAPS = (56, 46, 34, 24)
STAY = 32
SEND = 2 * CAPS[0] + STAY
SPARE = 8
HOPS = len(CAPS)
NZ, NY, NX, NR = 8, 4, 4, 64
LISTS = 2 * HOPS
HALF = 128
WCAPS = tuple((cap + 7) // 8 * 8 for cap in CAPS)
STAGES = 2 * HOPS


def taper_weights(positions, partners, counts, inverse_var, width, ensemble_members):
    center = (partners.astype(jnp.float32) + 0.5) * width
    offset = (positions.astype(jnp.float32)[..., None, :] - center[..., :, None]) / (2.0 * width)
    index = jnp.arange(positions.shape[-1], dtype=jnp.int32)
    live = index < counts[..., None]
    weight = jnp.exp(-offset * offset) * inverse_var[..., None, :] / (ensemble_members - 1.0)
    return jnp.where(live[..., None, :], weight, 0.0)


def pack_kernel(
    region, count, partner, pos, rinv, anom, innov, send, send_b, send_w, head, wall, held, size, fill, seats, place_at, sem
):
    nblock, members = anom.shape[0], anom.shape[2]
    width = 4096.0
    z = lax.axis_index("tile") // 8
    loads = [pltpu.make_async_copy(source, held.at[i], sem.at[i]) for i, source in enumerate((anom, innov))]
    for c in loads:
        c.start()

    deep = 8 * nblock
    lane = lax.broadcasted_iota(i32, (deep, 128), 1)
    repeat = (lax.broadcasted_iota(i32, (deep, nblock), 0) // 8 == lax.broadcasted_iota(i32, (deep, nblock), 1)).astype(f32)
    column = lax.broadcasted_iota(i32, (deep, 64), 1)
    quarter = (column // 16 == lax.broadcasted_iota(i32, (deep, 64), 0) % 8).astype(f32)
    fold = (lax.broadcasted_iota(i32, (64, 128), 0) % 16 == lax.broadcasted_iota(i32, (64, 128), 1) % 16).astype(f32)

    def exact(a, b):
        return jnp.dot(a, b, precision=lax.Precision.HIGHEST, preferred_element_type=f32)

    def spread(values):
        return exact(exact(repeat, values) * quarter, fold)

    partners = lax.dot_general(
        repeat, partner[...].astype(f32), (((1,), (1,)), ((), ())), precision=lax.Precision.HIGHEST, preferred_element_type=f32
    )
    block_of_lane = (lane // 16).astype(f32)
    paired = jnp.zeros((deep, 128), f32)
    for k in range(partner.shape[0]):
        paired = jnp.where(partners[:, k : k + 1] == block_of_lane, 1.0, paired)
    center = (block_of_lane + 0.5) * width
    offset = (spread(pos[...].astype(f32)) - center) / (2.0 * width)
    wall[...] = jnp.exp(-offset * offset) * spread(rinv[...]) / (members - 1.0) * paired

    def clear(i, c):
        size[i] = 0
        fill[i] = 0
        return c

    lax.fori_loop(0, NR, clear, 0, unroll=16)

    def blank(i, c):
        send[i] = jnp.zeros(send.shape[1:], bf16)
        send_b[i] = jnp.zeros(send_b.shape[1:], bf16)
        return c

    lax.fori_loop(0, SEND + SPARE, blank, 0, unroll=8)
    send_w[...] = jnp.zeros_like(send_w)

    def measure(o, c):
        r = region[o]
        size[r] = size[r] + count[o]
        return c

    lax.fori_loop(0, nblock, measure, 0, unroll=8)

    def plane(distance):
        return lax.rem(z + distance, NZ) * 8

    def total(distance):
        base = plane(distance)
        return sum(size[base + i] for i in range(8))

    head_row = lax.broadcasted_iota(i32, (8, 128), 0)
    head_lane = lax.broadcasted_iota(i32, (8, 128), 1)

    def noted(header, row, at, value):
        return jnp.where((head_row == row) & (head_lane == at), value, header)

    def begin(used, n):
        return jnp.where(used % ROWS + n > 8 * ROWS, (used + ROWS - 1) // ROWS * ROWS, used)

    def seat_far(i, carry):
        used_right, used_left, load_right, load_left, header = carry
        r = plane(4) + i
        n = size[r]
        to_right = load_right <= load_left
        right, left = begin(used_right, n), begin(used_left, n)
        header = noted(header, 0, r, jnp.where(to_right, right * 256 + n, 0))
        header = noted(header, 0, NR + r, jnp.where(to_right, 0, left * 256 + n))
        seats[r] = jnp.where(to_right, right, CAPS[0] * ROWS + left)
        used_right, used_left = jnp.where(to_right, right + n, used_right), jnp.where(to_right, used_left, left + n)
        load_right, load_left = jnp.where(to_right, load_right + n, load_right), jnp.where(to_right, load_left, load_left + n)
        return used_right, used_left, load_right, load_left, header

    loads_of = (total(1) + total(2) + total(3), total(5) + total(6) + total(7))
    none = jnp.zeros((), i32)
    used_right, used_left, _, _, header = lax.fori_loop(0, 8, seat_far, (none, none, *loads_of, jnp.zeros((8, 128), i32)), unroll=8)

    def seat_near(distance, base, row, shift, carry):
        def seat(i, carry):
            used, header = carry
            r = plane(distance) + i
            n = size[r]
            first = begin(used, n)
            seats[r] = base * ROWS + first
            return first + n, noted(header, row, shift + r, first * 256 + n)

        return lax.fori_loop(0, 8, seat, carry, unroll=8)

    over = (used_right > CAPS[3] * ROWS) | (used_left > CAPS[3] * ROWS)
    for hop, distance in ((2, 3), (1, 2), (0, 1)):
        used_right, header = seat_near(distance, 0, 0, 0, (used_right, header))
        used_left, header = seat_near(NZ - distance, CAPS[0], 0, NR, (used_left, header))
        over = over | (used_right > CAPS[hop] * ROWS) | (used_left > CAPS[hop] * ROWS)
    used_stay, header = seat_near(0, 2 * CAPS[0], 1, 0, (none, header))
    over = over | (used_stay > STAY * ROWS)
    head[...] = noted(header, 1, NR, over.astype(i32))

    def find(o, c):
        r = region[o]
        place_at[o] = seats[r] + fill[r]
        fill[r] = fill[r] + count[o]
        return c

    lax.fori_loop(0, nblock, find, 0, unroll=8)
    for c in loads:
        c.wait()

    deep_window = 5 * ROWS
    to_row = lax.broadcasted_iota(i32, (deep_window, 64), 0)
    from_row = lax.broadcasted_iota(i32, (deep_window, 64), 1)

    sub = lax.broadcasted_iota(i32, (8, 128), 0)
    row_of_lane = lax.broadcasted_iota(i32, (8, 128), 1) % ROWS

    def place(o, c):
        live, at = count[o], place_at[o]
        shift = at % ROWS
        grain = jnp.minimum(at // ROWS, SEND + SPARE - 8)
        weight = jnp.where(sub * ROWS + row_of_lane < live, wall[pl.ds(pl.multiple_of(o * 8, 8), 8), :], 0.0)
        same = pltpu.roll(weight, shift, 1)
        next_one = pltpu.roll(pltpu.roll(weight, 1, 0), shift + 128 - ROWS, 1)
        send_w[pl.ds(grain, 8), :] += jnp.where(row_of_lane >= shift, same, next_one)

        move = ((to_row - shift == from_row) & (from_row < live)).astype(bf16)
        anomalies = jnp.dot(move, held[0, o], preferred_element_type=f32).astype(bf16)
        innovations = jnp.dot(move, held[1, o], preferred_element_type=f32).astype(bf16)
        for q in range(5):
            rows = slice(q * ROWS, (q + 1) * ROWS)
            send[grain + q, :, 0:members] += anomalies[rows]
            send[grain + q, :, members : members + HALF] += innovations[rows, 0:HALF]
            send_b[grain + q] += innovations[rows, HALF:members]
        return c

    lax.fori_loop(0, nblock, place, 0, unroll=8)


def pack(region, count, partner, pos, rinv, anom, innov):
    members = anom.shape[2]
    vmem, smem = pl.BlockSpec(memory_space=pltpu.VMEM), pl.BlockSpec(memory_space=pltpu.SMEM)
    hbm = pl.BlockSpec(memory_space=pl.ANY)
    return pl.pallas_call(
        pack_kernel,
        out_shape=(
            jax.ShapeDtypeStruct((SEND + SPARE, ROWS, members + HALF), bf16),
            jax.ShapeDtypeStruct((SEND + SPARE, ROWS, HALF), bf16),
            jax.ShapeDtypeStruct((SEND + SPARE, 128), f32),
            jax.ShapeDtypeStruct((8, 128), i32),
        ),
        in_specs=[smem, smem, vmem, vmem, vmem, hbm, hbm],
        out_specs=(vmem, vmem, vmem, vmem),
        scratch_shapes=[
            pltpu.VMEM((8 * anom.shape[0], 128), f32),
            pltpu.VMEM((2, *anom.shape), bf16),
            *[pltpu.SMEM((NR,), i32)] * 3,
            pltpu.SMEM((anom.shape[0],), i32),
            pltpu.SemaphoreType.DMA((2,)),
        ],
        compiler_params=pltpu.CompilerParams(vmem_limit_bytes=16 * MIB),
    )(region, count, partner, pos, rinv, anom, innov)


def exchange_kernel(send, send_b, send_w, head, total, flag_out, *scratch):
    scratch = list(scratch)

    def take(n):
        out = scratch[:n]
        del scratch[:n]
        return out

    zm, zs, bm, bs = take(LISTS), take(LISTS + 1), take(LISTS), take(LISTS + 1)
    wm, ws = take(LISTS), take(LISTS + 1)
    hm, hs, hsm, pn, pw, kept_a, kept_w, acc, ff = take(9)
    p, ro, rd, sb, u, rd2 = (take(2) for _ in range(6))
    zsend, zrecv, ssend, srecv, hsem, sems, recvs, fsend, frecv = take(9)

    members = acc.shape[3]
    x, tile = lax.axis_index("grp"), lax.axis_index("tile")
    z, inner = tile // 8, tile % 8
    y, core = inner // 2, inner % 2
    sibling = tile + 1 - 2 * core

    def around(step):
        return x, lax.rem(z + step, NZ) * 8 + inner

    def along(axis, step):
        if axis == 0:
            return x, z * 8 + lax.rem(y + step, NY) * 2 + core
        return lax.rem(x + step, NX), tile

    ways = (around(1), around(NZ - 1))
    barrier = pltpu.get_barrier_semaphore()
    for other in (*ways, (x, sibling), *(along(axis, step) for axis in range(2) for step in (1, 2, 3))):
        pl.semaphore_signal(barrier, inc=1, device_id=other, device_id_type=MESH)
    pl.semaphore_wait(barrier, 9)

    def copy(src, dst, send_sem, recv_sem, other):
        return pltpu.make_async_remote_copy(
            src_ref=src, dst_ref=dst, send_sem=send_sem, recv_sem=recv_sem, device_id=other, device_id_type=MESH
        )

    edges = (0, *CAPS[::-1])

    def hop_copies(way, hop):
        entry = way * HOPS + hop
        base = way * CAPS[0]
        out = []
        for k in range(HOPS - hop):
            lo, n = edges[k], edges[k + 1] - edges[k]
            src = send.at[pl.ds(base + lo, n)] if hop == 0 else zm[entry - 1].at[pl.ds(lo, n)]
            out.append((k, src, zm[entry].at[pl.ds(lo, n)]))
        rows = WCAPS[hop]
        out.append((4, send_w.at[pl.ds(base, rows)] if hop == 0 else wm[entry - 1].at[pl.ds(0, rows)], wm[entry]))
        out.append((5, head if hop == 0 else hm.at[entry - 1], hm.at[entry]))
        for k in range(HOPS - hop):
            lo, n = edges[k], edges[k + 1] - edges[k]
            src = send_b.at[pl.ds(base + lo, n)] if hop == 0 else bm[entry - 1].at[pl.ds(lo, n)]
            out.append((6 + k, src, bm[entry].at[pl.ds(lo, n)]))
        return {k: copy(src, dst, zsend.at[way, hop, k], zrecv.at[way, hop, k], ways[way]) for k, src, dst in out}

    z_copies = [[hop_copies(way, hop) for hop in range(HOPS)] for way in range(2)]
    order = [[5, 4, *range(HOPS - hop)] for hop in range(HOPS)]
    stay = pl.ds(2 * CAPS[0], STAY)
    pairs = [((hm.at[e], hs.at[e]), (zm[e], zs[e]), (wm[e], ws[e]), (bm[e], bs[e])) for e in range(LISTS)]
    pairs.append((
        (head, hs.at[LISTS]), (send.at[stay], zs[LISTS]), (send_w.at[stay], ws[LISTS]), (send_b.at[stay], bs[LISTS])
    ))
    side = [
        [copy(s, t, ssend.at[e, i], srecv.at[e, i], (x, sibling)) for i, (s, t) in enumerate(pairs[e])] for e in range(LISTS + 1)
    ]
    to_scalar = [pltpu.make_async_copy(hm.at[e], hsm.at[e], hsem.at[e]) for e in range(LISTS)]
    to_scalar.append(pltpu.make_async_copy(head, hsm.at[LISTS], hsem.at[LISTS]))
    to_scalar += [pltpu.make_async_copy(hs.at[e], hsm.at[LISTS + 1 + e], hsem.at[LISTS + 1 + e]) for e in range(LISTS + 1)]

    for k in order[0]:
        for way in range(2):
            z_copies[way][0][k].start()
    for c in side[LISTS]:
        c.start()
    to_scalar[LISTS].start()

    expand = (lax.broadcasted_iota(i32, (1024, 64), 0) // 16 == lax.broadcasted_iota(i32, (1024, 64), 1)).astype(bf16)
    keep = (lax.broadcasted_iota(i32, (1024, 128), 0) % 16 == lax.broadcasted_iota(i32, (1024, 128), 1) % 16).astype(f32)
    pick = (lax.broadcasted_iota(i32, (8, 128), 1) // 16 == lax.broadcasted_iota(i32, (8, 128), 0)).astype(bf16)

    own_stage, far_stage = (LISTS,), (HOPS - 1, LISTS - 1)
    stages = [own_stage, *((way * HOPS + hop,) for hop in range(HOPS - 1) for way in range(2)), far_stage]

    def place_of(at, entry, r):
        row, shift = (1, 0) if entry == LISTS else (0, entry // HOPS * NR)
        value = hsm[at, row, shift + r]
        return value // 256, value % 256

    row_of_lane = lax.broadcasted_iota(i32, (1, 128), 1) % ROWS

    def slots(entries, who, r):
        found = []
        for entry in entries:
            start, rows = place_of(entry + who * (LISTS + 1), entry, r)
            own = entry == LISTS
            base = 2 * CAPS[0] if own and not who else 0
            found.append((start, rows, base, STAY if own else CAPS[entry % HOPS]))
        out = []
        for i in range(8):
            places = [base + jnp.minimum(start // ROWS + i, cap - 1) for start, _, base, cap in found]
            start, rows = found[0][0:2]
            in_first = None
            if len(found) == 2:
                in_first = rows > 0
                start, rows = jnp.where(in_first, start, found[1][0]), jnp.where(in_first, rows, found[1][1])
            at = row_of_lane + ((start // ROWS + i) * ROWS - start)
            out.append((in_first, places[0], places[-1], (at >= 0) & (at < rows)))
        return out

    def sources(entries, who, mine, theirs, own):
        return [theirs[e] if who else (own if e == LISTS else mine[e]) for e in entries]

    def multiply(stage, target):
        for yp in range(NY):
            turned = pn[yp].astype(f32).T
            anomalies = kept_a[stage, yp]
            for b in range(8):
                weight = kept_w[stage, b : b + 1, yp * 256 : (yp + 1) * 256]
                product = jnp.dot((turned * weight).astype(bf16), anomalies, preferred_element_type=f32)
                if stage == 0:
                    acc[yp, b] = product
                elif stage < STAGES - 1:
                    acc[yp, b] += product
                elif b % 2 == 0:
                    target[0, yp, b // 2] = (acc[yp, b] + product).astype(bf16)
                else:
                    target[1, b // 2, yp] = (acc[yp, b] + product).astype(bf16)

    def first_columns(stage):
        entries = stages[stage]

        def gather(yp, carry):
            r = z * 8 + yp * 2 + core
            for who in range(2):
                panels = sources(entries, who, zm, zs, send)
                weights = sources(entries, who, wm, ws, send_w)
                for i, (first_list, slot, slot_2, live) in enumerate(slots(entries, who, r)):
                    panel, weight = panels[0][slot], weights[0][pl.ds(slot, 1), :]
                    if first_list is not None:
                        panel = jnp.where(first_list, panel, panels[1][slot_2])
                        weight = jnp.where(first_list, weight, weights[1][pl.ds(slot_2, 1), :])
                    rows = pl.ds(who * 128 + i * ROWS, ROWS)
                    kept_a[stage, yp, rows, :] = panel[:, 0:members]
                    pn[yp, rows, :] = panel[:, members : members + HALF]
                    pw[pl.ds(yp * 16 + who * 8 + i, 1), :] = jnp.where(live, weight, 0.0)
            return carry

        lax.fori_loop(0, NY, gather, 0)
        wide = jnp.dot(expand, pw[...].astype(bf16), preferred_element_type=f32) * keep
        kept_w[stage] = lax.dot_general(pick, wide.astype(bf16), (((1,), (1,)), ((), ())), preferred_element_type=f32)
        multiply(stage, p[0])

    def other_columns(stage):
        entries = stages[stage]

        def gather(yp, carry):
            r = z * 8 + yp * 2 + core
            for who in range(2):
                panels = sources(entries, who, bm, bs, send_b)
                for i, (first_list, slot, slot_2, live) in enumerate(slots(entries, who, r)):
                    panel = panels[0][slot]
                    if first_list is not None:
                        panel = jnp.where(first_list, panel, panels[1][slot_2])
                    pn[yp, pl.ds(who * 128 + i * ROWS, ROWS), :] = panel
            return carry

        lax.fori_loop(0, NY, gather, 0)
        multiply(stage, p[1])

    def ready(entry):
        for c in side[entry][0:3]:
            c.wait_recv()
        for at in (entry, LISTS + 1 + entry):
            if at > LISTS:
                to_scalar[at].start()
            to_scalar[at].wait()

    def wide_of(ref):
        return ref[...].astype(f32)

    def flag_copy(src, dst, k, axis, step):
        return copy(ff.at[src], ff.at[dst], fsend.at[k], frecv.at[k], along(axis, step))

    flags = [
        flag_copy(0, 1, 0, 0, 1), flag_copy(0, 2, 1, 0, 3), flag_copy(3, 4, 2, 0, 1),
        flag_copy(5, 6, 3, 1, 1), flag_copy(5, 7, 4, 1, 3), flag_copy(8, 9, 5, 1, 1),
    ]

    def reducer(part):
        p_, ro_, rd_, sb_, u_, rd2_ = (buffers[part] for buffers in (p, ro, rd, sb, u, rd2))

        def half_copy(src, dst, half, phase, k, axis, step):
            return copy(src, dst, sems.at[part, half, phase, k], recvs.at[part, half, phase, k], along(axis, step))

        def triple(me):
            return lax.rem(me + 1, 4), lax.rem(me + 3, 4), lax.rem(me + 2, 4)

        first, second = [], []
        for half in range(2):
            me, other = (y, x) if half == 0 else (x, y)
            right, left, far = triple(me)
            lo, hi = pl.ds(0, 2), pl.ds(2, 2)
            first.append([
                half_copy(p_.at[half, far, lo], ro_.at[half, 0], half, 0, 0, half, 1),
                half_copy(p_.at[half, far, hi], ro_.at[half, 1], half, 0, 1, half, 3),
                half_copy(p_.at[half, right, hi], rd_.at[half, 0, hi], half, 0, 2, half, 1),
                half_copy(p_.at[half, left, lo], rd_.at[half, 1, lo], half, 0, 3, half, 3),
                half_copy(sb_.at[half, 0], rd_.at[half, 0, lo], half, 0, 4, half, 1),
                half_copy(sb_.at[half, 1], rd_.at[half, 1, hi], half, 0, 5, half, 3),
            ])
            axis = 1 - half
            second.append([
                half_copy(u_.at[half, lax.rem(other + step, 4)], rd2_.at[half, step - 1], half, 1, step - 1, axis, step)
                for step in (1, 2, 3)
            ])

        def begin():
            for k in range(4):
                for half in range(2):
                    first[half][k].start()
            if part == 0:
                flag = head[...] + hs[LISTS]
                for e in range(LISTS):
                    flag = flag + hm[e] + hs[e]
                ff[0] = flag.astype(f32)
                flags[0].start()
                flags[1].start()

        def pass_on():
            for k in range(2):
                for half in range(2):
                    me = y if half == 0 else x
                    to = lax.rem(me + (1 if k == 0 else 3), 4)
                    first[half][k].wait_recv()
                    for i in range(2):
                        sb_[half, k, i] = (wide_of(p_.at[half, to, 2 * k + i]) + wide_of(ro_.at[half, k, i])).astype(bf16)
                    first[half][4 + k].start()
            if part == 0:
                flags[0].wait_recv()
                ff[3] = ff[0] + ff[1]
                flags[2].start()

        def turn():
            for half in range(2):
                me = y if half == 0 else x
                for k in (2, 3, 4, 5):
                    first[half][k].wait_recv()
                for i in range(4):
                    u_[half, i] = (
                        wide_of(p_.at[half, me, i]) + wide_of(rd_.at[half, 0, i]) + wide_of(rd_.at[half, 1, i])
                    ).astype(bf16)
                for k in (1, 0, 2):
                    second[half][k].start()
            if part == 0:
                flags[1].wait_recv()
                flags[2].wait_recv()
                ff[5] = ff[0] + ff[2] + ff[4]
                flags[3].start()
                flags[4].start()

        def relay():
            if part == 0:
                flags[3].wait_recv()
                ff[8] = ff[5] + ff[6]
                flags[5].start()

        def finish():
            for half in range(2):
                other = x if half == 0 else y
                turned = wide_of(u_.at[half, other])
                for k in range(3):
                    second[half][k].wait_recv()
                    turned = turned + wide_of(rd2_.at[half, k])
                total[half, :, part * HALF : (part + 1) * HALF] = turned.T
            if part == 0:
                flags[4].wait_recv()
                flags[5].wait_recv()
                flag_out[...] = ff[5] + ff[7] + ff[9]

        def drain():
            for c in (*first[0], *first[1], *second[0], *second[1]):
                c.wait_send()

        return begin, (pass_on, turn, relay, finish), drain

    begin_a, steps_a, drain_a = reducer(0)
    begin_b, steps_b, drain_b = reducer(1)

    for hop in range(HOPS):
        for k in order[hop]:
            for way in range(2):
                entry = way * HOPS + hop
                z_copies[way][hop][k].wait_recv()
                if hop + 1 < HOPS and k in z_copies[way][hop + 1]:
                    z_copies[way][hop + 1][k].start()
                if k == 5:
                    side[entry][0].start()
                    to_scalar[entry].start()
        for way in range(2):
            entry = way * HOPS + hop
            side[entry][1].start()
            side[entry][2].start()
        if hop == HOPS - 2:
            for k in range(HOPS):
                for way in range(2):
                    z_copies[way][0][6 + k].start()
        if hop == 0:
            ready(LISTS)
            first_columns(0)
        else:
            for way in range(2):
                ready(way * HOPS + hop - 1)
                first_columns(1 + 2 * (hop - 1) + way)
    for entry in far_stage:
        ready(entry)
    first_columns(STAGES - 1)
    begin_a()

    for hop in range(HOPS):
        for k in range(HOPS - hop):
            for way in range(2):
                z_copies[way][hop][6 + k].wait_recv()
                if hop + 1 < HOPS and 6 + k in z_copies[way][hop + 1]:
                    z_copies[way][hop + 1][6 + k].start()
        for way in range(2):
            side[way * HOPS + hop][3].start()
        if hop == 0:
            side[LISTS][3].wait_recv()
            other_columns(0)
            steps_a[0]()
        else:
            for way in range(2):
                side[way * HOPS + hop - 1][3].wait_recv()
                other_columns(1 + 2 * (hop - 1) + way)
                if way == 0:
                    steps_a[hop]()
    for entry in far_stage:
        side[entry][3].wait_recv()
    other_columns(STAGES - 1)
    begin_b()
    for step in steps_b:
        step()

    drain_a()
    drain_b()
    for way in range(2):
        for hop in range(HOPS):
            for k in z_copies[way][hop]:
                z_copies[way][hop][k].wait_send()
    for group in side:
        for c in group:
            c.wait_send()
    for c in flags:
        c.wait_send()


def exchange(send, send_b, send_w, head):
    vmem = pl.BlockSpec(memory_space=pltpu.VMEM)
    members = send.shape[2] - HALF
    square, slab = (members, members), (HALF, members)
    dma = pltpu.SemaphoreType.DMA
    panels = [pltpu.VMEM((cap, ROWS, members + HALF), bf16) for cap in CAPS] * 2
    others = [pltpu.VMEM((cap, ROWS, HALF), bf16) for cap in CAPS] * 2
    weights = [pltpu.VMEM((cap, 128), f32) for cap in WCAPS] * 2
    return pl.pallas_call(
        exchange_kernel,
        out_shape=(
            jax.ShapeDtypeStruct((2, *square), f32),
            jax.ShapeDtypeStruct((8, 128), f32),
        ),
        in_specs=[vmem] * 4,
        out_specs=(vmem, vmem),
        scratch_shapes=[
            *panels,
            *panels,
            pltpu.VMEM((STAY, ROWS, members + HALF), bf16),
            *others,
            *others,
            pltpu.VMEM((STAY, ROWS, HALF), bf16),
            *weights,
            *weights,
            pltpu.VMEM((STAY, 128), f32),
            pltpu.VMEM((LISTS, 8, 128), i32),
            pltpu.VMEM((LISTS + 1, 8, 128), i32),
            pltpu.SMEM((2 * LISTS + 2, 8, 128), i32),
            pltpu.VMEM((NY, 256, HALF), bf16),
            pltpu.VMEM((NY * 16, 128), f32),
            pltpu.VMEM((STAGES, NY, 256, members), bf16),
            pltpu.VMEM((STAGES, 8, NY * 256), f32),
            pltpu.VMEM((NY, 8, *slab), f32),
            pltpu.VMEM((10, 8, 128), f32),
            *[pltpu.VMEM((2, 4, 4, *slab), bf16)] * 2,
            *[pltpu.VMEM((2, 2, 2, *slab), bf16)] * 2,
            *[pltpu.VMEM((2, 2, 4, *slab), bf16)] * 2,
            *[pltpu.VMEM((2, 2, 2, *slab), bf16)] * 2,
            *[pltpu.VMEM((2, 4, *slab), bf16)] * 2,
            *[pltpu.VMEM((2, 3, *slab), bf16)] * 2,
            dma((2, HOPS, 6 + HOPS)),
            dma((2, HOPS, 6 + HOPS)),
            dma((LISTS + 1, 4)),
            dma((LISTS + 1, 4)),
            dma((2 * LISTS + 2,)),
            dma((2, 2, 2, 6)),
            dma((2, 2, 2, 6)),
            dma((6,)),
            dma((6,)),
        ],
        compiler_params=pltpu.CompilerParams(collective_id=0, has_side_effects=True, vmem_limit_bytes=46 * MIB),
    )(send, send_b, send_w, head)


def update_kernel(state, coeff, total, updated, new_coeff, coef):
    @pl.when(pl.program_id(1) == 0)
    def _():
        new = (1.0 - relaxation) * coeff[...] + relaxation * total[...]
        new_coeff[...] = new
        coef[...] = new.astype(bf16)

    s = state[...]
    updated[...] = (s.astype(f32) + jnp.dot(s, coef[...], preferred_element_type=f32)).astype(bf16)


def update(state, coeff, total):
    _, blocks, width, members = state.shape
    step = 2048
    square = (members, members)
    rows = pl.BlockSpec((None, None, step, members), lambda j, i: (0, j, i, 0))
    one = pl.BlockSpec((None, None, *square), lambda j, i: (0, j, 0, 0))
    return pl.pallas_call(
        update_kernel,
        grid=(blocks, width // step),
        out_shape=(jax.ShapeDtypeStruct(state.shape, bf16), jax.ShapeDtypeStruct(coeff.shape, f32)),
        in_specs=[rows, one, pl.BlockSpec((None, *square), lambda j, i: (j, 0, 0))],
        out_specs=(rows, one),
        scratch_shapes=[pltpu.VMEM(square, bf16)],
        compiler_params=pltpu.CompilerParams(vmem_limit_bytes=16 * MIB),
    )(state, coeff, total)


def padded_total(obs_anom, innov, obs_rinv, obs_pos, obs_count, obs_region, obs_partner, blocks, width):
    tile_count = lax.axis_size("tile")
    nblock, observation_count, ensemble_members = obs_anom.shape
    partition_count = obs_partner.shape[1]
    nlocal = lax.axis_size("grp") * blocks
    per_neighbour = max(2, (2 * nblock + tile_count - 1) // tile_count)
    slot_count = tile_count * per_neighbour
    slot_grouping = 8
    region = obs_region[:, 0]
    order = jnp.arange(nblock, dtype=jnp.int32)
    before = (region[None, :] == region[:, None]) & (order[None, :] < order[:, None])
    destination = region * per_neighbour + jnp.sum(before.astype(jnp.int32), axis=1)
    assignment_rule = destination[None, :] == jnp.arange(slot_count, dtype=jnp.int32)[:, None]
    place_half = assignment_rule.astype(jnp.bfloat16)
    place_int = assignment_rule.astype(jnp.int32)
    labels = jnp.concatenate([obs_count[:, None], obs_partner], axis=1)
    sent_labels = jnp.dot(place_int, labels).reshape(tile_count, per_neighbour, partition_count + 1)
    stacked = jnp.concatenate([obs_anom, innov], axis=2).reshape(nblock, -1)
    packed = jnp.dot(place_half, stacked, preferred_element_type=jnp.bfloat16)
    packed = packed.reshape(tile_count, per_neighbour, observation_count, 2 * ensemble_members)
    sent_pos = jnp.dot(place_int, obs_pos).reshape(tile_count, per_neighbour, observation_count)
    sent_var = jnp.dot(assignment_rule.astype(jnp.float32), obs_rinv, precision=lax.Precision.HIGHEST)
    sent_var = sent_var.reshape(tile_count, per_neighbour, observation_count)

    def exchange(array):
        return lax.all_to_all(array, "tile", split_axis=0, concat_axis=0, tiled=True)

    received_panels = exchange(packed).reshape(slot_count, observation_count, 2 * ensemble_members)
    flattened_labels = exchange(sent_labels).reshape(slot_count, partition_count + 1)
    recv_anom = received_panels[:, :, :ensemble_members]
    recv_innov = received_panels[:, :, ensemble_members:]
    flattened_positions = exchange(sent_pos).reshape(slot_count, observation_count)
    flattened_variances = exchange(sent_var).reshape(slot_count, observation_count)
    partners = flattened_labels[:, 1:]
    block_index = jnp.arange(nlocal, dtype=jnp.int32)

    def accumulate_group(step, total):
        start = step * slot_grouping

        def part(array):
            return lax.dynamic_slice_in_dim(array, start, slot_grouping, 0)

        weights = taper_weights(
            part(flattened_positions), part(partners), part(flattened_labels)[:, 0], part(flattened_variances), width,
            ensemble_members,
        )
        scaled_part = (weights[..., None] * part(recv_innov)[:, None].astype(jnp.float32)).astype(jnp.bfloat16)
        picked = (part(partners)[..., None] == block_index).astype(jnp.bfloat16)
        by_block = jnp.einsum("qkb,qkin->qbin", picked, scaled_part, preferred_element_type=jnp.float32).astype(jnp.bfloat16)
        return total + jnp.einsum("qim,qbin->bmn", part(recv_anom), by_block, preferred_element_type=jnp.float32)

    initial_total = jnp.zeros((nlocal, ensemble_members, ensemble_members), jnp.float32)
    running_totals = lax.fori_loop(0, slot_count // slot_grouping, accumulate_group, initial_total)
    return lax.psum_scatter(running_totals.astype(jnp.bfloat16), "grp", scatter_dimension=0, tiled=True).astype(jnp.float32)


def on_device(obs_anom, innov, obs_rinv, obs_pos, obs_count, obs_region, obs_partner, state_anom, coeff):
    send, send_b, send_w, head = pack(obs_region[:, 0], obs_count, obs_partner.T, obs_pos, obs_rinv, obs_anom, innov)
    fast, flags = exchange(send, send_b, send_w, head)
    blocks, width = state_anom.shape[1:3]
    total = lax.cond(
        flags[1, NR] > 0,
        lambda *obs: padded_total(*obs[:-1], blocks, width),
        lambda *obs: obs[-1],
        obs_anom, innov, obs_rinv, obs_pos, obs_count, obs_region, obs_partner, fast,
    )
    return update(state_anom, coeff, total)


def solution(mesh):
    return jax.shard_map(
        on_device,
        mesh=mesh,
        in_specs=(
            P(("grp", "tile"), None, None),
            P(("grp", "tile"), None, None),
            P(("grp", "tile"), None),
            P(("grp", "tile"), None),
            P(("grp", "tile")),
            P(("grp", "tile"), None),
            P(("grp", "tile"), None),
            P("grp", "tile", None, None),
            P("grp", "tile", None, None),
        ),
        out_specs=(P("grp", "tile", None, None), P("grp", "tile", None, None)),
        check_vma=False,
    )
```

```python
import jax
import jax.numpy as jnp
from jax import lax
from jax.experimental import pallas as pl
from jax.experimental.pallas import tpu as pltpu
from jax.sharding import PartitionSpec as P

relaxation = 0.5
bf16, f32, i32 = jnp.bfloat16, jnp.float32, jnp.int32
MESH = pl.DeviceIdType.MESH
MIB = 1024 * 1024

ROWS = 16
CAPS = (56, 46, 34, 24)
STAY = 32
SEND = 2 * CAPS[0] + STAY
SPARE = 8
HOPS = len(CAPS)
NZ, NY, NX, NR = 8, 4, 4, 64
LISTS = 2 * HOPS
HALF = 128
WCAPS = tuple((cap + 7) // 8 * 8 for cap in CAPS)
STAGES = 2 * HOPS


def taper_weights(positions, partners, counts, inverse_var, width, ensemble_members):
    center = (partners.astype(jnp.float32) + 0.5) * width
    offset = (positions.astype(jnp.float32)[..., None, :] - center[..., :, None]) / (2.0 * width)
    index = jnp.arange(positions.shape[-1], dtype=jnp.int32)
    live = index < counts[..., None]
    weight = jnp.exp(-offset * offset) * inverse_var[..., None, :] / (ensemble_members - 1.0)
    return jnp.where(live[..., None, :], weight, 0.0)


def pack_kernel(
    region, count, partner, pos, rinv, anom, innov, send, send_b, send_w, head, wall, held, size, fill, seats, place_at, sem
):
    nblock, members = anom.shape[0], anom.shape[2]
    width = 4096.0
    z = lax.axis_index("tile") // 8
    loads = [pltpu.make_async_copy(source, held.at[i], sem.at[i]) for i, source in enumerate((anom, innov))]
    for c in loads:
        c.start()

    deep = 8 * nblock
    lane = lax.broadcasted_iota(i32, (deep, 128), 1)
    repeat = (lax.broadcasted_iota(i32, (deep, nblock), 0) // 8 == lax.broadcasted_iota(i32, (deep, nblock), 1)).astype(f32)
    column = lax.broadcasted_iota(i32, (deep, 64), 1)
    quarter = (column // 16 == lax.broadcasted_iota(i32, (deep, 64), 0) % 8).astype(f32)
    fold = (lax.broadcasted_iota(i32, (64, 128), 0) % 16 == lax.broadcasted_iota(i32, (64, 128), 1) % 16).astype(f32)

    def exact(a, b):
        return jnp.dot(a, b, precision=lax.Precision.HIGHEST, preferred_element_type=f32)

    def spread(values):
        return exact(exact(repeat, values) * quarter, fold)

    partners = lax.dot_general(
        repeat, partner[...].astype(f32), (((1,), (1,)), ((), ())), precision=lax.Precision.HIGHEST, preferred_element_type=f32
    )
    block_of_lane = (lane // 16).astype(f32)
    paired = jnp.zeros((deep, 128), f32)
    for k in range(partner.shape[0]):
        paired = jnp.where(partners[:, k : k + 1] == block_of_lane, 1.0, paired)
    center = (block_of_lane + 0.5) * width
    offset = (spread(pos[...].astype(f32)) - center) / (2.0 * width)
    wall[...] = jnp.exp(-offset * offset) * spread(rinv[...]) / (members - 1.0) * paired

    def clear(i, c):
        size[i] = 0
        fill[i] = 0
        return c

    lax.fori_loop(0, NR, clear, 0, unroll=16)

    def blank(i, c):
        send[i] = jnp.zeros(send.shape[1:], bf16)
        send_b[i] = jnp.zeros(send_b.shape[1:], bf16)
        return c

    lax.fori_loop(0, SEND + SPARE, blank, 0, unroll=8)
    send_w[...] = jnp.zeros_like(send_w)

    def measure(o, c):
        r = region[o]
        size[r] = size[r] + count[o]
        return c

    lax.fori_loop(0, nblock, measure, 0, unroll=8)

    def plane(distance):
        return lax.rem(z + distance, NZ) * 8

    def total(distance):
        base = plane(distance)
        return sum(size[base + i] for i in range(8))

    head_row = lax.broadcasted_iota(i32, (8, 128), 0)
    head_lane = lax.broadcasted_iota(i32, (8, 128), 1)

    def noted(header, row, at, value):
        return jnp.where((head_row == row) & (head_lane == at), value, header)

    def begin(used, n):
        return jnp.where(used % ROWS + n > 8 * ROWS, (used + ROWS - 1) // ROWS * ROWS, used)

    def seat_far(i, carry):
        used_right, used_left, load_right, load_left, header = carry
        r = plane(4) + i
        n = size[r]
        to_right = load_right <= load_left
        right, left = begin(used_right, n), begin(used_left, n)
        header = noted(header, 0, r, jnp.where(to_right, right * 256 + n, 0))
        header = noted(header, 0, NR + r, jnp.where(to_right, 0, left * 256 + n))
        seats[r] = jnp.where(to_right, right, CAPS[0] * ROWS + left)
        used_right, used_left = jnp.where(to_right, right + n, used_right), jnp.where(to_right, used_left, left + n)
        load_right, load_left = jnp.where(to_right, load_right + n, load_right), jnp.where(to_right, load_left, load_left + n)
        return used_right, used_left, load_right, load_left, header

    loads_of = (total(1) + total(2) + total(3), total(5) + total(6) + total(7))
    none = jnp.zeros((), i32)
    used_right, used_left, _, _, header = lax.fori_loop(0, 8, seat_far, (none, none, *loads_of, jnp.zeros((8, 128), i32)), unroll=8)

    def seat_near(distance, base, row, shift, carry):
        def seat(i, carry):
            used, header = carry
            r = plane(distance) + i
            n = size[r]
            first = begin(used, n)
            seats[r] = base * ROWS + first
            return first + n, noted(header, row, shift + r, first * 256 + n)

        return lax.fori_loop(0, 8, seat, carry, unroll=8)

    over = (used_right > CAPS[3] * ROWS) | (used_left > CAPS[3] * ROWS)
    for hop, distance in ((2, 3), (1, 2), (0, 1)):
        used_right, header = seat_near(distance, 0, 0, 0, (used_right, header))
        used_left, header = seat_near(NZ - distance, CAPS[0], 0, NR, (used_left, header))
        over = over | (used_right > CAPS[hop] * ROWS) | (used_left > CAPS[hop] * ROWS)
    used_stay, header = seat_near(0, 2 * CAPS[0], 1, 0, (none, header))
    over = over | (used_stay > STAY * ROWS)
    head[...] = noted(header, 1, NR, over.astype(i32))

    def find(o, c):
        r = region[o]
        place_at[o] = seats[r] + fill[r]
        fill[r] = fill[r] + count[o]
        return c

    lax.fori_loop(0, nblock, find, 0, unroll=8)
    for c in loads:
        c.wait()

    deep_window = 5 * ROWS
    to_row = lax.broadcasted_iota(i32, (deep_window, 64), 0)
    from_row = lax.broadcasted_iota(i32, (deep_window, 64), 1)

    sub = lax.broadcasted_iota(i32, (8, 128), 0)
    row_of_lane = lax.broadcasted_iota(i32, (8, 128), 1) % ROWS

    def place(o, c):
        live, at = count[o], place_at[o]
        shift = at % ROWS
        grain = jnp.minimum(at // ROWS, SEND + SPARE - 8)
        weight = jnp.where(sub * ROWS + row_of_lane < live, wall[pl.ds(pl.multiple_of(o * 8, 8), 8), :], 0.0)
        same = pltpu.roll(weight, shift, 1)
        next_one = pltpu.roll(pltpu.roll(weight, 1, 0), shift + 128 - ROWS, 1)
        send_w[pl.ds(grain, 8), :] += jnp.where(row_of_lane >= shift, same, next_one)

        move = ((to_row - shift == from_row) & (from_row < live)).astype(bf16)
        anomalies = jnp.dot(move, held[0, o], preferred_element_type=f32).astype(bf16)
        innovations = jnp.dot(move, held[1, o], preferred_element_type=f32).astype(bf16)
        for q in range(5):
            rows = slice(q * ROWS, (q + 1) * ROWS)
            send[grain + q, :, 0:members] += anomalies[rows]
            send[grain + q, :, members : members + HALF] += innovations[rows, 0:HALF]
            send_b[grain + q] += innovations[rows, HALF:members]
        return c

    lax.fori_loop(0, nblock, place, 0, unroll=8)


def pack(region, count, partner, pos, rinv, anom, innov):
    members = anom.shape[2]
    vmem, smem = pl.BlockSpec(memory_space=pltpu.VMEM), pl.BlockSpec(memory_space=pltpu.SMEM)
    hbm = pl.BlockSpec(memory_space=pl.ANY)
    return pl.pallas_call(
        pack_kernel,
        out_shape=(
            jax.ShapeDtypeStruct((SEND + SPARE, ROWS, members + HALF), bf16),
            jax.ShapeDtypeStruct((SEND + SPARE, ROWS, HALF), bf16),
            jax.ShapeDtypeStruct((SEND + SPARE, 128), f32),
            jax.ShapeDtypeStruct((8, 128), i32),
        ),
        in_specs=[smem, smem, vmem, vmem, vmem, hbm, hbm],
        out_specs=(vmem, vmem, vmem, vmem),
        scratch_shapes=[
            pltpu.VMEM((8 * anom.shape[0], 128), f32),
            pltpu.VMEM((2, *anom.shape), bf16),
            *[pltpu.SMEM((NR,), i32)] * 3,
            pltpu.SMEM((anom.shape[0],), i32),
            pltpu.SemaphoreType.DMA((2,)),
        ],
        compiler_params=pltpu.CompilerParams(vmem_limit_bytes=16 * MIB),
    )(region, count, partner, pos, rinv, anom, innov)


def exchange_kernel(send, send_b, send_w, head, total, flag_out, *scratch):
    scratch = list(scratch)

    def take(n):
        out = scratch[:n]
        del scratch[:n]
        return out

    zm, zs, bm, bs = take(LISTS), take(LISTS + 1), take(LISTS), take(LISTS + 1)
    wm, ws = take(LISTS), take(LISTS + 1)
    hm, hs, hsm, pn, pw, kept_a, kept_w, acc, ff = take(9)
    p, ro, rd, sb, u, rd2 = (take(2) for _ in range(6))
    zsend, zrecv, ssend, srecv, hsem, sems, recvs, fsend, frecv = take(9)

    members = acc.shape[3]
    x, tile = lax.axis_index("grp"), lax.axis_index("tile")
    z, inner = tile // 8, tile % 8
    y, core = inner // 2, inner % 2
    sibling = tile + 1 - 2 * core

    def around(step):
        return x, lax.rem(z + step, NZ) * 8 + inner

    def along(axis, step):
        if axis == 0:
            return x, z * 8 + lax.rem(y + step, NY) * 2 + core
        return lax.rem(x + step, NX), tile

    ways = (around(1), around(NZ - 1))
    barrier = pltpu.get_barrier_semaphore()
    for other in (*ways, (x, sibling), *(along(axis, step) for axis in range(2) for step in (1, 2, 3))):
        pl.semaphore_signal(barrier, inc=1, device_id=other, device_id_type=MESH)
    pl.semaphore_wait(barrier, 9)

    def copy(src, dst, send_sem, recv_sem, other):
        return pltpu.make_async_remote_copy(
            src_ref=src, dst_ref=dst, send_sem=send_sem, recv_sem=recv_sem, device_id=other, device_id_type=MESH
        )

    edges = (0, *CAPS[::-1])

    def hop_copies(way, hop):
        entry = way * HOPS + hop
        base = way * CAPS[0]
        out = []
        for k in range(HOPS - hop):
            lo, n = edges[k], edges[k + 1] - edges[k]
            src = send.at[pl.ds(base + lo, n)] if hop == 0 else zm[entry - 1].at[pl.ds(lo, n)]
            out.append((k, src, zm[entry].at[pl.ds(lo, n)]))
        rows = WCAPS[hop]
        out.append((4, send_w.at[pl.ds(base, rows)] if hop == 0 else wm[entry - 1].at[pl.ds(0, rows)], wm[entry]))
        out.append((5, head if hop == 0 else hm.at[entry - 1], hm.at[entry]))
        for k in range(HOPS - hop):
            lo, n = edges[k], edges[k + 1] - edges[k]
            src = send_b.at[pl.ds(base + lo, n)] if hop == 0 else bm[entry - 1].at[pl.ds(lo, n)]
            out.append((6 + k, src, bm[entry].at[pl.ds(lo, n)]))
        return {k: copy(src, dst, zsend.at[way, hop, k], zrecv.at[way, hop, k], ways[way]) for k, src, dst in out}

    z_copies = [[hop_copies(way, hop) for hop in range(HOPS)] for way in range(2)]
    order = [[5, 4, *range(HOPS - hop)] for hop in range(HOPS)]
    stay = pl.ds(2 * CAPS[0], STAY)
    pairs = [((hm.at[e], hs.at[e]), (zm[e], zs[e]), (wm[e], ws[e]), (bm[e], bs[e])) for e in range(LISTS)]
    pairs.append((
        (head, hs.at[LISTS]), (send.at[stay], zs[LISTS]), (send_w.at[stay], ws[LISTS]), (send_b.at[stay], bs[LISTS])
    ))
    side = [
        [copy(s, t, ssend.at[e, i], srecv.at[e, i], (x, sibling)) for i, (s, t) in enumerate(pairs[e])] for e in range(LISTS + 1)
    ]
    to_scalar = [pltpu.make_async_copy(hm.at[e], hsm.at[e], hsem.at[e]) for e in range(LISTS)]
    to_scalar.append(pltpu.make_async_copy(head, hsm.at[LISTS], hsem.at[LISTS]))
    to_scalar += [pltpu.make_async_copy(hs.at[e], hsm.at[LISTS + 1 + e], hsem.at[LISTS + 1 + e]) for e in range(LISTS + 1)]

    for k in order[0]:
        for way in range(2):
            z_copies[way][0][k].start()
    for c in side[LISTS]:
        c.start()
    to_scalar[LISTS].start()

    expand = (lax.broadcasted_iota(i32, (1024, 64), 0) // 16 == lax.broadcasted_iota(i32, (1024, 64), 1)).astype(bf16)
    keep = (lax.broadcasted_iota(i32, (1024, 128), 0) % 16 == lax.broadcasted_iota(i32, (1024, 128), 1) % 16).astype(f32)
    pick = (lax.broadcasted_iota(i32, (8, 128), 1) // 16 == lax.broadcasted_iota(i32, (8, 128), 0)).astype(bf16)

    own_stage, far_stage = (LISTS,), (HOPS - 1, LISTS - 1)
    stages = [own_stage, *((way * HOPS + hop,) for hop in range(HOPS - 1) for way in range(2)), far_stage]

    def place_of(at, entry, r):
        row, shift = (1, 0) if entry == LISTS else (0, entry // HOPS * NR)
        value = hsm[at, row, shift + r]
        return value // 256, value % 256

    row_of_lane = lax.broadcasted_iota(i32, (1, 128), 1) % ROWS

    def slots(entries, who, r):
        found = []
        for entry in entries:
            start, rows = place_of(entry + who * (LISTS + 1), entry, r)
            own = entry == LISTS
            base = 2 * CAPS[0] if own and not who else 0
            found.append((start, rows, base, STAY if own else CAPS[entry % HOPS]))
        out = []
        for i in range(8):
            places = [base + jnp.minimum(start // ROWS + i, cap - 1) for start, _, base, cap in found]
            start, rows = found[0][0:2]
            in_first = None
            if len(found) == 2:
                in_first = rows > 0
                start, rows = jnp.where(in_first, start, found[1][0]), jnp.where(in_first, rows, found[1][1])
            at = row_of_lane + ((start // ROWS + i) * ROWS - start)
            out.append((in_first, places[0], places[-1], (at >= 0) & (at < rows)))
        return out

    def sources(entries, who, mine, theirs, own):
        return [theirs[e] if who else (own if e == LISTS else mine[e]) for e in entries]

    def multiply(stage, target):
        for yp in range(NY):
            turned = pn[yp].astype(f32).T
            anomalies = kept_a[stage, yp]
            for b in range(8):
                weight = kept_w[stage, b : b + 1, yp * 256 : (yp + 1) * 256]
                product = jnp.dot((turned * weight).astype(bf16), anomalies, preferred_element_type=f32)
                if stage == 0:
                    acc[yp, b] = product
                elif stage < STAGES - 1:
                    acc[yp, b] += product
                elif b % 2 == 0:
                    target[0, yp, b // 2] = (acc[yp, b] + product).astype(bf16)
                else:
                    target[1, b // 2, yp] = (acc[yp, b] + product).astype(bf16)

    def first_columns(stage):
        entries = stages[stage]

        def gather(yp, carry):
            r = z * 8 + yp * 2 + core
            for who in range(2):
                panels = sources(entries, who, zm, zs, send)
                weights = sources(entries, who, wm, ws, send_w)
                for i, (first_list, slot, slot_2, live) in enumerate(slots(entries, who, r)):
                    panel, weight = panels[0][slot], weights[0][pl.ds(slot, 1), :]
                    if first_list is not None:
                        panel = jnp.where(first_list, panel, panels[1][slot_2])
                        weight = jnp.where(first_list, weight, weights[1][pl.ds(slot_2, 1), :])
                    rows = pl.ds(who * 128 + i * ROWS, ROWS)
                    kept_a[stage, yp, rows, :] = panel[:, 0:members]
                    pn[yp, rows, :] = panel[:, members : members + HALF]
                    pw[pl.ds(yp * 16 + who * 8 + i, 1), :] = jnp.where(live, weight, 0.0)
            return carry

        lax.fori_loop(0, NY, gather, 0)
        wide = jnp.dot(expand, pw[...].astype(bf16), preferred_element_type=f32) * keep
        kept_w[stage] = lax.dot_general(pick, wide.astype(bf16), (((1,), (1,)), ((), ())), preferred_element_type=f32)
        multiply(stage, p[0])

    def other_columns(stage):
        entries = stages[stage]

        def gather(yp, carry):
            r = z * 8 + yp * 2 + core
            for who in range(2):
                panels = sources(entries, who, bm, bs, send_b)
                for i, (first_list, slot, slot_2, live) in enumerate(slots(entries, who, r)):
                    panel = panels[0][slot]
                    if first_list is not None:
                        panel = jnp.where(first_list, panel, panels[1][slot_2])
                    pn[yp, pl.ds(who * 128 + i * ROWS, ROWS), :] = panel
            return carry

        lax.fori_loop(0, NY, gather, 0)
        multiply(stage, p[1])

    def ready(entry):
        for c in side[entry][0:3]:
            c.wait_recv()
        for at in (entry, LISTS + 1 + entry):
            if at > LISTS:
                to_scalar[at].start()
            to_scalar[at].wait()

    def wide_of(ref):
        return ref[...].astype(f32)

    def flag_copy(src, dst, k, axis, step):
        return copy(ff.at[src], ff.at[dst], fsend.at[k], frecv.at[k], along(axis, step))

    flags = [
        flag_copy(0, 1, 0, 0, 1), flag_copy(0, 2, 1, 0, 3), flag_copy(3, 4, 2, 0, 1),
        flag_copy(5, 6, 3, 1, 1), flag_copy(5, 7, 4, 1, 3), flag_copy(8, 9, 5, 1, 1),
    ]

    def reducer(part):
        p_, ro_, rd_, sb_, u_, rd2_ = (buffers[part] for buffers in (p, ro, rd, sb, u, rd2))

        def half_copy(src, dst, half, phase, k, axis, step):
            return copy(src, dst, sems.at[part, half, phase, k], recvs.at[part, half, phase, k], along(axis, step))

        def triple(me):
            return lax.rem(me + 1, 4), lax.rem(me + 3, 4), lax.rem(me + 2, 4)

        first, second = [], []
        for half in range(2):
            me, other = (y, x) if half == 0 else (x, y)
            right, left, far = triple(me)
            lo, hi = pl.ds(0, 2), pl.ds(2, 2)
            first.append([
                half_copy(p_.at[half, far, lo], ro_.at[half, 0], half, 0, 0, half, 1),
                half_copy(p_.at[half, far, hi], ro_.at[half, 1], half, 0, 1, half, 3),
                half_copy(p_.at[half, right, hi], rd_.at[half, 0, hi], half, 0, 2, half, 1),
                half_copy(p_.at[half, left, lo], rd_.at[half, 1, lo], half, 0, 3, half, 3),
                half_copy(sb_.at[half, 0], rd_.at[half, 0, lo], half, 0, 4, half, 1),
                half_copy(sb_.at[half, 1], rd_.at[half, 1, hi], half, 0, 5, half, 3),
            ])
            axis = 1 - half
            second.append([
                half_copy(u_.at[half, lax.rem(other + step, 4)], rd2_.at[half, step - 1], half, 1, step - 1, axis, step)
                for step in (1, 2, 3)
            ])

        def begin():
            for k in range(4):
                for half in range(2):
                    first[half][k].start()
            if part == 0:
                flag = head[...] + hs[LISTS]
                for e in range(LISTS):
                    flag = flag + hm[e] + hs[e]
                ff[0] = flag.astype(f32)
                flags[0].start()
                flags[1].start()

        def pass_on():
            for k in range(2):
                for half in range(2):
                    me = y if half == 0 else x
                    to = lax.rem(me + (1 if k == 0 else 3), 4)
                    first[half][k].wait_recv()
                    for i in range(2):
                        sb_[half, k, i] = (wide_of(p_.at[half, to, 2 * k + i]) + wide_of(ro_.at[half, k, i])).astype(bf16)
                    first[half][4 + k].start()
            if part == 0:
                flags[0].wait_recv()
                ff[3] = ff[0] + ff[1]
                flags[2].start()

        def turn():
            for half in range(2):
                me = y if half == 0 else x
                for k in (2, 3, 4, 5):
                    first[half][k].wait_recv()
                for i in range(4):
                    u_[half, i] = (
                        wide_of(p_.at[half, me, i]) + wide_of(rd_.at[half, 0, i]) + wide_of(rd_.at[half, 1, i])
                    ).astype(bf16)
                for k in (1, 0, 2):
                    second[half][k].start()
            if part == 0:
                flags[1].wait_recv()
                flags[2].wait_recv()
                ff[5] = ff[0] + ff[2] + ff[4]
                flags[3].start()
                flags[4].start()

        def relay():
            if part == 0:
                flags[3].wait_recv()
                ff[8] = ff[5] + ff[6]
                flags[5].start()

        def finish():
            for half in range(2):
                other = x if half == 0 else y
                turned = wide_of(u_.at[half, other])
                for k in range(3):
                    second[half][k].wait_recv()
                    turned = turned + wide_of(rd2_.at[half, k])
                total[half, :, part * HALF : (part + 1) * HALF] = turned.T
            if part == 0:
                flags[4].wait_recv()
                flags[5].wait_recv()
                flag_out[...] = ff[5] + ff[7] + ff[9]

        def drain():
            for c in (*first[0], *first[1], *second[0], *second[1]):
                c.wait_send()

        return begin, (pass_on, turn, relay, finish), drain

    begin_a, steps_a, drain_a = reducer(0)
    begin_b, steps_b, drain_b = reducer(1)

    for hop in range(HOPS):
        for k in order[hop]:
            for way in range(2):
                entry = way * HOPS + hop
                z_copies[way][hop][k].wait_recv()
                if hop + 1 < HOPS and k in z_copies[way][hop + 1]:
                    z_copies[way][hop + 1][k].start()
                if k == 5:
                    side[entry][0].start()
                    to_scalar[entry].start()
        for way in range(2):
            entry = way * HOPS + hop
            side[entry][1].start()
            side[entry][2].start()
        if hop == HOPS - 1:
            for k in range(HOPS):
                for way in range(2):
                    z_copies[way][0][6 + k].start()
        if hop == 0:
            ready(LISTS)
            first_columns(0)
        else:
            for way in range(2):
                ready(way * HOPS + hop - 1)
                first_columns(1 + 2 * (hop - 1) + way)
    for entry in far_stage:
        ready(entry)
    first_columns(STAGES - 1)
    begin_a()

    for hop in range(HOPS):
        for k in range(HOPS - hop):
            for way in range(2):
                z_copies[way][hop][6 + k].wait_recv()
                if hop + 1 < HOPS and 6 + k in z_copies[way][hop + 1]:
                    z_copies[way][hop + 1][6 + k].start()
        for way in range(2):
            side[way * HOPS + hop][3].start()
        if hop == 0:
            side[LISTS][3].wait_recv()
            other_columns(0)
            steps_a[0]()
        else:
            for way in range(2):
                side[way * HOPS + hop - 1][3].wait_recv()
                other_columns(1 + 2 * (hop - 1) + way)
                if way == 0:
                    steps_a[hop]()
    for entry in far_stage:
        side[entry][3].wait_recv()
    other_columns(STAGES - 1)
    begin_b()
    for step in steps_b:
        step()

    drain_a()
    drain_b()
    for way in range(2):
        for hop in range(HOPS):
            for k in z_copies[way][hop]:
                z_copies[way][hop][k].wait_send()
    for group in side:
        for c in group:
            c.wait_send()
    for c in flags:
        c.wait_send()


def exchange(send, send_b, send_w, head):
    vmem = pl.BlockSpec(memory_space=pltpu.VMEM)
    members = send.shape[2] - HALF
    square, slab = (members, members), (HALF, members)
    dma = pltpu.SemaphoreType.DMA
    panels = [pltpu.VMEM((cap, ROWS, members + HALF), bf16) for cap in CAPS] * 2
    others = [pltpu.VMEM((cap, ROWS, HALF), bf16) for cap in CAPS] * 2
    weights = [pltpu.VMEM((cap, 128), f32) for cap in WCAPS] * 2
    return pl.pallas_call(
        exchange_kernel,
        out_shape=(
            jax.ShapeDtypeStruct((2, *square), f32),
            jax.ShapeDtypeStruct((8, 128), f32),
        ),
        in_specs=[vmem] * 4,
        out_specs=(vmem, vmem),
        scratch_shapes=[
            *panels,
            *panels,
            pltpu.VMEM((STAY, ROWS, members + HALF), bf16),
            *others,
            *others,
            pltpu.VMEM((STAY, ROWS, HALF), bf16),
            *weights,
            *weights,
            pltpu.VMEM((STAY, 128), f32),
            pltpu.VMEM((LISTS, 8, 128), i32),
            pltpu.VMEM((LISTS + 1, 8, 128), i32),
            pltpu.SMEM((2 * LISTS + 2, 8, 128), i32),
            pltpu.VMEM((NY, 256, HALF), bf16),
            pltpu.VMEM((NY * 16, 128), f32),
            pltpu.VMEM((STAGES, NY, 256, members), bf16),
            pltpu.VMEM((STAGES, 8, NY * 256), f32),
            pltpu.VMEM((NY, 8, *slab), f32),
            pltpu.VMEM((10, 8, 128), f32),
            *[pltpu.VMEM((2, 4, 4, *slab), bf16)] * 2,
            *[pltpu.VMEM((2, 2, 2, *slab), bf16)] * 2,
            *[pltpu.VMEM((2, 2, 4, *slab), bf16)] * 2,
            *[pltpu.VMEM((2, 2, 2, *slab), bf16)] * 2,
            *[pltpu.VMEM((2, 4, *slab), bf16)] * 2,
            *[pltpu.VMEM((2, 3, *slab), bf16)] * 2,
            dma((2, HOPS, 6 + HOPS)),
            dma((2, HOPS, 6 + HOPS)),
            dma((LISTS + 1, 4)),
            dma((LISTS + 1, 4)),
            dma((2 * LISTS + 2,)),
            dma((2, 2, 2, 6)),
            dma((2, 2, 2, 6)),
            dma((6,)),
            dma((6,)),
        ],
        compiler_params=pltpu.CompilerParams(collective_id=0, has_side_effects=True, vmem_limit_bytes=46 * MIB),
    )(send, send_b, send_w, head)


def update_kernel(state, coeff, total, updated, new_coeff, coef):
    @pl.when(pl.program_id(1) == 0)
    def _():
        new = (1.0 - relaxation) * coeff[...] + relaxation * total[...]
        new_coeff[...] = new
        coef[...] = new.astype(bf16)

    s = state[...]
    updated[...] = (s.astype(f32) + jnp.dot(s, coef[...], preferred_element_type=f32)).astype(bf16)


def update(state, coeff, total):
    _, blocks, width, members = state.shape
    step = 4096
    square = (members, members)
    rows = pl.BlockSpec((None, None, step, members), lambda j, i: (0, j, i, 0))
    one = pl.BlockSpec((None, None, *square), lambda j, i: (0, j, 0, 0))
    return pl.pallas_call(
        update_kernel,
        grid=(blocks, width // step),
        out_shape=(jax.ShapeDtypeStruct(state.shape, bf16), jax.ShapeDtypeStruct(coeff.shape, f32)),
        in_specs=[rows, one, pl.BlockSpec((None, *square), lambda j, i: (j, 0, 0))],
        out_specs=(rows, one),
        scratch_shapes=[pltpu.VMEM(square, bf16)],
        compiler_params=pltpu.CompilerParams(vmem_limit_bytes=60 * MIB),
    )(state, coeff, total)


def padded_total(obs_anom, innov, obs_rinv, obs_pos, obs_count, obs_region, obs_partner, blocks, width):
    tile_count = lax.axis_size("tile")
    nblock, observation_count, ensemble_members = obs_anom.shape
    partition_count = obs_partner.shape[1]
    nlocal = lax.axis_size("grp") * blocks
    per_neighbour = max(2, (2 * nblock + tile_count - 1) // tile_count)
    slot_count = tile_count * per_neighbour
    slot_grouping = 8
    region = obs_region[:, 0]
    order = jnp.arange(nblock, dtype=jnp.int32)
    before = (region[None, :] == region[:, None]) & (order[None, :] < order[:, None])
    destination = region * per_neighbour + jnp.sum(before.astype(jnp.int32), axis=1)
    assignment_rule = destination[None, :] == jnp.arange(slot_count, dtype=jnp.int32)[:, None]
    place_half = assignment_rule.astype(jnp.bfloat16)
    place_int = assignment_rule.astype(jnp.int32)
    labels = jnp.concatenate([obs_count[:, None], obs_partner], axis=1)
    sent_labels = jnp.dot(place_int, labels).reshape(tile_count, per_neighbour, partition_count + 1)
    stacked = jnp.concatenate([obs_anom, innov], axis=2).reshape(nblock, -1)
    packed = jnp.dot(place_half, stacked, preferred_element_type=jnp.bfloat16)
    packed = packed.reshape(tile_count, per_neighbour, observation_count, 2 * ensemble_members)
    sent_pos = jnp.dot(place_int, obs_pos).reshape(tile_count, per_neighbour, observation_count)
    sent_var = jnp.dot(assignment_rule.astype(jnp.float32), obs_rinv, precision=lax.Precision.HIGHEST)
    sent_var = sent_var.reshape(tile_count, per_neighbour, observation_count)

    def exchange(array):
        return lax.all_to_all(array, "tile", split_axis=0, concat_axis=0, tiled=True)

    received_panels = exchange(packed).reshape(slot_count, observation_count, 2 * ensemble_members)
    flattened_labels = exchange(sent_labels).reshape(slot_count, partition_count + 1)
    recv_anom = received_panels[:, :, :ensemble_members]
    recv_innov = received_panels[:, :, ensemble_members:]
    flattened_positions = exchange(sent_pos).reshape(slot_count, observation_count)
    flattened_variances = exchange(sent_var).reshape(slot_count, observation_count)
    partners = flattened_labels[:, 1:]
    block_index = jnp.arange(nlocal, dtype=jnp.int32)

    def accumulate_group(step, total):
        start = step * slot_grouping

        def part(array):
            return lax.dynamic_slice_in_dim(array, start, slot_grouping, 0)

        weights = taper_weights(
            part(flattened_positions), part(partners), part(flattened_labels)[:, 0], part(flattened_variances), width,
            ensemble_members,
        )
        scaled_part = (weights[..., None] * part(recv_innov)[:, None].astype(jnp.float32)).astype(jnp.bfloat16)
        picked = (part(partners)[..., None] == block_index).astype(jnp.bfloat16)
        by_block = jnp.einsum("qkb,qkin->qbin", picked, scaled_part, preferred_element_type=jnp.float32).astype(jnp.bfloat16)
        return total + jnp.einsum("qim,qbin->bmn", part(recv_anom), by_block, preferred_element_type=jnp.float32)

    initial_total = jnp.zeros((nlocal, ensemble_members, ensemble_members), jnp.float32)
    running_totals = lax.fori_loop(0, slot_count // slot_grouping, accumulate_group, initial_total)
    return lax.psum_scatter(running_totals.astype(jnp.bfloat16), "grp", scatter_dimension=0, tiled=True).astype(jnp.float32)


def on_device(obs_anom, innov, obs_rinv, obs_pos, obs_count, obs_region, obs_partner, state_anom, coeff):
    send, send_b, send_w, head = pack(obs_region[:, 0], obs_count, obs_partner.T, obs_pos, obs_rinv, obs_anom, innov)
    fast, flags = exchange(send, send_b, send_w, head)
    blocks, width = state_anom.shape[1:3]
    total = lax.cond(
        flags[1, NR] > 0,
        lambda *obs: padded_total(*obs[:-1], blocks, width),
        lambda *obs: obs[-1],
        obs_anom, innov, obs_rinv, obs_pos, obs_count, obs_region, obs_partner, fast,
    )
    return update(state_anom, coeff, total)


def solution(mesh):
    return jax.shard_map(
        on_device,
        mesh=mesh,
        in_specs=(
            P(("grp", "tile"), None, None),
            P(("grp", "tile"), None, None),
            P(("grp", "tile"), None),
            P(("grp", "tile"), None),
            P(("grp", "tile")),
            P(("grp", "tile"), None),
            P(("grp", "tile"), None),
            P("grp", "tile", None, None),
            P("grp", "tile", None, None),
        ),
        out_specs=(P("grp", "tile", None, None), P("grp", "tile", None, None)),
        check_vma=False,
    )
```

```python
import jax
import jax.numpy as jnp
from jax import lax
from jax.experimental import pallas as pl
from jax.experimental.pallas import tpu as pltpu
from jax.sharding import PartitionSpec as P

relaxation = 0.5
bf16, f32, i32 = jnp.bfloat16, jnp.float32, jnp.int32
MESH = pl.DeviceIdType.MESH
MIB = 1024 * 1024

ROWS = 16
CAPS = (56, 46, 34, 24)
STAY = 32
SEND = 2 * CAPS[0] + STAY
SPARE = 8
HOPS = len(CAPS)
NZ, NY, NX, NR = 8, 4, 4, 64
LISTS = 2 * HOPS
HALF = 128
WCAPS = tuple((cap + 7) // 8 * 8 for cap in CAPS)
STAGES = 2 * HOPS


def taper_weights(positions, partners, counts, inverse_var, width, ensemble_members):
    center = (partners.astype(jnp.float32) + 0.5) * width
    offset = (positions.astype(jnp.float32)[..., None, :] - center[..., :, None]) / (2.0 * width)
    index = jnp.arange(positions.shape[-1], dtype=jnp.int32)
    live = index < counts[..., None]
    weight = jnp.exp(-offset * offset) * inverse_var[..., None, :] / (ensemble_members - 1.0)
    return jnp.where(live[..., None, :], weight, 0.0)


def pack_kernel(
    region, count, partner, pos, rinv, anom, innov, send, send_b, send_w, head, wall, held, size, fill, seats, place_at, sem
):
    nblock, members = anom.shape[0], anom.shape[2]
    width = 4096.0
    z = lax.axis_index("tile") // 8
    loads = [pltpu.make_async_copy(source, held.at[i], sem.at[i]) for i, source in enumerate((anom, innov))]
    for c in loads:
        c.start()

    deep = 8 * nblock
    lane = lax.broadcasted_iota(i32, (deep, 128), 1)
    repeat = (lax.broadcasted_iota(i32, (deep, nblock), 0) // 8 == lax.broadcasted_iota(i32, (deep, nblock), 1)).astype(f32)
    column = lax.broadcasted_iota(i32, (deep, 64), 1)
    quarter = (column // 16 == lax.broadcasted_iota(i32, (deep, 64), 0) % 8).astype(f32)
    fold = (lax.broadcasted_iota(i32, (64, 128), 0) % 16 == lax.broadcasted_iota(i32, (64, 128), 1) % 16).astype(f32)

    def exact(a, b):
        return jnp.dot(a, b, precision=lax.Precision.HIGHEST, preferred_element_type=f32)

    def spread(values):
        return exact(exact(repeat, values) * quarter, fold)

    partners = lax.dot_general(
        repeat, partner[...].astype(f32), (((1,), (1,)), ((), ())), precision=lax.Precision.HIGHEST, preferred_element_type=f32
    )
    block_of_lane = (lane // 16).astype(f32)
    paired = jnp.zeros((deep, 128), f32)
    for k in range(partner.shape[0]):
        paired = jnp.where(partners[:, k : k + 1] == block_of_lane, 1.0, paired)
    center = (block_of_lane + 0.5) * width
    offset = (spread(pos[...].astype(f32)) - center) / (2.0 * width)
    wall[...] = jnp.exp(-offset * offset) * spread(rinv[...]) / (members - 1.0) * paired

    def clear(i, c):
        size[i] = 0
        fill[i] = 0
        return c

    lax.fori_loop(0, NR, clear, 0, unroll=16)

    def blank(i, c):
        send[i] = jnp.zeros(send.shape[1:], bf16)
        send_b[i] = jnp.zeros(send_b.shape[1:], bf16)
        return c

    lax.fori_loop(0, SEND + SPARE, blank, 0, unroll=8)
    send_w[...] = jnp.zeros_like(send_w)

    def measure(o, c):
        r = region[o]
        size[r] = size[r] + count[o]
        return c

    lax.fori_loop(0, nblock, measure, 0, unroll=8)

    def plane(distance):
        return lax.rem(z + distance, NZ) * 8

    def total(distance):
        base = plane(distance)
        return sum(size[base + i] for i in range(8))

    head_row = lax.broadcasted_iota(i32, (8, 128), 0)
    head_lane = lax.broadcasted_iota(i32, (8, 128), 1)

    def noted(header, row, at, value):
        return jnp.where((head_row == row) & (head_lane == at), value, header)

    def begin(used, n):
        return jnp.where(used % ROWS + n > 8 * ROWS, (used + ROWS - 1) // ROWS * ROWS, used)

    def seat_far(i, carry):
        used_right, used_left, load_right, load_left, header = carry
        r = plane(4) + i
        n = size[r]
        to_right = load_right <= load_left
        right, left = begin(used_right, n), begin(used_left, n)
        header = noted(header, 0, r, jnp.where(to_right, right * 256 + n, 0))
        header = noted(header, 0, NR + r, jnp.where(to_right, 0, left * 256 + n))
        seats[r] = jnp.where(to_right, right, CAPS[0] * ROWS + left)
        used_right, used_left = jnp.where(to_right, right + n, used_right), jnp.where(to_right, used_left, left + n)
        load_right, load_left = jnp.where(to_right, load_right + n, load_right), jnp.where(to_right, load_left, load_left + n)
        return used_right, used_left, load_right, load_left, header

    loads_of = (total(1) + total(2) + total(3), total(5) + total(6) + total(7))
    none = jnp.zeros((), i32)
    used_right, used_left, _, _, header = lax.fori_loop(0, 8, seat_far, (none, none, *loads_of, jnp.zeros((8, 128), i32)), unroll=8)

    def seat_near(distance, base, row, shift, carry):
        def seat(i, carry):
            used, header = carry
            r = plane(distance) + i
            n = size[r]
            first = begin(used, n)
            seats[r] = base * ROWS + first
            return first + n, noted(header, row, shift + r, first * 256 + n)

        return lax.fori_loop(0, 8, seat, carry, unroll=8)

    over = (used_right > CAPS[3] * ROWS) | (used_left > CAPS[3] * ROWS)
    for hop, distance in ((2, 3), (1, 2), (0, 1)):
        used_right, header = seat_near(distance, 0, 0, 0, (used_right, header))
        used_left, header = seat_near(NZ - distance, CAPS[0], 0, NR, (used_left, header))
        over = over | (used_right > CAPS[hop] * ROWS) | (used_left > CAPS[hop] * ROWS)
    used_stay, header = seat_near(0, 2 * CAPS[0], 1, 0, (none, header))
    over = over | (used_stay > STAY * ROWS)
    head[...] = noted(header, 1, NR, over.astype(i32))

    def find(o, c):
        r = region[o]
        place_at[o] = seats[r] + fill[r]
        fill[r] = fill[r] + count[o]
        return c

    lax.fori_loop(0, nblock, find, 0, unroll=8)
    for c in loads:
        c.wait()

    deep_window = 5 * ROWS
    to_row = lax.broadcasted_iota(i32, (deep_window, 64), 0)
    from_row = lax.broadcasted_iota(i32, (deep_window, 64), 1)

    sub = lax.broadcasted_iota(i32, (8, 128), 0)
    row_of_lane = lax.broadcasted_iota(i32, (8, 128), 1) % ROWS

    def place(o, c):
        live, at = count[o], place_at[o]
        shift = at % ROWS
        grain = jnp.minimum(at // ROWS, SEND + SPARE - 8)
        weight = jnp.where(sub * ROWS + row_of_lane < live, wall[pl.ds(pl.multiple_of(o * 8, 8), 8), :], 0.0)
        same = pltpu.roll(weight, shift, 1)
        next_one = pltpu.roll(pltpu.roll(weight, 1, 0), shift + 128 - ROWS, 1)
        send_w[pl.ds(grain, 8), :] += jnp.where(row_of_lane >= shift, same, next_one)

        move = ((to_row - shift == from_row) & (from_row < live)).astype(bf16)
        anomalies = jnp.dot(move, held[0, o], preferred_element_type=f32).astype(bf16)
        innovations = jnp.dot(move, held[1, o], preferred_element_type=f32).astype(bf16)
        for q in range(5):
            rows = slice(q * ROWS, (q + 1) * ROWS)
            send[grain + q, :, 0:members] += anomalies[rows]
            send[grain + q, :, members : members + HALF] += innovations[rows, 0:HALF]
            send_b[grain + q] += innovations[rows, HALF:members]
        return c

    lax.fori_loop(0, nblock, place, 0, unroll=8)


def pack(region, count, partner, pos, rinv, anom, innov):
    members = anom.shape[2]
    vmem, smem = pl.BlockSpec(memory_space=pltpu.VMEM), pl.BlockSpec(memory_space=pltpu.SMEM)
    hbm = pl.BlockSpec(memory_space=pl.ANY)
    return pl.pallas_call(
        pack_kernel,
        out_shape=(
            jax.ShapeDtypeStruct((SEND + SPARE, ROWS, members + HALF), bf16),
            jax.ShapeDtypeStruct((SEND + SPARE, ROWS, HALF), bf16),
            jax.ShapeDtypeStruct((SEND + SPARE, 128), f32),
            jax.ShapeDtypeStruct((8, 128), i32),
        ),
        in_specs=[smem, smem, vmem, vmem, vmem, hbm, hbm],
        out_specs=(vmem, vmem, vmem, vmem),
        scratch_shapes=[
            pltpu.VMEM((8 * anom.shape[0], 128), f32),
            pltpu.VMEM((2, *anom.shape), bf16),
            *[pltpu.SMEM((NR,), i32)] * 3,
            pltpu.SMEM((anom.shape[0],), i32),
            pltpu.SemaphoreType.DMA((2,)),
        ],
        compiler_params=pltpu.CompilerParams(vmem_limit_bytes=16 * MIB),
    )(region, count, partner, pos, rinv, anom, innov)


def exchange_kernel(send, send_b, send_w, head, total, flag_out, *scratch):
    scratch = list(scratch)

    def take(n):
        out = scratch[:n]
        del scratch[:n]
        return out

    zm, zs, bm, bs = take(LISTS), take(LISTS + 1), take(LISTS), take(LISTS + 1)
    wm, ws = take(LISTS), take(LISTS + 1)
    hm, hs, hsm, pn, pw, kept_a, kept_w, acc, ff = take(9)
    p, ro, rd, sb, u, rd2 = (take(2) for _ in range(6))
    zsend, zrecv, ssend, srecv, hsem, sems, recvs, fsend, frecv = take(9)

    members = acc.shape[3]
    x, tile = lax.axis_index("grp"), lax.axis_index("tile")
    z, inner = tile // 8, tile % 8
    y, core = inner // 2, inner % 2
    sibling = tile + 1 - 2 * core

    def around(step):
        return x, lax.rem(z + step, NZ) * 8 + inner

    def along(axis, step):
        if axis == 0:
            return x, z * 8 + lax.rem(y + step, NY) * 2 + core
        return lax.rem(x + step, NX), tile

    ways = (around(1), around(NZ - 1))
    barrier = pltpu.get_barrier_semaphore()
    for other in (*ways, (x, sibling), *(along(axis, step) for axis in range(2) for step in (1, 2, 3))):
        pl.semaphore_signal(barrier, inc=1, device_id=other, device_id_type=MESH)
    pl.semaphore_wait(barrier, 9)

    def copy(src, dst, send_sem, recv_sem, other):
        return pltpu.make_async_remote_copy(
            src_ref=src, dst_ref=dst, send_sem=send_sem, recv_sem=recv_sem, device_id=other, device_id_type=MESH
        )

    edges = (0, *CAPS[::-1])

    def hop_copies(way, hop):
        entry = way * HOPS + hop
        base = way * CAPS[0]
        out = []
        for k in range(HOPS - hop):
            lo, n = edges[k], edges[k + 1] - edges[k]
            src = send.at[pl.ds(base + lo, n)] if hop == 0 else zm[entry - 1].at[pl.ds(lo, n)]
            out.append((k, src, zm[entry].at[pl.ds(lo, n)]))
        rows = WCAPS[hop]
        out.append((4, send_w.at[pl.ds(base, rows)] if hop == 0 else wm[entry - 1].at[pl.ds(0, rows)], wm[entry]))
        out.append((5, head if hop == 0 else hm.at[entry - 1], hm.at[entry]))
        for k in range(HOPS - hop):
            lo, n = edges[k], edges[k + 1] - edges[k]
            src = send_b.at[pl.ds(base + lo, n)] if hop == 0 else bm[entry - 1].at[pl.ds(lo, n)]
            out.append((6 + k, src, bm[entry].at[pl.ds(lo, n)]))
        return {k: copy(src, dst, zsend.at[way, hop, k], zrecv.at[way, hop, k], ways[way]) for k, src, dst in out}

    z_copies = [[hop_copies(way, hop) for hop in range(HOPS)] for way in range(2)]
    order = [[5, 4, *range(HOPS - hop)] for hop in range(HOPS)]
    stay = pl.ds(2 * CAPS[0], STAY)
    pairs = [((hm.at[e], hs.at[e]), (zm[e], zs[e]), (wm[e], ws[e]), (bm[e], bs[e])) for e in range(LISTS)]
    pairs.append((
        (head, hs.at[LISTS]), (send.at[stay], zs[LISTS]), (send_w.at[stay], ws[LISTS]), (send_b.at[stay], bs[LISTS])
    ))
    side = [
        [copy(s, t, ssend.at[e, i], srecv.at[e, i], (x, sibling)) for i, (s, t) in enumerate(pairs[e])] for e in range(LISTS + 1)
    ]
    to_scalar = [pltpu.make_async_copy(hm.at[e], hsm.at[e], hsem.at[e]) for e in range(LISTS)]
    to_scalar.append(pltpu.make_async_copy(head, hsm.at[LISTS], hsem.at[LISTS]))
    to_scalar += [pltpu.make_async_copy(hs.at[e], hsm.at[LISTS + 1 + e], hsem.at[LISTS + 1 + e]) for e in range(LISTS + 1)]

    for k in order[0]:
        for way in range(2):
            z_copies[way][0][k].start()
    for c in side[LISTS]:
        c.start()
    to_scalar[LISTS].start()

    expand = (lax.broadcasted_iota(i32, (1024, 64), 0) // 16 == lax.broadcasted_iota(i32, (1024, 64), 1)).astype(bf16)
    keep = (lax.broadcasted_iota(i32, (1024, 128), 0) % 16 == lax.broadcasted_iota(i32, (1024, 128), 1) % 16).astype(f32)
    pick = (lax.broadcasted_iota(i32, (8, 128), 1) // 16 == lax.broadcasted_iota(i32, (8, 128), 0)).astype(bf16)

    own_stage, far_stage = (LISTS,), (HOPS - 1, LISTS - 1)
    stages = [own_stage, *((way * HOPS + hop,) for hop in range(HOPS - 1) for way in range(2)), far_stage]

    def place_of(at, entry, r):
        row, shift = (1, 0) if entry == LISTS else (0, entry // HOPS * NR)
        value = hsm[at, row, shift + r]
        return value // 256, value % 256

    row_of_lane = lax.broadcasted_iota(i32, (1, 128), 1) % ROWS

    def slots(entries, who, r):
        found = []
        for entry in entries:
            start, rows = place_of(entry + who * (LISTS + 1), entry, r)
            own = entry == LISTS
            base = 2 * CAPS[0] if own and not who else 0
            found.append((start, rows, base, STAY if own else CAPS[entry % HOPS]))
        out = []
        for i in range(8):
            places = [base + jnp.minimum(start // ROWS + i, cap - 1) for start, _, base, cap in found]
            start, rows = found[0][0:2]
            in_first = None
            if len(found) == 2:
                in_first = rows > 0
                start, rows = jnp.where(in_first, start, found[1][0]), jnp.where(in_first, rows, found[1][1])
            at = row_of_lane + ((start // ROWS + i) * ROWS - start)
            out.append((in_first, places[0], places[-1], (at >= 0) & (at < rows)))
        return out

    def sources(entries, who, mine, theirs, own):
        return [theirs[e] if who else (own if e == LISTS else mine[e]) for e in entries]

    def multiply(stage, target):
        for yp in range(NY):
            turned = pn[yp].astype(f32).T
            anomalies = kept_a[stage, yp]
            for b in range(8):
                weight = kept_w[stage, b : b + 1, yp * 256 : (yp + 1) * 256]
                product = jnp.dot((turned * weight).astype(bf16), anomalies, preferred_element_type=f32)
                if stage == 0:
                    acc[yp, b] = product
                elif stage < STAGES - 1:
                    acc[yp, b] += product
                elif b % 2 == 0:
                    target[0, yp, b // 2] = (acc[yp, b] + product).astype(bf16)
                else:
                    target[1, b // 2, yp] = (acc[yp, b] + product).astype(bf16)

    def first_columns(stage):
        entries = stages[stage]

        def gather(yp, carry):
            r = z * 8 + yp * 2 + core
            for who in range(2):
                panels = sources(entries, who, zm, zs, send)
                weights = sources(entries, who, wm, ws, send_w)
                for i, (first_list, slot, slot_2, live) in enumerate(slots(entries, who, r)):
                    panel, weight = panels[0][slot], weights[0][pl.ds(slot, 1), :]
                    if first_list is not None:
                        panel = jnp.where(first_list, panel, panels[1][slot_2])
                        weight = jnp.where(first_list, weight, weights[1][pl.ds(slot_2, 1), :])
                    rows = pl.ds(who * 128 + i * ROWS, ROWS)
                    kept_a[stage, yp, rows, :] = panel[:, 0:members]
                    pn[yp, rows, :] = panel[:, members : members + HALF]
                    pw[pl.ds(yp * 16 + who * 8 + i, 1), :] = jnp.where(live, weight, 0.0)
            return carry

        lax.fori_loop(0, NY, gather, 0)
        wide = jnp.dot(expand, pw[...].astype(bf16), preferred_element_type=f32) * keep
        kept_w[stage] = lax.dot_general(pick, wide.astype(bf16), (((1,), (1,)), ((), ())), preferred_element_type=f32)
        multiply(stage, p[0])

    def other_columns(stage):
        entries = stages[stage]

        def gather(yp, carry):
            r = z * 8 + yp * 2 + core
            for who in range(2):
                panels = sources(entries, who, bm, bs, send_b)
                for i, (first_list, slot, slot_2, live) in enumerate(slots(entries, who, r)):
                    panel = panels[0][slot]
                    if first_list is not None:
                        panel = jnp.where(first_list, panel, panels[1][slot_2])
                    pn[yp, pl.ds(who * 128 + i * ROWS, ROWS), :] = panel
            return carry

        lax.fori_loop(0, NY, gather, 0)
        multiply(stage, p[1])

    def ready(entry):
        for c in side[entry][0:3]:
            c.wait_recv()
        for at in (entry, LISTS + 1 + entry):
            if at > LISTS:
                to_scalar[at].start()
            to_scalar[at].wait()

    def wide_of(ref):
        return ref[...].astype(f32)

    def flag_copy(src, dst, k, axis, step):
        return copy(ff.at[src], ff.at[dst], fsend.at[k], frecv.at[k], along(axis, step))

    flags = [
        flag_copy(0, 1, 0, 0, 1), flag_copy(0, 2, 1, 0, 3), flag_copy(3, 4, 2, 0, 1),
        flag_copy(5, 6, 3, 1, 1), flag_copy(5, 7, 4, 1, 3), flag_copy(8, 9, 5, 1, 1),
    ]

    def reducer(part):
        p_, ro_, rd_, sb_, u_, rd2_ = (buffers[part] for buffers in (p, ro, rd, sb, u, rd2))

        def half_copy(src, dst, half, phase, k, axis, step):
            return copy(src, dst, sems.at[part, half, phase, k], recvs.at[part, half, phase, k], along(axis, step))

        def triple(me):
            return lax.rem(me + 1, 4), lax.rem(me + 3, 4), lax.rem(me + 2, 4)

        first, second = [], []
        for half in range(2):
            me, other = (y, x) if half == 0 else (x, y)
            right, left, far = triple(me)
            lo, hi = pl.ds(0, 2), pl.ds(2, 2)
            first.append([
                half_copy(p_.at[half, far, lo], ro_.at[half, 0], half, 0, 0, half, 1),
                half_copy(p_.at[half, far, hi], ro_.at[half, 1], half, 0, 1, half, 3),
                half_copy(p_.at[half, right, hi], rd_.at[half, 0, hi], half, 0, 2, half, 1),
                half_copy(p_.at[half, left, lo], rd_.at[half, 1, lo], half, 0, 3, half, 3),
                half_copy(sb_.at[half, 0], rd_.at[half, 0, lo], half, 0, 4, half, 1),
                half_copy(sb_.at[half, 1], rd_.at[half, 1, hi], half, 0, 5, half, 3),
            ])
            axis = 1 - half
            second.append([
                half_copy(u_.at[half, lax.rem(other + step, 4)], rd2_.at[half, step - 1], half, 1, step - 1, axis, step)
                for step in (1, 2, 3)
            ])

        def begin():
            for k in range(4):
                for half in range(2):
                    first[half][k].start()
            if part == 0:
                flag = head[...] + hs[LISTS]
                for e in range(LISTS):
                    flag = flag + hm[e] + hs[e]
                ff[0] = flag.astype(f32)
                flags[0].start()
                flags[1].start()

        def pass_on():
            for k in range(2):
                for half in range(2):
                    me = y if half == 0 else x
                    to = lax.rem(me + (1 if k == 0 else 3), 4)
                    first[half][k].wait_recv()
                    for i in range(2):
                        sb_[half, k, i] = (wide_of(p_.at[half, to, 2 * k + i]) + wide_of(ro_.at[half, k, i])).astype(bf16)
                    first[half][4 + k].start()
            if part == 0:
                flags[0].wait_recv()
                ff[3] = ff[0] + ff[1]
                flags[2].start()

        def turn():
            for half in range(2):
                me = y if half == 0 else x
                for k in (2, 3, 4, 5):
                    first[half][k].wait_recv()
                for i in range(4):
                    u_[half, i] = (
                        wide_of(p_.at[half, me, i]) + wide_of(rd_.at[half, 0, i]) + wide_of(rd_.at[half, 1, i])
                    ).astype(bf16)
                for k in (1, 0, 2):
                    second[half][k].start()
            if part == 0:
                flags[1].wait_recv()
                flags[2].wait_recv()
                ff[5] = ff[0] + ff[2] + ff[4]
                flags[3].start()
                flags[4].start()

        def relay():
            if part == 0:
                flags[3].wait_recv()
                ff[8] = ff[5] + ff[6]
                flags[5].start()

        def finish():
            for half in range(2):
                other = x if half == 0 else y
                turned = wide_of(u_.at[half, other])
                for k in range(3):
                    second[half][k].wait_recv()
                    turned = turned + wide_of(rd2_.at[half, k])
                total[half, :, part * HALF : (part + 1) * HALF] = turned.T
            if part == 0:
                flags[4].wait_recv()
                flags[5].wait_recv()
                flag_out[...] = ff[5] + ff[7] + ff[9]

        def drain():
            for c in (*first[0], *first[1], *second[0], *second[1]):
                c.wait_send()

        return begin, (pass_on, turn, relay, finish), drain

    begin_a, steps_a, drain_a = reducer(0)
    begin_b, steps_b, drain_b = reducer(1)

    for hop in range(HOPS):
        for k in order[hop]:
            for way in range(2):
                entry = way * HOPS + hop
                z_copies[way][hop][k].wait_recv()
                if hop + 1 < HOPS and k in z_copies[way][hop + 1]:
                    z_copies[way][hop + 1][k].start()
                if k == 5:
                    side[entry][0].start()
                    to_scalar[entry].start()
        for way in range(2):
            entry = way * HOPS + hop
            side[entry][1].start()
            side[entry][2].start()
        if hop == HOPS - 1:
            for k in range(HOPS):
                for way in range(2):
                    z_copies[way][0][6 + k].start()
        if hop == 0:
            ready(LISTS)
            first_columns(0)
        else:
            for way in range(2):
                ready(way * HOPS + hop - 1)
                first_columns(1 + 2 * (hop - 1) + way)
    for entry in far_stage:
        ready(entry)
    first_columns(STAGES - 1)
    begin_a()

    for hop in range(HOPS):
        for k in range(HOPS - hop):
            for way in range(2):
                z_copies[way][hop][6 + k].wait_recv()
                if hop + 1 < HOPS and 6 + k in z_copies[way][hop + 1]:
                    z_copies[way][hop + 1][6 + k].start()
        for way in range(2):
            side[way * HOPS + hop][3].start()
        steps_a[hop]()
        if hop == 0:
            side[LISTS][3].wait_recv()
            other_columns(0)
        else:
            for way in range(2):
                side[way * HOPS + hop - 1][3].wait_recv()
                other_columns(1 + 2 * (hop - 1) + way)
    for entry in far_stage:
        side[entry][3].wait_recv()
    other_columns(STAGES - 1)
    begin_b()
    for step in steps_b:
        step()

    drain_a()
    drain_b()
    for way in range(2):
        for hop in range(HOPS):
            for k in z_copies[way][hop]:
                z_copies[way][hop][k].wait_send()
    for group in side:
        for c in group:
            c.wait_send()
    for c in flags:
        c.wait_send()


def exchange(send, send_b, send_w, head):
    vmem = pl.BlockSpec(memory_space=pltpu.VMEM)
    members = send.shape[2] - HALF
    square, slab = (members, members), (HALF, members)
    dma = pltpu.SemaphoreType.DMA
    panels = [pltpu.VMEM((cap, ROWS, members + HALF), bf16) for cap in CAPS] * 2
    others = [pltpu.VMEM((cap, ROWS, HALF), bf16) for cap in CAPS] * 2
    weights = [pltpu.VMEM((cap, 128), f32) for cap in WCAPS] * 2
    return pl.pallas_call(
        exchange_kernel,
        out_shape=(
            jax.ShapeDtypeStruct((2, *square), f32),
            jax.ShapeDtypeStruct((8, 128), f32),
        ),
        in_specs=[vmem] * 4,
        out_specs=(vmem, vmem),
        scratch_shapes=[
            *panels,
            *panels,
            pltpu.VMEM((STAY, ROWS, members + HALF), bf16),
            *others,
            *others,
            pltpu.VMEM((STAY, ROWS, HALF), bf16),
            *weights,
            *weights,
            pltpu.VMEM((STAY, 128), f32),
            pltpu.VMEM((LISTS, 8, 128), i32),
            pltpu.VMEM((LISTS + 1, 8, 128), i32),
            pltpu.SMEM((2 * LISTS + 2, 8, 128), i32),
            pltpu.VMEM((NY, 256, HALF), bf16),
            pltpu.VMEM((NY * 16, 128), f32),
            pltpu.VMEM((STAGES, NY, 256, members), bf16),
            pltpu.VMEM((STAGES, 8, NY * 256), f32),
            pltpu.VMEM((NY, 8, *slab), f32),
            pltpu.VMEM((10, 8, 128), f32),
            *[pltpu.VMEM((2, 4, 4, *slab), bf16)] * 2,
            *[pltpu.VMEM((2, 2, 2, *slab), bf16)] * 2,
            *[pltpu.VMEM((2, 2, 4, *slab), bf16)] * 2,
            *[pltpu.VMEM((2, 2, 2, *slab), bf16)] * 2,
            *[pltpu.VMEM((2, 4, *slab), bf16)] * 2,
            *[pltpu.VMEM((2, 3, *slab), bf16)] * 2,
            dma((2, HOPS, 6 + HOPS)),
            dma((2, HOPS, 6 + HOPS)),
            dma((LISTS + 1, 4)),
            dma((LISTS + 1, 4)),
            dma((2 * LISTS + 2,)),
            dma((2, 2, 2, 6)),
            dma((2, 2, 2, 6)),
            dma((6,)),
            dma((6,)),
        ],
        compiler_params=pltpu.CompilerParams(collective_id=0, has_side_effects=True, vmem_limit_bytes=46 * MIB),
    )(send, send_b, send_w, head)


def update_kernel(state, coeff, total, updated, new_coeff, coef):
    @pl.when(pl.program_id(1) == 0)
    def _():
        new = (1.0 - relaxation) * coeff[...] + relaxation * total[...]
        new_coeff[...] = new
        coef[...] = new.astype(bf16)

    s = state[...]
    updated[...] = (s.astype(f32) + jnp.dot(s, coef[...], preferred_element_type=f32)).astype(bf16)


def update(state, coeff, total):
    _, blocks, width, members = state.shape
    step = 4096
    square = (members, members)
    rows = pl.BlockSpec((None, None, step, members), lambda j, i: (0, j, i, 0))
    one = pl.BlockSpec((None, None, *square), lambda j, i: (0, j, 0, 0))
    return pl.pallas_call(
        update_kernel,
        grid=(blocks, width // step),
        out_shape=(jax.ShapeDtypeStruct(state.shape, bf16), jax.ShapeDtypeStruct(coeff.shape, f32)),
        in_specs=[rows, one, pl.BlockSpec((None, *square), lambda j, i: (j, 0, 0))],
        out_specs=(rows, one),
        scratch_shapes=[pltpu.VMEM(square, bf16)],
        compiler_params=pltpu.CompilerParams(vmem_limit_bytes=60 * MIB),
    )(state, coeff, total)


def padded_total(obs_anom, innov, obs_rinv, obs_pos, obs_count, obs_region, obs_partner, blocks, width):
    tile_count = lax.axis_size("tile")
    nblock, observation_count, ensemble_members = obs_anom.shape
    partition_count = obs_partner.shape[1]
    nlocal = lax.axis_size("grp") * blocks
    per_neighbour = max(2, (2 * nblock + tile_count - 1) // tile_count)
    slot_count = tile_count * per_neighbour
    slot_grouping = 8
    region = obs_region[:, 0]
    order = jnp.arange(nblock, dtype=jnp.int32)
    before = (region[None, :] == region[:, None]) & (order[None, :] < order[:, None])
    destination = region * per_neighbour + jnp.sum(before.astype(jnp.int32), axis=1)
    assignment_rule = destination[None, :] == jnp.arange(slot_count, dtype=jnp.int32)[:, None]
    place_half = assignment_rule.astype(jnp.bfloat16)
    place_int = assignment_rule.astype(jnp.int32)
    labels = jnp.concatenate([obs_count[:, None], obs_partner], axis=1)
    sent_labels = jnp.dot(place_int, labels).reshape(tile_count, per_neighbour, partition_count + 1)
    stacked = jnp.concatenate([obs_anom, innov], axis=2).reshape(nblock, -1)
    packed = jnp.dot(place_half, stacked, preferred_element_type=jnp.bfloat16)
    packed = packed.reshape(tile_count, per_neighbour, observation_count, 2 * ensemble_members)
    sent_pos = jnp.dot(place_int, obs_pos).reshape(tile_count, per_neighbour, observation_count)
    sent_var = jnp.dot(assignment_rule.astype(jnp.float32), obs_rinv, precision=lax.Precision.HIGHEST)
    sent_var = sent_var.reshape(tile_count, per_neighbour, observation_count)

    def exchange(array):
        return lax.all_to_all(array, "tile", split_axis=0, concat_axis=0, tiled=True)

    received_panels = exchange(packed).reshape(slot_count, observation_count, 2 * ensemble_members)
    flattened_labels = exchange(sent_labels).reshape(slot_count, partition_count + 1)
    recv_anom = received_panels[:, :, :ensemble_members]
    recv_innov = received_panels[:, :, ensemble_members:]
    flattened_positions = exchange(sent_pos).reshape(slot_count, observation_count)
    flattened_variances = exchange(sent_var).reshape(slot_count, observation_count)
    partners = flattened_labels[:, 1:]
    block_index = jnp.arange(nlocal, dtype=jnp.int32)

    def accumulate_group(step, total):
        start = step * slot_grouping

        def part(array):
            return lax.dynamic_slice_in_dim(array, start, slot_grouping, 0)

        weights = taper_weights(
            part(flattened_positions), part(partners), part(flattened_labels)[:, 0], part(flattened_variances), width,
            ensemble_members,
        )
        scaled_part = (weights[..., None] * part(recv_innov)[:, None].astype(jnp.float32)).astype(jnp.bfloat16)
        picked = (part(partners)[..., None] == block_index).astype(jnp.bfloat16)
        by_block = jnp.einsum("qkb,qkin->qbin", picked, scaled_part, preferred_element_type=jnp.float32).astype(jnp.bfloat16)
        return total + jnp.einsum("qim,qbin->bmn", part(recv_anom), by_block, preferred_element_type=jnp.float32)

    initial_total = jnp.zeros((nlocal, ensemble_members, ensemble_members), jnp.float32)
    running_totals = lax.fori_loop(0, slot_count // slot_grouping, accumulate_group, initial_total)
    return lax.psum_scatter(running_totals.astype(jnp.bfloat16), "grp", scatter_dimension=0, tiled=True).astype(jnp.float32)


def on_device(obs_anom, innov, obs_rinv, obs_pos, obs_count, obs_region, obs_partner, state_anom, coeff):
    send, send_b, send_w, head = pack(obs_region[:, 0], obs_count, obs_partner.T, obs_pos, obs_rinv, obs_anom, innov)
    fast, flags = exchange(send, send_b, send_w, head)
    blocks, width = state_anom.shape[1:3]
    total = lax.cond(
        flags[1, NR] > 0,
        lambda *obs: padded_total(*obs[:-1], blocks, width),
        lambda *obs: obs[-1],
        obs_anom, innov, obs_rinv, obs_pos, obs_count, obs_region, obs_partner, fast,
    )
    return update(state_anom, coeff, total)


def solution(mesh):
    return jax.shard_map(
        on_device,
        mesh=mesh,
        in_specs=(
            P(("grp", "tile"), None, None),
            P(("grp", "tile"), None, None),
            P(("grp", "tile"), None),
            P(("grp", "tile"), None),
            P(("grp", "tile")),
            P(("grp", "tile"), None),
            P(("grp", "tile"), None),
            P("grp", "tile", None, None),
            P("grp", "tile", None, None),
        ),
        out_specs=(P("grp", "tile", None, None), P("grp", "tile", None, None)),
        check_vma=False,
    )
```
